256 devices in a mesh: replica: 32 (over y_hi, z, core), tensor: 8 (over x, y_lo).
Axes of the slice: x: 4, y: 4 (y_hi: 2, y_lo: 2; y = y_hi * 2 + y_lo), z: 8, core: 2. Of those that a mesh axis runs over, the one named last changes fastest.
Arguments:
- hidden: bfloat16 [1024, 2, 5120], P('replica'), may hold values from -6 to 6
- queries: bfloat16 [1024, 2, 4096], P('replica', None, 'tensor'), may hold values from -170 to 170
- cache_keys: bfloat16 [1024, 256, 1024], P('replica', None, 'tensor'), may hold values from -6 to 6
- cache_values: bfloat16 [1024, 256, 1024], P('replica', None, 'tensor'), may hold values from -6 to 6
- key_weight: bfloat16 [5120, 1024], P(None, 'tensor'), may hold values from -0.078125 to 0.078125
- value_weight: bfloat16 [5120, 1024], P(None, 'tensor'), may hold values from -0.078125 to 0.078125
- key_gain: float32 [128], replicated, may hold values from 0.1 to 1.9
- out_weight: bfloat16 [4096, 5120], P('tensor'), may hold values from -0.09375 to 0.09375
- lengths: int32 [1024], replicated, may hold values from 0 to 254, as said below
- move_src: int32 [448], replicated, may hold values from 0 to 1023, as said below
- move_dst: int32 [448], replicated, may hold values from 1 to 1022, as said below
Outputs:
- attn_branch: bfloat16 [1024, 2, 5120], P('replica', None, 'tensor')
- keys_out: bfloat16 [1024, 256, 1024], P('replica', None, 'tensor')
- values_out: bfloat16 [1024, 256, 1024], P('replica', None, 'tensor')
The draws below stay inside these ranges and needn't reach their ends.
Inputs may be any that keep to these rules, and one draw needn't show every extreme that they name: `lengths`: every replica has exactly 14 slots with length 0 and all its other slots hold 2 or more tokens; some slot holds exactly 254. `move_src`: entries k * 14 to (k + 1) * 14 - 1 are slots of replica k; all are distinct slots with nonzero length; slots 0 and 1023 always leave. `move_dst`: all distinct slots of length 0; every replica receives exactly 14 rollouts; no move stays within a replica, and no two moves go from the same replica to the same replica; slots 1 and 1022 always receive.
All inputs are finite; a program needn't handle non-finite values.
Results may differ from the reference program's by a relative error of at most 0.0058.
Values may be sent and summed in bfloat16 or wider, within the bound.
A program may use at most 64 MiB of HBM per device.

```python
import math
import jax
import jax.numpy as jnp
from jax import lax

D = 5120
HEADS = 32
KVH = 8
HD = 128
ROLL_DEV = 32
LMAX = 256
MOVE_DEV = 14
ROLLOUTS = 1024


def pinned(order, first, second):
    spot = jnp.argmax(order == first).astype(jnp.int32)
    leading = order[0]
    order = order.at[spot].set(leading).at[0].set(first)
    spot = jnp.argmax(order == second).astype(jnp.int32)
    there = order[MOVE_DEV]
    order = order.at[spot].set(there).at[MOVE_DEV].set(second)
    return order.astype(jnp.int32)


def migration_plan(key):
    replicas = ROLLOUTS // ROLL_DEV
    key_shift, key_order, key_long, key_short = jax.random.split(jax.random.fold_in(key, 11), 4)
    shuffled = (jax.random.permutation(key_shift, replicas - 1) + 1).astype(jnp.int32)
    places = jnp.arange(replicas - 1, dtype=jnp.int32)
    priority = jnp.where(shuffled == 1, -2, jnp.where(shuffled == replicas // 2, -1, places)).astype(jnp.int32)
    ranking = jnp.argsort(priority, stable=True).astype(jnp.int32)
    offsets = shuffled[ranking][:MOVE_DEV]
    orders = jax.vmap(lambda part_key: jax.random.permutation(part_key, ROLL_DEV))(jax.random.split(key_order, replicas)).astype(jnp.int32)
    orders = orders.at[0].set(pinned(orders[0], 0, 1))
    orders = orders.at[replicas - 1].set(pinned(orders[replicas - 1], ROLL_DEV - 1, ROLL_DEV - 2))
    sources = jnp.arange(replicas, dtype=jnp.int32)[:, None]
    columns = jnp.arange(MOVE_DEV, dtype=jnp.int32)[None, :]
    targets = (sources + offsets[None, :]) % replicas
    move_src = sources * ROLL_DEV + orders[:, :MOVE_DEV]
    move_dst = targets * ROLL_DEV + orders[targets, MOVE_DEV + columns]
    rank_ids = jnp.arange(ROLL_DEV, dtype=jnp.int32)[None, :]
    longest = LMAX - 2 - jax.random.randint(key_long, (replicas, ROLL_DEV), 0, LMAX // 4)
    longest = jnp.where(rank_ids == 0, LMAX - 2, longest)
    shorter = jax.random.randint(key_short, (replicas, ROLL_DEV), 2, LMAX - 1)
    by_rank = jnp.where(rank_ids < MOVE_DEV, longest, jnp.where(rank_ids < 2 * MOVE_DEV, 0, shorter))
    rows_index = jnp.broadcast_to(sources, (replicas, ROLL_DEV))
    lengths = jnp.zeros((replicas, ROLL_DEV), jnp.int32).at[rows_index, orders].set(by_rank)
    return (lengths.reshape(-1).astype(jnp.int32), move_src.reshape(-1).astype(jnp.int32), move_dst.reshape(-1).astype(jnp.int32))


def first_key_row(key):
    normal_rows = jax.random.normal(jax.random.fold_in(key, 29), (ROLLOUTS, KVH * HD), jnp.float32)
    return jnp.clip(normal_rows, -6.0, 6.0)


def draw_lengths(key, part):
    return migration_plan(key)[0]


def draw_move_src(key, part):
    return migration_plan(key)[1]


def draw_move_dst(key, part):
    return migration_plan(key)[2]


def draw_cache_keys(key, part):
    head_row = first_key_row(key)
    key = jax.random.fold_in(key, 3)
    others = jnp.clip(jax.random.normal(key, (ROLLOUTS, LMAX - 1, KVH * HD), jnp.float32), -6.0, 6.0)
    return jnp.concatenate([head_row[:, None, :], others], 1).astype(jnp.bfloat16)


def draw_queries(key, part):
    key = jax.random.fold_in(key, 5)
    values = jnp.clip(jax.random.normal(key, (ROLLOUTS, 2, HEADS, HD), jnp.float32), -6.0, 6.0)
    return values.reshape(ROLLOUTS, 2, HEADS * HD).astype(jnp.bfloat16)


def shard_levels(stream_key, dims, pieces, low, top_value):
    level = 1.0
    for axis_at, parts in pieces:
        steps = jax.random.uniform(jax.random.fold_in(jax.random.fold_in(stream_key, 6), axis_at), (parts,), jnp.float32, low / len(pieces), top_value / len(pieces))
        level = level * jnp.repeat(jnp.exp(steps), dims[axis_at] // parts).reshape((-1,) + (1,) * (len(dims) - 1 - axis_at))
    return level


def noise(rng, extent, scale, reach, shards=(), kind=jnp.bfloat16):
    gain = shard_levels(rng, extent, shards, -0.22, 0.18) if shards else 1.0
    entries = jax.random.normal(rng, extent, jnp.float32) * scale * gain
    return jnp.minimum(jnp.maximum(entries, -reach), reach).astype(kind)


def setup_inputs(seed: int = 0) -> dict:
    keys = jax.random.split(jax.random.key(seed), 12)
    hidden = noise(keys[0], (ROLLOUTS, 2, D), 1.0, 6.0, ((0, 32),))
    queries = draw_queries(jax.random.fold_in(keys[11], 71), 0)
    cache_keys = draw_cache_keys(jax.random.fold_in(keys[11], 71), 0)
    cache_values = noise(keys[3], (ROLLOUTS, LMAX, KVH * HD), 1.0, 6.0, ((0, 32), (2, 8)))
    key_weight = noise(keys[4], (D, KVH * HD), D ** -0.5, 0.078125, ((1, 8),))
    value_weight = noise(keys[5], (D, KVH * HD), D ** -0.5, 0.078125, ((1, 8),))
    key_gain = jnp.clip(1.0 + 0.18 * jax.random.normal(keys[6], (HD,), jnp.float32), 0.1, 1.9)
    out_weight = noise(keys[7], (HEADS * HD, D), (HEADS * HD) ** -0.5, 0.09375, ((0, 8),))
    lengths = draw_lengths(jax.random.fold_in(keys[11], 71), 0)
    move_src = draw_move_src(jax.random.fold_in(keys[11], 71), 0)
    move_dst = draw_move_dst(jax.random.fold_in(keys[11], 71), 0)
    return dict(hidden=hidden, queries=queries, cache_keys=cache_keys, cache_values=cache_values, key_weight=key_weight, value_weight=value_weight, key_gain=key_gain, out_weight=out_weight, lengths=lengths, move_src=move_src, move_dst=move_dst)


EPS = 1e-06
THETA = 1000000.0

def rotate(vectors, positions):
    half_width = vectors.shape[-1] // 2
    indices = jnp.arange(half_width, dtype=jnp.float32)
    frequency = jnp.exp(indices * (-2.0 * math.log(THETA) / vectors.shape[-1]))
    angles = positions[:, :, None, None] * frequency
    cosine = jnp.cos(angles)
    sine_values = jnp.sin(angles)
    former = vectors[..., :half_width]
    latter = vectors[..., half_width:]
    return jnp.concatenate([former * cosine - latter * sine_values, latter * cosine + former * sine_values], -1)

def new_entries(hidden, key_weight, value_weight, key_gain, length):
    row_count = hidden.shape[0]
    flat_rows = hidden.reshape(row_count * 2, hidden.shape[2])
    raw_keys = jnp.dot(flat_rows, key_weight, preferred_element_type=jnp.float32).reshape(row_count, 2, -1, key_gain.shape[0])
    mean_square = lax.optimization_barrier(jnp.mean(raw_keys * raw_keys, axis=-1, keepdims=True))
    normed = raw_keys * lax.rsqrt(mean_square + EPS) * key_gain.astype(jnp.float32)
    positions = (length[:, None] + jnp.arange(2, dtype=jnp.int32)[None, :]).astype(jnp.float32)
    fresh_keys = rotate(normed, positions).reshape(row_count, 2, -1).astype(jnp.bfloat16)
    fresh_values = jnp.dot(flat_rows, value_weight, preferred_element_type=jnp.float32).reshape(row_count, 2, -1).astype(jnp.bfloat16)
    return (fresh_keys, fresh_values)

def place(stored, fresh, length, active):
    row_ids = jnp.arange(stored.shape[1], dtype=jnp.int32)[None, :, None]
    border = length[:, None, None]
    kept = jnp.where(row_ids < border, stored, jnp.zeros_like(stored))
    kept = jnp.where(row_ids == border, fresh[:, 0:1, :], kept)
    kept = jnp.where(row_ids == border + 1, fresh[:, 1:2, :], kept)
    return jnp.where(active[:, None, None], kept, jnp.zeros_like(kept))

def attend(full_keys, full_values, length, queries, head_dim):
    row_count, key_rows, width = full_keys.shape
    kv_heads = width // head_dim
    group_size = queries.shape[-1] // width
    query_heads = queries.reshape(row_count, 2, kv_heads, group_size, head_dim).astype(jnp.float32)
    key_heads = full_keys.reshape(row_count, key_rows, kv_heads, head_dim).astype(jnp.float32)
    value_heads = full_values.reshape(row_count, key_rows, kv_heads, head_dim).astype(jnp.float32)
    scores = jnp.einsum('rsvgh,rlvh->rvsgl', query_heads, key_heads) * head_dim ** (-0.5)
    row_ids = jnp.arange(key_rows, dtype=jnp.int32)[None, None, :]
    limits = length[:, None, None] + jnp.arange(2, dtype=jnp.int32)[None, :, None]
    visible = row_ids <= limits
    scores = jnp.where(visible[:, None, :, None, :], scores, -jnp.inf)
    highest = lax.optimization_barrier(jnp.max(scores, axis=-1, keepdims=True))
    weights = jnp.exp(scores - highest)
    shares = (weights / lax.optimization_barrier(jnp.sum(weights, axis=-1, keepdims=True))).astype(jnp.bfloat16)
    mixture = jnp.einsum('rvsgl,rlvh->rsvgh', shares.astype(jnp.float32), value_heads)
    return mixture.reshape(row_count, 2, -1).astype(jnp.bfloat16)

def reference(hidden, queries, cache_keys, cache_values, key_weight, value_weight, key_gain, out_weight, lengths, move_src, move_dst):
    all_slots = jnp.arange(ROLLOUTS, dtype=jnp.int32)
    anchor = all_slots.at[move_src].set(-1).at[move_dst].set(move_src)
    holding = anchor >= 0
    safe_anchor = jnp.where(holding, anchor, 0).astype(jnp.int32)
    new_length = jnp.where(holding, lengths[safe_anchor], 0).astype(jnp.int32)
    alive = new_length > 0
    moved_keys = cache_keys[safe_anchor]
    moved_values = cache_values[safe_anchor]
    head_dim = key_gain.shape[0]

    def one_block(items):
        block_hidden, block_queries, block_keys, block_values, block_length, block_alive = items
        fresh_keys, fresh_values = new_entries(block_hidden, key_weight, value_weight, key_gain, block_length)
        full_keys = place(block_keys, fresh_keys, block_length, block_alive)
        full_values = place(block_values, fresh_values, block_length, block_alive)
        mixture = attend(full_keys, full_values, block_length, block_queries, head_dim)
        branch = jnp.dot(mixture.reshape(-1, mixture.shape[-1]), out_weight, preferred_element_type=jnp.float32)
        branch = branch.reshape(block_hidden.shape[0], 2, -1)
        branch = jnp.where(block_alive[:, None, None], branch, jnp.zeros_like(branch)).astype(jnp.bfloat16)
        return (branch, full_keys, full_values)
    groups = ROLLOUTS // ROLL_DEV

    def shaped(array):
        return array.reshape((groups, ROLL_DEV) + array.shape[1:])
    branch, keys_out, values_out = lax.map(one_block, (shaped(hidden), shaped(queries), shaped(moved_keys), shaped(moved_values), shaped(new_length), shaped(alive)))
    attn_branch = branch.reshape(ROLLOUTS, 2, -1)
    keys_out = keys_out.reshape(ROLLOUTS, LMAX, -1)
    values_out = values_out.reshape(ROLLOUTS, LMAX, -1)
    return (attn_branch, keys_out, values_out)
```

```python
import functools
import math

import jax
import jax.numpy as jnp
from jax import lax
from jax.experimental import pallas as pl
from jax.experimental.pallas import tpu as pltpu
from jax.sharding import PartitionSpec as P

EPS = 1e-06
THETA = 1000000.0
MESH = pl.DeviceIdType.MESH
MOVES = 14
STEP_ROWS = 24


def plan_kernel(slots, replicas, me_ref, len_ref, src_ref, dst_ref, send_ref, from_ref, live_ref, llen_ref, dead_ref, pos_ref, row_ref, found, mark, newlen):
    me = me_ref[0]
    kept_count = slots - 2 * MOVES

    def clear(i, _):
        mark[i] = -1
        newlen[i] = 0
        return 0

    lax.fori_loop(0, slots, clear, 0)

    def clear_sends(i, _):
        send_ref[i] = 0
        return 0

    lax.fori_loop(0, replicas, clear_sends, 0)

    def out(k, _):
        s, d = src_ref[me * MOVES + k], dst_ref[me * MOVES + k]
        mark[s % slots] = -2
        send_ref[(d // slots - me) % replicas] = s % slots
        return 0

    lax.fori_loop(0, MOVES, out, 0)

    def search(j, count):
        found[count] = j
        return count + jnp.where(dst_ref[j] // slots == me, 1, 0)

    lax.fori_loop(0, src_ref.shape[0], search, 0, unroll=8)

    def keep(s, count):
        length = len_ref[me * slots + s]
        stays = (mark[s] != -2) & (length > 0)
        live_ref[count] = s
        llen_ref[count] = length
        mark[s] = jnp.where(stays, count, -1)
        newlen[s] = jnp.where(stays, length, 0)
        return count + jnp.where(stays, 1, 0)

    lax.fori_loop(0, slots, keep, 0)

    def arrive(e, _):
        j = found[e]
        s, d = src_ref[j], dst_ref[j] % slots
        length = len_ref[s]
        from_ref[e] = (me - s // slots) % replicas
        live_ref[kept_count + e] = d
        llen_ref[kept_count + e] = length
        mark[d] = kept_count + e
        newlen[d] = length
        return 0

    lax.fori_loop(0, MOVES, arrive, 0)

    def finish(s, count):
        at = mark[s]
        dead_ref[count] = s
        for t in range(2):
            pos_ref[pl.ds(2 * s + t, 1), :] = jnp.full((1, 128), newlen[s] + t, jnp.int32).astype(jnp.float32)
            row_ref[pl.ds(2 * s + t, 1), :] = jnp.full((1, 128), jnp.where(at < 0, -1, at + t * STEP_ROWS), jnp.int32)
        return count + jnp.where(at < 0, 1, 0)

    lax.fori_loop(0, slots, finish, 0)


def plan(me, lengths, move_src, move_dst, slots, replicas):
    smem = pl.BlockSpec(memory_space=pltpu.SMEM)
    vmem = pl.BlockSpec(memory_space=pltpu.VMEM)
    ints = lambda n: jax.ShapeDtypeStruct((n,), jnp.int32)
    live = slots - MOVES
    return pl.pallas_call(
        functools.partial(plan_kernel, slots, replicas),
        out_shape=(
            ints(replicas),
            ints(MOVES),
            ints(live + 1),
            ints(live + 1),
            ints(MOVES + 1),
            jax.ShapeDtypeStruct((2 * slots, 128), jnp.float32),
            jax.ShapeDtypeStruct((2 * slots, 128), jnp.int32),
        ),
        in_specs=[smem] * 4,
        out_specs=(smem,) * 5 + (vmem,) * 2,
        scratch_shapes=[
            pltpu.SMEM((MOVES + 1,), jnp.int32),
            pltpu.SMEM((slots,), jnp.int32),
            pltpu.SMEM((slots,), jnp.int32),
        ],
    )(me, lengths, move_src, move_dst)


def layer_kernel(
    replicas,
    tensors,
    send_ref,
    from_ref,
    live_ref,
    llen_ref,
    pos_ref,
    row_ref,
    gain_ref,
    hidden_hbm,
    query_hbm,
    ck_hbm,
    cv_hbm,
    kw_hbm,
    vw_hbm,
    ow_hbm,
    branch_ref,
    list_hbm,
    ck,
    cv,
    hid,
    qry,
    kw,
    vw,
    ow,
    stage,
    recv,
    listed,
    fresh_k,
    fresh_v,
    mix,
    rs_stage,
    rs_recv,
    reduced,
    in_sem,
    send_sem,
    recv_sem,
    rs_send_sem,
    rs_recv_sem,
    list_sem,
):
    me = lax.axis_index("replica")
    at = lax.axis_index("tensor")
    slots, rows, width = ck.shape
    live = listed.shape[0]
    kept = live - MOVES
    groups = query_hbm.shape[2] // width

    loads = [
        pltpu.make_async_copy(source, target, in_sem.at[i])
        for i, (source, target) in enumerate(
            (
                (ck_hbm, ck),
                (cv_hbm, cv),
                (hidden_hbm, hid),
                (kw_hbm, kw),
                (vw_hbm, vw),
                (query_hbm, qry),
                (ow_hbm, ow),
            )
        )
    ]
    for load in loads:
        load.start()

    barrier = pltpu.get_barrier_semaphore()

    def greet(j, _):
        pl.semaphore_signal(barrier, inc=1, device_id={"replica": lax.rem(me + j, replicas)}, device_id_type=MESH)
        return 0

    lax.fori_loop(1, replicas, greet, 0)

    def greet_tensor(j, _):
        pl.semaphore_signal(barrier, inc=1, device_id={"tensor": lax.rem(at + j, tensors)}, device_id_type=MESH)
        return 0

    lax.fori_loop(1, tensors, greet_tensor, 0)
    pl.semaphore_wait(barrier, replicas - 1 + tensors - 1)

    loads[0].wait()
    loads[1].wait()

    def move(j):
        return pltpu.make_async_remote_copy(
            src_ref=stage.at[j],
            dst_ref=recv.at[j],
            send_sem=send_sem.at[j],
            recv_sem=recv_sem.at[j],
            device_id={"replica": lax.rem(me + j, replicas)},
            device_id_type=MESH,
        )

    def send(j, _):
        slot = send_ref[j]
        stage[j, :rows, :] = ck[slot]
        stage[j, rows:, :] = cv[slot]
        move(j).start()
        return 0

    lax.fori_loop(1, replicas, send, 0)

    loads[2].wait()
    loads[3].wait()
    loads[4].wait()
    raw_k = jnp.dot(hid[...], kw[...], preferred_element_type=jnp.float32)
    raw_v = jnp.dot(hid[...], vw[...], preferred_element_type=jnp.float32)
    mean_square = jnp.mean(raw_k * raw_k, axis=-1, keepdims=True)
    normed = raw_k * lax.rsqrt(mean_square + EPS) * gain_ref[...]
    lane = lax.broadcasted_iota(jnp.int32, (1, width), 1)
    half = width // 2
    index = jnp.where(lane < half, lane, lane - half).astype(jnp.float32)
    angles = pos_ref[...] * jnp.exp(index * (-2.0 * math.log(THETA) / width))
    turned = pltpu.roll(normed, half, 1)
    sine = jnp.sin(angles)
    rotated = normed * jnp.cos(angles) + turned * jnp.where(lane < half, -sine, sine)
    fresh_k[...] = rotated.astype(jnp.bfloat16).astype(jnp.float32)
    fresh_v[...] = raw_v.astype(jnp.bfloat16).astype(jnp.float32)
    loads[5].wait()

    row_ids = lax.broadcasted_iota(jnp.int32, (rows, width), 0)
    column_ids = lax.broadcasted_iota(jnp.int32, (2 * groups, rows), 1)
    step_ids = lax.broadcasted_iota(jnp.int32, (2 * groups, rows), 0) % 2

    def placed(stored, fresh, slot, length):
        full = jnp.where(row_ids < length, stored.astype(jnp.float32), 0.0)
        full = jnp.where(row_ids == length, fresh[pl.ds(2 * slot, 1), :], full)
        full = jnp.where(row_ids == length + 1, fresh[pl.ds(2 * slot + 1, 1), :], full)
        return full.astype(jnp.bfloat16)

    def attend(e, stored_k, stored_v):
        slot, length = live_ref[e], llen_ref[e]
        keys = placed(stored_k, fresh_k, slot, length)
        values = placed(stored_v, fresh_v, slot, length)
        listed[e, :rows, :] = keys
        listed[e, rows:, :] = values
        pltpu.make_async_copy(listed.at[e], list_hbm.at[e], list_sem.at[e]).start()
        q = qry[slot].astype(jnp.float32)
        q = jnp.concatenate([q[:, g * width : (g + 1) * width] for g in range(groups)], axis=0).astype(jnp.bfloat16)
        scores = lax.dot_general(q, keys, (((1,), (1,)), ((), ())), preferred_element_type=jnp.float32) * width ** (-0.5)
        scores = jnp.where(column_ids <= length + step_ids, scores, -jnp.inf)
        weights = jnp.exp(scores - jnp.max(scores, axis=-1, keepdims=True))
        shares = (weights / jnp.sum(weights, axis=-1, keepdims=True)).astype(jnp.bfloat16)
        mix[pl.ds(pl.multiple_of(e * 2 * groups, 2 * groups), 2 * groups), :] = jnp.dot(shares, values, preferred_element_type=jnp.float32)

    def attend_kept(e, _):
        slot = live_ref[e]
        attend(e, ck[slot], cv[slot])
        return 0

    lax.fori_loop(0, kept, attend_kept, 0)
    mix[2 * groups * live :, :] = jnp.zeros((mix.shape[0] - 2 * groups * live, width), jnp.float32)
    reduced[...] = jnp.zeros_like(reduced)
    loads[6].wait()

    def arrived(j, _):
        move(j).wait_recv()
        return 0

    lax.fori_loop(1, replicas, arrived, 0)

    def attend_arrived(i, _):
        source = from_ref[i]
        attend(kept + i, recv[source, :rows, :], recv[source, rows:, :])
        return 0

    lax.fori_loop(0, MOVES, attend_arrived, 0, unroll=2)

    steps = [
        jnp.concatenate([mix[pl.ds(2 * g + t, STEP_ROWS, stride=2 * groups), :] for g in range(groups)], axis=1)
        for t in range(2)
    ]
    mixture = jnp.concatenate(steps, axis=0).astype(jnp.bfloat16)
    out_width = branch_ref.shape[1]

    def part(j):
        first = pl.multiple_of(lax.rem(at + j, tensors) * out_width, 128)
        return jnp.dot(mixture, ow[:, pl.ds(first, out_width)], preferred_element_type=jnp.float32)

    def give(j):
        return pltpu.make_async_remote_copy(
            src_ref=rs_stage.at[j],
            dst_ref=rs_recv.at[j],
            send_sem=rs_send_sem.at[j],
            recv_sem=rs_recv_sem.at[j],
            device_id={"tensor": lax.rem(at + j, tensors)},
            device_id_type=MESH,
        )

    def give_part(j, _):
        rs_stage[j] = part(j).astype(jnp.bfloat16)
        give(j).start()
        return 0

    lax.fori_loop(1, tensors, give_part, 0)
    total = part(0)
    for j in range(1, tensors):
        give(j).wait_recv()
        total = total + rs_recv[j].astype(jnp.float32)
    reduced[: 2 * STEP_ROWS, :] = total.astype(jnp.bfloat16)
    pick = (lax.broadcasted_iota(jnp.int32, row_ref.shape, 1) == row_ref[...]).astype(jnp.float32).astype(jnp.bfloat16)
    branch_ref[...] = jnp.dot(pick, reduced[...], preferred_element_type=jnp.float32).astype(jnp.bfloat16)

    def sent(j, _):
        move(j).wait_send()
        return 0

    lax.fori_loop(1, replicas, sent, 0)

    def given(j, _):
        give(j).wait_send()
        return 0

    lax.fori_loop(1, tensors, given, 0)

    def written(e, _):
        pltpu.make_async_copy(listed.at[e], list_hbm.at[e], list_sem.at[e]).wait()
        return 0

    lax.fori_loop(0, live, written, 0)


def layer(replicas, tensors, scalars, rows_at, gain, hidden, queries, cache_keys, cache_values, key_weight, value_weight, out_weight):
    slots, rows, width = cache_keys.shape
    live = slots - MOVES
    groups = queries.shape[2] // width
    out_width = out_weight.shape[1] // tensors
    smem = pl.BlockSpec(memory_space=pltpu.SMEM)
    vmem = pl.BlockSpec(memory_space=pltpu.VMEM)
    any_ = pl.BlockSpec(memory_space=pl.ANY)
    bf16 = jnp.bfloat16
    dma = pltpu.SemaphoreType.DMA
    operands = (hidden, queries, cache_keys, cache_values, key_weight, value_weight, out_weight)
    return pl.pallas_call(
        functools.partial(layer_kernel, replicas, tensors),
        out_shape=(
            jax.ShapeDtypeStruct((2 * slots, out_width), bf16),
            jax.ShapeDtypeStruct((live, 2 * rows, width), bf16),
        ),
        in_specs=[smem] * 4 + [vmem] * 3 + [any_] * len(operands),
        out_specs=(vmem, any_),
        scratch_shapes=[
            pltpu.VMEM(cache_keys.shape, bf16),
            pltpu.VMEM(cache_values.shape, bf16),
            pltpu.VMEM(hidden.shape, bf16),
            pltpu.VMEM(queries.shape, bf16),
            pltpu.VMEM(key_weight.shape, bf16),
            pltpu.VMEM(value_weight.shape, bf16),
            pltpu.VMEM(out_weight.shape, bf16),
            pltpu.VMEM((replicas, 2 * rows, width), bf16),
            pltpu.VMEM((replicas, 2 * rows, width), bf16),
            pltpu.VMEM((live, 2 * rows, width), bf16),
            pltpu.VMEM((2 * slots, width), jnp.float32),
            pltpu.VMEM((2 * slots, width), jnp.float32),
            pltpu.VMEM((2 * groups * STEP_ROWS, width), jnp.float32),
            pltpu.VMEM((tensors, 2 * STEP_ROWS, out_width), bf16),
            pltpu.VMEM((tensors, 2 * STEP_ROWS, out_width), bf16),
            pltpu.VMEM((128, out_width), bf16),
            dma((len(operands),)),
            dma((replicas,)),
            dma((replicas,)),
            dma((tensors,)),
            dma((tensors,)),
            dma((live,)),
        ],
        compiler_params=pltpu.CompilerParams(
            collective_id=0, has_side_effects=True, vmem_limit_bytes=48 * 1024 * 1024
        ),
    )(*scalars, *rows_at, gain, *operands)


def place_kernel(live_ref, dead_ref, list_hbm, keys_hbm, values_hbm, zeros, sem):
    rows = zeros.shape[0]
    live = list_hbm.shape[0]
    zeros[...] = jnp.zeros_like(zeros)

    def copies(e):
        slot = live_ref[e]
        return (
            pltpu.make_async_copy(list_hbm.at[e, pl.ds(0, rows)], keys_hbm.at[slot], sem.at[e, 0]),
            pltpu.make_async_copy(list_hbm.at[e, pl.ds(rows, rows)], values_hbm.at[slot], sem.at[e, 1]),
        )

    def clears(e):
        slot = dead_ref[e]
        return (
            pltpu.make_async_copy(zeros, keys_hbm.at[slot], sem.at[live + e, 0]),
            pltpu.make_async_copy(zeros, values_hbm.at[slot], sem.at[live + e, 1]),
        )

    for act in ("start", "wait"):
        for make, count in ((copies, live), (clears, MOVES)):

            def each(e, _):
                for copy in make(e):
                    getattr(copy, act)()
                return 0

            lax.fori_loop(0, count, each, 0)


def place(live_slots, dead_slots, listed, slots):
    live, both, width = listed.shape
    shape = jax.ShapeDtypeStruct((slots, both // 2, width), listed.dtype)
    smem = pl.BlockSpec(memory_space=pltpu.SMEM)
    any_ = pl.BlockSpec(memory_space=pl.ANY)
    return pl.pallas_call(
        place_kernel,
        out_shape=(shape, shape),
        in_specs=[smem, smem, any_],
        out_specs=(any_, any_),
        scratch_shapes=[
            pltpu.VMEM((both // 2, width), listed.dtype),
            pltpu.SemaphoreType.DMA((slots, 2)),
        ],
    )(live_slots, dead_slots, listed)


def shards(hidden, queries, cache_keys, cache_values, key_weight, value_weight, key_gain, out_weight, lengths, move_src, move_dst):
    slots = cache_keys.shape[0]
    replicas, tensors = lax.axis_size("replica"), lax.axis_size("tensor")
    me = lax.axis_index("replica").astype(jnp.int32).reshape(1)
    send, source, live, llen, dead, pos, row = plan(me, lengths, move_src, move_dst, slots, replicas)
    branch, listed = layer(
        replicas,
        tensors,
        (send, source, live, llen),
        (pos, row),
        key_gain.reshape(1, -1),
        hidden.reshape(2 * slots, -1),
        queries,
        cache_keys,
        cache_values,
        key_weight,
        value_weight,
        out_weight,
    )
    keys_out, values_out = place(live, dead, listed, slots)
    return (branch.reshape(slots, 2, -1), keys_out, values_out)


def solution(mesh):
    placed = (
        P("replica", None, None),
        P("replica", None, "tensor"),
        P("replica", None, "tensor"),
        P("replica", None, "tensor"),
        P(None, "tensor"),
        P(None, "tensor"),
        P(),
        P("tensor", None),
        P(),
        P(),
        P(),
    )
    return jax.shard_map(
        shards,
        mesh=mesh,
        in_specs=placed,
        out_specs=(
            P("replica", None, "tensor"),
            P("replica", None, "tensor"),
            P("replica", None, "tensor"),
        ),
        check_vma=False,
    )
```

```python
import functools
import math

import jax
import jax.numpy as jnp
from jax import lax
from jax.experimental import pallas as pl
from jax.experimental.pallas import tpu as pltpu
from jax.sharding import PartitionSpec as P

EPS = 1e-06
THETA = 1000000.0
MESH = pl.DeviceIdType.MESH
VMEM_LIMIT = 60 * 1024 * 1024
MOVES = 14
STEP_ROWS = 24
TIERS = (((7, 5, 3, 2), 10), ((8, 6, 4, 2), 11), ((10, 8, 5, 3), 14))


def route(me, lengths, move_src, move_dst, slots, replicas):
    ring = replicas // 4
    count = move_src.shape[0]
    order = jnp.arange(count, dtype=jnp.int32)
    from_rep, to_rep = move_src // slots, move_dst // slots
    ys, zs, cs = from_rep // (2 * ring), (from_rep // 2) % ring, from_rep % 2
    yd, zd = to_rep // (2 * ring), (to_rep // 2) % ring
    ahead = (zd - zs) % ring
    half = ring // 2
    group = (yd * ring + zs) * 2 + cs
    same = group[:, None] == group[None, :]
    before = order[None, :] < order[:, None]
    distance = jnp.where(ahead <= half, ahead, ring - ahead)
    pull = jnp.where(ahead == half, 0, jnp.where(ahead < half, ahead, ahead - ring))
    lean = jnp.sum(jnp.where(same, pull[None, :], 0), axis=1)
    rank_far = jnp.sum(same & before & (ahead == half)[None, :], axis=1, dtype=jnp.int32)
    way = jnp.where(ahead < half, 0, 1)
    for i in range(4):
        back = lean > 0
        way = jnp.where((ahead == half) & (rank_far == i), back.astype(jnp.int32), way)
        lean = lean + jnp.where(back, -half, half)
    travels = ahead != 0
    sort_key = jnp.where(travels, (group * 2 + way) * 8 - distance, -1)
    same_way = (sort_key[:, None] + 7) // 8 == (sort_key[None, :] + 7) // 8
    lower = (sort_key[None, :] < sort_key[:, None]) | ((sort_key[None, :] == sort_key[:, None]) & before)
    place_in = jnp.sum(same_way & lower & travels[None, :], axis=1, dtype=jnp.int32)
    spot = 2 * place_in + way
    crosses = travels & (ys != yd)
    y_key = jnp.where(crosses, from_rep * 64 + spot, -1)
    y_rank = jnp.sum(
        (from_rep[None, :] == from_rep[:, None]) & crosses[None, :] & (y_key[None, :] < y_key[:, None]), axis=1, dtype=jnp.int32
    )

    def fits(caps, y_cap):
        reach = sum((place_in < c).astype(jnp.int32) for c in caps)
        return jnp.all(~travels | ((distance <= reach) & (~crosses | (y_rank < y_cap))))

    tier = jnp.int32(len(TIERS))
    for i, (caps, y_cap) in reversed(list(enumerate(TIERS))):
        tier = jnp.where(fits(caps, y_cap), i, tier)

    my_y, my_z, my_c = me // (2 * ring), (me // 2) % ring, me % 2
    mine = from_rep == me
    in_group = travels & (group == (my_y * ring + my_z) * 2 + my_c)
    kind = jnp.where(ys == yd, 0, jnp.where(cs == to_rep % 2, 1, 2))
    spot_code = jnp.where(mine, move_src % slots, slots + y_rank)
    address = jnp.where(
        in_group,
        jnp.where(spot < 32, spot, -1),
        jnp.where(
            mine,
            jnp.where(travels, jnp.where(y_rank < 16, 32 + y_rank, -1), 48 + kind),
            jnp.where(to_rep == me, 64 + move_dst % slots, -1),
        ),
    )
    code = (((place_in * 2 + way) * 8 + distance) * 4 + kind) * 1024 + move_src + 1
    value = jnp.where(in_group, spot_code, jnp.where(mine, move_src % slots, code))
    wanted = jnp.arange(64 + slots, dtype=jnp.int32)
    table = jnp.sum(jnp.where(wanted[:, None] == address[None, :], value[None, :], 0), axis=1)
    return tier, table


SEND, INJECT, ACROSS, NEAR, LIVE, LENGTH, SOURCE, LANE, SPOT, KIND, TABLE = 0, 32, 64, 80, 96, 128, 160, 176, 192, 208, 224


def plan_kernel(slots, replicas, me_ref, len_ref, src_ref, dst_ref, table_ref, dead_ref, out_ref, row_ref, mark):
    me = me_ref[0]

    def clear(i, _):
        mark[i] = 0
        out_ref[SEND + i] = 0
        return 0

    lax.fori_loop(0, slots, clear, 0, unroll=8)

    def out(k, _):
        s, d = src_ref[me * MOVES + k], dst_ref[me * MOVES + k]
        mark[s % slots] = 1
        out_ref[SEND + (d // slots - me) % replicas] = s % slots
        return 0

    lax.fori_loop(0, MOVES, out, 0, unroll=2)

    def copy(i, _):
        out_ref[INJECT + i] = table_ref[i]
        return 0

    lax.fori_loop(0, 64, copy, 0, unroll=8)

    def each(s, counts):
        kept_count, in_count, dead_count = counts
        code = table_ref[64 + s]
        incoming = code > 0
        source = jnp.where(incoming, (code - 1) % 1024, me * slots + s)
        length = len_ref[source]
        stays = jnp.logical_not(incoming) & (mark[s] == 0) & (length > 0)
        alive = incoming | stays
        length = jnp.where(alive, length, 0)
        at = jnp.where(incoming, slots - 2 * MOVES + in_count, kept_count)
        where = jnp.where(alive, at, slots - 1)
        out_ref[LIVE + where] = s
        out_ref[LENGTH + where] = length
        dead_ref[dead_count] = s
        rest = (code - 1) // 1024
        kind = rest % 4
        distance = (rest // 4) % 8
        way = (rest // 32) % 2
        source_rep = source // slots
        slot_in = jnp.where(incoming, in_count, MOVES)
        out_ref[SOURCE + slot_in] = (me - source_rep) % replicas
        other_core = jnp.where(source_rep % 2 == me % 2, 0, 1)
        out_ref[LANE + slot_in] = (other_core * 2 + way) * 4 + distance - 1
        out_ref[SPOT + slot_in] = rest // 64
        out_ref[KIND + slot_in] = jnp.where(distance == 0, kind, -1)
        for t in range(2):
            row_ref[pl.ds(2 * s + t, 1), :] = jnp.full((1, 128), length + t, jnp.int32).astype(jnp.float32)
            row_ref[pl.ds(2 * (slots + s) + t, 1), :] = jnp.full(
                (1, 128), jnp.where(alive, at + t * STEP_ROWS, -1), jnp.int32
            ).astype(jnp.float32)
        one = jnp.int32(1)
        return (
            kept_count + jnp.where(stays, one, 0),
            in_count + jnp.where(incoming, one, 0),
            dead_count + jnp.where(alive, 0, one),
        )

    zero = jnp.int32(0)
    lax.fori_loop(0, slots, each, (zero, zero, zero))


def plan(me, lengths, move_src, move_dst, table, slots, replicas):
    smem = pl.BlockSpec(memory_space=pltpu.SMEM)
    vmem = pl.BlockSpec(memory_space=pltpu.VMEM)
    ints = lambda n: jax.ShapeDtypeStruct((n,), jnp.int32)
    return pl.pallas_call(
        functools.partial(plan_kernel, slots, replicas),
        out_shape=(ints(slots + 1), ints(TABLE), jax.ShapeDtypeStruct((4 * slots, 128), jnp.float32)),
        in_specs=[smem] * 5,
        out_specs=(smem, smem, vmem),
        scratch_shapes=[pltpu.SMEM((slots,), jnp.int32)],
    )(me, lengths, move_src, move_dst, table)


def timetable(caps, y_cap):
    ready = [(min(i, y_cap - 1) + 2.0, 0, "inject", i % 2, 1, i // 2) for i in range(2 * caps[0])]
    free = [0.0, 0.0]
    events = []
    while ready:
        ready.sort()
        event = ready.pop(0)
        events.append(event[2:])
        time, _, what, way, hop, spot = event
        if what == "inject" or (hop < len(caps) and spot < caps[hop]):
            free[way] = max(free[way], time) + 1.0
            onward = hop if what == "inject" else hop + 1
            ready.append((free[way] + 0.5, 1, "pass", way, onward, spot))
    return events


class Direct:
    def __init__(self, replicas, me, scalars, caches, stage, arrived, send_sem, recv_sem):
        self.replicas, self.me, self.scalars, self.caches = replicas, me, scalars, caches
        self.stage, self.arrived, self.send_sem, self.recv_sem = stage, arrived, send_sem, recv_sem
        self.partners = replicas - 1

    def each(self, act):
        def step(j, _):
            act(j)
            return 0

        lax.fori_loop(1, self.replicas, step, 0)

    def peer(self, j):
        return {"replica": lax.rem(self.me + j, self.replicas)}

    def greet(self, barrier):
        self.each(lambda j: pl.semaphore_signal(barrier, inc=1, device_id=self.peer(j), device_id_type=MESH))

    def move(self, j):
        return pltpu.make_async_remote_copy(
            src_ref=self.stage.at[j],
            dst_ref=self.arrived.at[j],
            send_sem=self.send_sem.at[j],
            recv_sem=self.recv_sem.at[j],
            device_id=self.peer(j),
            device_id_type=MESH,
        )

    def start(self):
        rows = self.caches[0].shape[1]

        def send(j):
            slot = self.scalars[SEND + j]
            self.stage[j, :rows, :] = self.caches[0][slot]
            self.stage[j, rows:, :] = self.caches[1][slot]
            self.move(j).start()

        self.each(send)

    def carry(self):
        self.each(lambda j: self.move(j).wait_recv())

    def where(self, i):
        return self.scalars[SOURCE + i]

    def finish(self):
        self.each(lambda j: self.move(j).wait_send())


class Ring:
    def __init__(self, tier, replicas, me, scalars, caches, arrived, inject, across, across_in, near, *sems):
        self.caps, self.y_cap = tier
        self.me, self.scalars, self.caches = me, scalars, caches
        self.arrived, self.inject, self.across, self.across_in, self.near = arrived, inject, across, across_in, near
        self.hop_send, self.hop_recv, self.core_send, self.core_recv, self.y_send, self.y_recv, self.near_send, self.near_recv = sems
        half = replicas // 2
        line = (me // half) * half
        ahead = line + lax.rem(me - line + 2, half)
        behind = line + lax.rem(me - line + half - 2, half)
        core = me + 1 - 2 * lax.rem(me, 2)
        opposite = lax.rem(me + half, replicas)
        both = lax.rem(core + half, replicas)
        self.ways = (ahead, behind)
        self.core, self.opposite = core, opposite
        self.near_peers = (core, opposite, both)
        self.partners = 5
        self.events = timetable(self.caps, self.y_cap)
        self.lanes = 2 * len(self.caps) * self.caps[0]

    def greet(self, barrier):
        for peer in self.ways + self.near_peers:
            pl.semaphore_signal(barrier, inc=1, device_id={"replica": peer}, device_id_type=MESH)

    def copy(self, source, target, send_sem, recv_sem, peer):
        return pltpu.make_async_remote_copy(
            src_ref=source, dst_ref=target, send_sem=send_sem, recv_sem=recv_sem, device_id={"replica": peer}, device_id_type=MESH
        )

    def lane(self, way, hop, spot):
        return (way * len(self.caps) + hop - 1) * self.caps[0] + spot

    def cross(self, b):
        return self.copy(self.across.at[b], self.across_in.at[b], self.y_send.at[b], self.y_recv.at[b], self.opposite)

    def next_door(self, j):
        target = self.arrived.at[2 * self.lanes + j]
        return self.copy(self.near.at[j], target, self.near_send.at[j], self.near_recv.at[j], self.near_peers[j])

    def hop(self, way, hop, spot):
        source = self.inject.at[2 * spot + way] if hop == 1 else self.arrived.at[self.lane(way, hop - 1, spot)]
        to = self.lane(way, hop, spot)
        return self.copy(source, self.arrived.at[to], self.hop_send.at[to], self.hop_recv.at[to], self.ways[way])

    def hand_over(self, way, hop, spot):
        at = self.lane(way, hop, spot)
        return self.copy(
            self.arrived.at[at], self.arrived.at[self.lanes + at], self.core_send.at[at], self.core_recv.at[at], self.core
        )

    def pack(self, target, at, slot):
        rows = self.caches[0].shape[1]
        target[at, :rows, :] = self.caches[0][slot]
        target[at, rows:, :] = self.caches[1][slot]

    def start(self):
        for b in range(self.y_cap):
            self.pack(self.across, b, self.scalars[ACROSS + b])
            self.cross(b).start()
        for j in range(3):
            self.pack(self.near, j, self.scalars[NEAR + j])
            self.next_door(j).start()

    def carry(self):
        slots, rows, _ = self.caches[0].shape
        crossed = 0
        for what, way, hop, spot in self.events:
            if what == "inject":
                i = 2 * spot + way
                while crossed < min(i + 1, self.y_cap):
                    self.cross(crossed).wait_recv()
                    crossed += 1
                code = self.scalars[INJECT + i]
                slot = jnp.where(code < slots, code, 0)
                for part in range(2):
                    block = self.caches[part][slot]
                    for b in range(crossed):
                        block = jnp.where(code == slots + b, self.across_in[b, part * rows : (part + 1) * rows, :], block)
                    self.inject[i, part * rows : (part + 1) * rows, :] = block
                self.hop(way, 1, spot).start()
            else:
                self.hop(way, hop, spot).wait_recv()
                if hop < len(self.caps) and spot < self.caps[hop]:
                    self.hop(way, hop + 1, spot).start()
                self.hand_over(way, hop, spot).start()
        for j in range(3):
            self.next_door(j).wait_recv()
        for what, way, hop, spot in self.events:
            if what == "pass":
                self.hand_over(way, hop, spot).wait_recv()

    def where(self, i):
        kind = self.scalars[KIND + i]
        return jnp.where(kind >= 0, 2 * self.lanes + kind, self.scalars[LANE + i] * self.caps[0] + self.scalars[SPOT + i])

    def finish(self):
        for b in range(self.y_cap):
            self.cross(b).wait_send()
        for j in range(3):
            self.next_door(j).wait_send()
        for what, way, hop, spot in self.events:
            if what == "pass":
                self.hop(way, hop, spot).wait_send()
                self.hand_over(way, hop, spot).wait_send()


def layer_kernel(
    replicas,
    tensors,
    tier,
    scalar_ref,
    row_ref,
    gain_ref,
    hidden_hbm,
    query_hbm,
    ck_hbm,
    cv_hbm,
    kw_hbm,
    vw_hbm,
    ow_hbm,
    branch_ref,
    list_hbm,
    ck,
    cv,
    hid,
    qry,
    kw,
    vw,
    ow,
    listed,
    fresh_k,
    fresh_v,
    mix,
    rs_stage,
    rs_recv,
    reduced,
    in_sem,
    rs_send_sem,
    rs_recv_sem,
    list_sem,
    *transport,
):
    me = lax.axis_index("replica")
    at = lax.axis_index("tensor")
    slots, rows, width = ck.shape
    live = listed.shape[0]
    kept = live - MOVES
    groups = query_hbm.shape[2] // width

    loads = [
        pltpu.make_async_copy(source, target, in_sem.at[i])
        for i, (source, target) in enumerate(
            (
                (ck_hbm, ck),
                (cv_hbm, cv),
                (hidden_hbm, hid),
                (kw_hbm, kw),
                (vw_hbm, vw),
                (query_hbm, qry),
                (ow_hbm, ow),
            )
        )
    ]
    for load in loads:
        load.start()

    caches = (ck, cv)
    if tier is None:
        road = Direct(replicas, me, scalar_ref, caches, *transport)
    else:
        road = Ring(tier, replicas, me, scalar_ref, caches, *transport)

    barrier = pltpu.get_barrier_semaphore()
    road.greet(barrier)

    def greet_tensor(j, _):
        pl.semaphore_signal(barrier, inc=1, device_id={"tensor": lax.rem(at + j, tensors)}, device_id_type=MESH)
        return 0

    lax.fori_loop(1, tensors, greet_tensor, 0)
    pl.semaphore_wait(barrier, road.partners + tensors - 1)

    loads[0].wait()
    loads[1].wait()
    road.start()

    loads[2].wait()
    loads[3].wait()
    loads[4].wait()
    raw_k = jnp.dot(hid[...], kw[...], preferred_element_type=jnp.float32)
    raw_v = jnp.dot(hid[...], vw[...], preferred_element_type=jnp.float32)
    mean_square = jnp.mean(raw_k * raw_k, axis=-1, keepdims=True)
    normed = raw_k * lax.rsqrt(mean_square + EPS) * gain_ref[...]
    lane = lax.broadcasted_iota(jnp.int32, (1, width), 1)
    half = width // 2
    index = jnp.where(lane < half, lane, lane - half).astype(jnp.float32)
    angles = row_ref[: 2 * slots, :] * jnp.exp(index * (-2.0 * math.log(THETA) / width))
    turned = pltpu.roll(normed, half, 1)
    sine = jnp.sin(angles)
    rotated = normed * jnp.cos(angles) + turned * jnp.where(lane < half, -sine, sine)
    fresh_k[...] = rotated.astype(jnp.bfloat16).astype(jnp.float32)
    fresh_v[...] = raw_v.astype(jnp.bfloat16).astype(jnp.float32)
    loads[5].wait()

    row_ids = lax.broadcasted_iota(jnp.int32, (rows, width), 0)
    column_ids = lax.broadcasted_iota(jnp.int32, (2 * groups, rows), 1)
    step_ids = lax.broadcasted_iota(jnp.int32, (2 * groups, rows), 0) % 2

    def placed(stored, fresh, slot, length):
        full = jnp.where(row_ids < length, stored.astype(jnp.float32), 0.0)
        full = jnp.where(row_ids == length, fresh[pl.ds(2 * slot, 1), :], full)
        full = jnp.where(row_ids == length + 1, fresh[pl.ds(2 * slot + 1, 1), :], full)
        return full.astype(jnp.bfloat16)

    def attend(e, stored_k, stored_v):
        slot, length = scalar_ref[LIVE + e], scalar_ref[LENGTH + e]
        keys = placed(stored_k, fresh_k, slot, length)
        values = placed(stored_v, fresh_v, slot, length)
        listed[e, :rows, :] = keys
        listed[e, rows:, :] = values
        pltpu.make_async_copy(listed.at[e], list_hbm.at[e], list_sem.at[e]).start()
        q = qry[slot].astype(jnp.float32)
        q = jnp.concatenate([q[:, g * width : (g + 1) * width] for g in range(groups)], axis=0).astype(jnp.bfloat16)
        scores = lax.dot_general(q, keys, (((1,), (1,)), ((), ())), preferred_element_type=jnp.float32) * width ** (-0.5)
        scores = jnp.where(column_ids <= length + step_ids, scores, -jnp.inf)
        weights = jnp.exp(scores - jnp.max(scores, axis=-1, keepdims=True))
        shares = (weights / jnp.sum(weights, axis=-1, keepdims=True)).astype(jnp.bfloat16)
        mix[pl.ds(pl.multiple_of(e * 2 * groups, 2 * groups), 2 * groups), :] = jnp.dot(shares, values, preferred_element_type=jnp.float32)

    def attend_kept(e, _):
        slot = scalar_ref[LIVE + e]
        attend(e, ck[slot], cv[slot])
        return 0

    lax.fori_loop(0, kept, attend_kept, 0)
    mix[2 * groups * live :, :] = jnp.zeros((mix.shape[0] - 2 * groups * live, width), jnp.float32)
    reduced[...] = jnp.zeros_like(reduced)
    loads[6].wait()

    road.carry()

    def attend_arrived(i, _):
        source = road.where(i)
        attend(kept + i, road.arrived[source, :rows, :], road.arrived[source, rows:, :])
        return 0

    lax.fori_loop(0, MOVES, attend_arrived, 0, unroll=2)

    steps = [
        jnp.concatenate([mix[pl.ds(2 * g + t, STEP_ROWS, stride=2 * groups), :] for g in range(groups)], axis=1)
        for t in range(2)
    ]
    mixture = jnp.concatenate(steps, axis=0).astype(jnp.bfloat16)
    out_width = branch_ref.shape[1]

    def part(j):
        first = pl.multiple_of(lax.rem(at + j, tensors) * out_width, 128)
        return jnp.dot(mixture, ow[:, pl.ds(first, out_width)], preferred_element_type=jnp.float32)

    def give(j):
        return pltpu.make_async_remote_copy(
            src_ref=rs_stage.at[j],
            dst_ref=rs_recv.at[j],
            send_sem=rs_send_sem.at[j],
            recv_sem=rs_recv_sem.at[j],
            device_id={"tensor": lax.rem(at + j, tensors)},
            device_id_type=MESH,
        )

    def give_part(j, _):
        rs_stage[j] = part(j).astype(jnp.bfloat16)
        give(j).start()
        return 0

    lax.fori_loop(1, tensors, give_part, 0)
    total = part(0)
    for j in range(1, tensors):
        give(j).wait_recv()
        total = total + rs_recv[j].astype(jnp.float32)
    reduced[: 2 * STEP_ROWS, :] = total.astype(jnp.bfloat16)
    rows_at = row_ref[2 * slots :, :]
    pick = (lane.astype(jnp.float32) == rows_at).astype(jnp.float32).astype(jnp.bfloat16)
    branch_ref[...] = jnp.dot(pick, reduced[...], preferred_element_type=jnp.float32).astype(jnp.bfloat16)

    road.finish()

    def given(j, _):
        give(j).wait_send()
        return 0

    lax.fori_loop(1, tensors, given, 0)

    def written(e, _):
        pltpu.make_async_copy(listed.at[e], list_hbm.at[e], list_sem.at[e]).wait()
        return 0

    lax.fori_loop(0, live, written, 0)


def layer(tier, replicas, tensors, scalars, rows_at, gain, *operands):
    hidden, queries, cache_keys, cache_values, key_weight, value_weight, out_weight = operands
    slots, rows, width = cache_keys.shape
    live = slots - MOVES
    groups = queries.shape[2] // width
    out_width = out_weight.shape[1] // tensors
    smem = pl.BlockSpec(memory_space=pltpu.SMEM)
    vmem = pl.BlockSpec(memory_space=pltpu.VMEM)
    any_ = pl.BlockSpec(memory_space=pl.ANY)
    bf16 = jnp.bfloat16
    dma = pltpu.SemaphoreType.DMA

    def rollouts(n):
        return pltpu.VMEM((n, 2 * rows, width), bf16)

    if tier is None:
        transport = [rollouts(replicas), rollouts(replicas), dma((replicas,)), dma((replicas,))]
    else:
        caps, y_cap = tier
        lanes = 2 * len(caps) * caps[0]
        transport = [
            rollouts(2 * lanes + 3),
            rollouts(2 * caps[0]),
            rollouts(y_cap),
            rollouts(y_cap),
            rollouts(3),
        ] + [dma((n,)) for n in (lanes, lanes, lanes, lanes, y_cap, y_cap, 3, 3)]
    return pl.pallas_call(
        functools.partial(layer_kernel, replicas, tensors, tier),
        out_shape=(
            jax.ShapeDtypeStruct((2 * slots, out_width), bf16),
            jax.ShapeDtypeStruct((live, 2 * rows, width), bf16),
        ),
        in_specs=[smem] + [vmem] * 2 + [any_] * len(operands),
        out_specs=(vmem, any_),
        scratch_shapes=[
            pltpu.VMEM(cache_keys.shape, bf16),
            pltpu.VMEM(cache_values.shape, bf16),
            pltpu.VMEM(hidden.shape, bf16),
            pltpu.VMEM(queries.shape, bf16),
            pltpu.VMEM(key_weight.shape, bf16),
            pltpu.VMEM(value_weight.shape, bf16),
            pltpu.VMEM(out_weight.shape, bf16),
            pltpu.VMEM((live, 2 * rows, width), bf16),
            pltpu.VMEM((2 * slots, width), jnp.float32),
            pltpu.VMEM((2 * slots, width), jnp.float32),
            pltpu.VMEM((2 * groups * STEP_ROWS, width), jnp.float32),
            pltpu.VMEM((tensors, 2 * STEP_ROWS, out_width), bf16),
            pltpu.VMEM((tensors, 2 * STEP_ROWS, out_width), bf16),
            pltpu.VMEM((128, out_width), bf16),
            dma((len(operands),)),
            dma((tensors,)),
            dma((tensors,)),
            dma((live,)),
        ]
        + transport,
        compiler_params=pltpu.CompilerParams(
            collective_id=len(TIERS) if tier is None else TIERS.index(tier),
            has_side_effects=True,
            vmem_limit_bytes=VMEM_LIMIT,
        ),
    )(scalars, rows_at, gain, *operands)


def place_kernel(scalar_ref, dead_ref, list_hbm, keys_hbm, values_hbm, listed, zeros, sem):
    rows = zeros.shape[0]
    live = listed.shape[0]
    load = pltpu.make_async_copy(list_hbm, listed, sem.at[live + MOVES, 0])
    load.start()
    zeros[...] = jnp.zeros_like(zeros)

    def copies(e):
        slot = scalar_ref[LIVE + e]
        return (
            pltpu.make_async_copy(listed.at[e, pl.ds(0, rows)], keys_hbm.at[slot], sem.at[e, 0]),
            pltpu.make_async_copy(listed.at[e, pl.ds(rows, rows)], values_hbm.at[slot], sem.at[e, 1]),
        )

    def clears(e):
        slot = dead_ref[e]
        return (
            pltpu.make_async_copy(zeros, keys_hbm.at[slot], sem.at[live + e, 0]),
            pltpu.make_async_copy(zeros, values_hbm.at[slot], sem.at[live + e, 1]),
        )

    def run(make, count, act):
        def each(e, _):
            for copy in make(e):
                getattr(copy, act)()
            return 0

        lax.fori_loop(0, count, each, 0)

    run(clears, MOVES, "start")
    load.wait()
    run(copies, live, "start")
    run(clears, MOVES, "wait")
    run(copies, live, "wait")


def place(scalars, dead_slots, listed, slots):
    live, both, width = listed.shape
    shape = jax.ShapeDtypeStruct((slots, both // 2, width), listed.dtype)
    smem = pl.BlockSpec(memory_space=pltpu.SMEM)
    any_ = pl.BlockSpec(memory_space=pl.ANY)
    return pl.pallas_call(
        place_kernel,
        out_shape=(shape, shape),
        in_specs=[smem, smem, any_],
        out_specs=(any_, any_),
        scratch_shapes=[
            pltpu.VMEM(listed.shape, listed.dtype),
            pltpu.VMEM((both // 2, width), listed.dtype),
            pltpu.SemaphoreType.DMA((slots + 1, 2)),
        ],
    )(scalars, dead_slots, listed)


def shards(hidden, queries, cache_keys, cache_values, key_weight, value_weight, key_gain, out_weight, lengths, move_src, move_dst):
    slots = cache_keys.shape[0]
    replicas, tensors = lax.axis_size("replica"), lax.axis_size("tensor")
    me = lax.axis_index("replica").astype(jnp.int32)
    tier, table = route(me, lengths, move_src, move_dst, slots, replicas)
    dead, scalars, rows_at = plan(me.reshape(1), lengths, move_src, move_dst, table, slots, replicas)
    operands = (
        scalars,
        rows_at,
        key_gain.reshape(1, -1),
        hidden.reshape(2 * slots, -1),
        queries,
        cache_keys,
        cache_values,
        key_weight,
        value_weight,
        out_weight,
    )
    branches = [functools.partial(layer, t, replicas, tensors) for t in TIERS + (None,)]
    branch, listed = lax.switch(tier, branches, *operands)
    keys_out, values_out = place(scalars, dead, listed, slots)
    return (branch.reshape(slots, 2, -1), keys_out, values_out)


def solution(mesh):
    placed = (
        P("replica", None, None),
        P("replica", None, "tensor"),
        P("replica", None, "tensor"),
        P("replica", None, "tensor"),
        P(None, "tensor"),
        P(None, "tensor"),
        P(),
        P("tensor", None),
        P(),
        P(),
        P(),
    )
    return jax.shard_map(
        shards,
        mesh=mesh,
        in_specs=placed,
        out_specs=(
            P("replica", None, "tensor"),
            P("replica", None, "tensor"),
            P("replica", None, "tensor"),
        ),
        check_vma=False,
    )
```

```python
import functools
import math

import jax
import jax.numpy as jnp
from jax import lax
from jax.experimental import pallas as pl
from jax.experimental.pallas import tpu as pltpu
from jax.sharding import PartitionSpec as P

EPS = 1e-06
THETA = 1000000.0
MESH = pl.DeviceIdType.MESH
VMEM_LIMIT = 60 * 1024 * 1024
MOVES = 14
STEP_ROWS = 24
TIERS = (((7, 5, 3, 2), 10), ((8, 6, 4, 2), 11), ((9, 7, 5, 3), 12), ((16, 12, 8, 4), 14))
PARTS = 2
Y_WINDOW = 6
HAND_WINDOW = 6
PAUSES = (5, 9, 13, 17, 21)


def route(slots, replicas, me, src, dst, column):
    ring = replicas // 4
    half = ring // 2
    moves = src.shape[1]
    order = lax.broadcasted_iota(jnp.int32, (1, moves), 1)
    exists = order < replicas * MOVES
    from_rep, to_rep = src // slots, dst // slots
    ys, zs, cs = from_rep // (2 * ring), (from_rep // 2) % ring, from_rep % 2
    yd, zd = to_rep // (2 * ring), (to_rep // 2) % ring
    ahead = jnp.where(exists, (zd - zs + ring) % ring, 0)
    group = (yd * ring + zs) * 2 + cs
    distance = jnp.where(ahead <= half, ahead, ring - ahead)
    travels = ahead != 0
    pull = jnp.where((ahead == half) | ~travels, 0, jnp.where(ahead < half, ahead, ahead - ring))
    farthest = ahead == half

    def count(hits):
        return jnp.sum(jnp.where(hits, 1, 0), axis=0, keepdims=True)

    other = column(order)
    before = other < order
    same = column(group) == group
    lean = jnp.sum(jnp.where(same, column(pull), 0), axis=0, keepdims=True)
    rank_far = count((column(jnp.where(farthest, group, -1)) == group) & before)
    way = jnp.where(ahead < half, 0, 1)
    for i in range(4):
        back = lean > 0
        way = jnp.where(farthest & (rank_far == i), jnp.where(back, 1, 0), way)
        lean = lean + jnp.where(back, -half, half)
    list_key = group * 2 + way
    sort_key = (list_key * 8 + 7 - distance) * moves + order
    other_list = column(jnp.where(travels, list_key, -1))
    place_in = count((other_list == list_key) & (column(sort_key) < sort_key))
    spot = 2 * place_in + way
    crosses = travels & (ys != yd)
    y_key = from_rep * 64 + spot
    other_y = column(jnp.where(crosses, y_key, -1))
    y_rank = count((other_y >= from_rep * 64) & (other_y < y_key))

    tier = jnp.full((1, 1), len(TIERS) - 1, jnp.int32)
    for i, (caps, y_cap) in reversed(list(enumerate(TIERS[:-1]))):
        reach = sum(jnp.where(place_in < c, 1, 0) for c in caps)
        misfit = travels & ((distance > reach) | (crosses & (y_rank >= y_cap)))
        tier = jnp.where(jnp.sum(jnp.where(misfit, 1, 0), axis=1, keepdims=True) == 0, i, tier)

    my_y, my_z, my_c = me // (2 * ring), (me // 2) % ring, me % 2
    mine = exists & (from_rep == me)
    in_group = travels & (group == (my_y * ring + my_z) * 2 + my_c)
    kind = jnp.where(ys == yd, 0, jnp.where(cs == to_rep % 2, 1, 2))
    address = jnp.where(
        in_group,
        spot,
        jnp.where(
            mine,
            jnp.where(travels, 32 + y_rank, 48 + kind),
            jnp.where(exists & (to_rep == me), 64 + dst % slots, -1),
        ),
    )
    code = (((place_in * 2 + way) * 8 + distance) * 4 + kind) * 1024 + src + 1
    value = jnp.where(in_group, jnp.where(mine, src % slots, slots + y_rank), jnp.where(mine, src % slots, code))
    width = 128
    lane = lax.broadcasted_iota(jnp.int32, (1, width), 1)
    hit = column(address)[:, :width] == lane
    table = jnp.sum(jnp.where(hit, column(value)[:, :width], 0), axis=0, keepdims=True)
    return jnp.where(lane == width - 1, tier, table)


INJECT, ACROSS, NEAR, LIVE, LENGTH, LANE, SPOT, KIND, TABLE = 0, 32, 48, 64, 96, 128, 144, 160, 176


def plan_kernel(
    slots,
    replicas,
    me_ref,
    len_ref,
    src_ref,
    src_row,
    dst_row,
    tier_ref,
    dead_ref,
    out_ref,
    row_ref,
    mark,
    padded,
    table_vmem,
    table_ref,
    sem,
):
    me = me_ref[0]
    moves = padded.shape[1]
    count = src_row.shape[1]
    padded[...] = jnp.zeros_like(padded)
    padded[0:1, :count] = src_row[...]
    padded[1:2, :count] = dst_row[...]

    def column(row):
        tall = jnp.broadcast_to(row.astype(jnp.float32), (128, moves))
        tall = jnp.concatenate([tall[:, i : i + 128].T for i in range(0, moves, 128)], axis=0).astype(jnp.int32)
        return jnp.concatenate([tall] * (moves // 128), axis=1)

    table_vmem[...] = route(slots, replicas, me, padded[0:1, :], padded[1:2, :], column)
    fetch = pltpu.make_async_copy(table_vmem, table_ref, sem)
    fetch.start()

    def clear(i, _):
        mark[i] = 0
        return 0

    lax.fori_loop(0, slots, clear, 0, unroll=8)

    def out(k, _):
        mark[src_ref[me * MOVES + k] % slots] = 1
        return 0

    lax.fori_loop(0, MOVES, out, 0, unroll=2)
    fetch.wait()
    tier_ref[0] = table_ref[0, 127]

    def copy(i, _):
        out_ref[INJECT + i] = table_ref[0, i]
        return 0

    lax.fori_loop(0, 64, copy, 0, unroll=8)

    def each(s, counts):
        kept_count, in_count, dead_count = counts
        code = table_ref[0, 64 + s]
        incoming = code > 0
        source = jnp.where(incoming, (code - 1) % 1024, me * slots + s)
        length = len_ref[source]
        stays = jnp.logical_not(incoming) & (mark[s] == 0) & (length > 0)
        alive = incoming | stays
        length = jnp.where(alive, length, 0)
        at = jnp.where(incoming, slots - 2 * MOVES + in_count, kept_count)
        where = jnp.where(alive, at, slots - 1)
        out_ref[LIVE + where] = s
        out_ref[LENGTH + where] = length
        dead_ref[dead_count] = s
        rest = (code - 1) // 1024
        kind = rest % 4
        distance = (rest // 4) % 8
        way = (rest // 32) % 2
        source_rep = source // slots
        slot_in = jnp.where(incoming, in_count, MOVES)
        other_core = jnp.where(source_rep % 2 == me % 2, 0, 1)
        out_ref[LANE + slot_in] = (other_core * 2 + way) * 4 + distance - 1
        out_ref[SPOT + slot_in] = rest // 64
        out_ref[KIND + slot_in] = jnp.where(distance == 0, kind, -1)
        for t in range(2):
            row_ref[pl.ds(2 * s + t, 1), :] = jnp.full((1, 128), length + t, jnp.int32).astype(jnp.float32)
            row_ref[pl.ds(2 * (slots + s) + t, 1), :] = jnp.full(
                (1, 128), jnp.where(alive, at + t * STEP_ROWS, -1), jnp.int32
            ).astype(jnp.float32)
        one = jnp.int32(1)
        return (
            kept_count + jnp.where(stays, one, 0),
            in_count + jnp.where(incoming, one, 0),
            dead_count + jnp.where(alive, 0, one),
        )

    zero = jnp.int32(0)
    lax.fori_loop(0, slots, each, (zero, zero, zero), unroll=2)


def plan(me, lengths, move_src, move_dst, slots, replicas):
    smem = pl.BlockSpec(memory_space=pltpu.SMEM)
    vmem = pl.BlockSpec(memory_space=pltpu.VMEM)
    ints = lambda n: jax.ShapeDtypeStruct((n,), jnp.int32)
    moves = -(-move_src.shape[0] // 128) * 128
    return pl.pallas_call(
        functools.partial(plan_kernel, slots, replicas),
        out_shape=(ints(1), ints(slots + 1), ints(TABLE), jax.ShapeDtypeStruct((4 * slots, 128), jnp.float32)),
        in_specs=[smem] * 3 + [vmem] * 2,
        out_specs=(smem,) * 3 + (vmem,),
        scratch_shapes=[
            pltpu.SMEM((slots,), jnp.int32),
            pltpu.VMEM((8, moves), jnp.int32),
            pltpu.VMEM((1, 128), jnp.int32),
            pltpu.SMEM((1, 128), jnp.int32),
            pltpu.SemaphoreType.DMA,
        ],
    )(me, lengths, move_src, move_src.reshape(1, -1), move_dst.reshape(1, -1))


def crossings(y_cap):
    return [(b, part) for low in range(0, y_cap, 2) for part in range(PARTS) for b in range(low, min(low + 2, y_cap))]


def timetable(caps, y_cap):
    step, lag = 1.0 / PARTS, 0.5
    across = {key: (n + 1) * step + lag for n, key in enumerate(crossings(y_cap))}
    ready = [
        (across[min(i, y_cap - 1), part] + 0.01 * max(0, i - y_cap), 1, "inject", i % 2, 1, i // 2, part)
        for i in range(2 * caps[0])
        for part in range(PARTS)
    ]
    free = [0.0, 0.0]
    events = []
    while ready:
        ready.sort()
        time, _, what, way, hop, spot, part = event = ready.pop(0)
        events.append(event[2:])
        if what == "inject" or (hop < len(caps) and spot < caps[hop]):
            free[way] = max(free[way], time) + step
            onward = hop if what == "inject" else hop + 1
            ready.append((free[way] + lag, 0, "pass", way, onward, spot, part))
    return events


class Ring:
    def __init__(self, tier, replicas, me, scalars, caches, arrived, inject, across, across_in, near, *sems):
        self.caps, self.y_cap = tier
        self.me, self.scalars, self.caches = me, scalars, caches
        self.arrived, self.inject, self.across, self.across_in, self.near = arrived, inject, across, across_in, near
        self.hop_send, self.hop_recv, self.core_send, self.core_recv, self.y_send, self.y_recv, self.near_send, self.near_recv = sems
        half = replicas // 2
        line = (me // half) * half
        ahead = line + lax.rem(me - line + 2, half)
        behind = line + lax.rem(me - line + half - 2, half)
        core = me + 1 - 2 * lax.rem(me, 2)
        opposite = lax.rem(me + half, replicas)
        both = lax.rem(core + half, replicas)
        self.ways = (ahead, behind)
        self.core, self.opposite = core, opposite
        self.near_peers = (core, opposite, both)
        self.partners = 5
        self.events = timetable(self.caps, self.y_cap)
        self.lanes = 2 * sum(self.caps)

    def greet(self, barrier):
        for peer in self.ways + self.near_peers:
            pl.semaphore_signal(barrier, inc=1, device_id={"replica": peer}, device_id_type=MESH)

    def copy(self, source, target, send_sem, recv_sem, peer):
        return pltpu.make_async_remote_copy(
            src_ref=source, dst_ref=target, send_sem=send_sem, recv_sem=recv_sem, device_id={"replica": peer}, device_id_type=MESH
        )

    def lane(self, way, hop, spot):
        return way * sum(self.caps) + sum(self.caps[: hop - 1]) + spot

    def half(self, ref, at, part):
        rows = self.caches[0].shape[1]
        return ref.at[at, pl.ds(part * rows, rows)]

    def cross(self, b, part):
        at = b * PARTS + part
        return self.copy(
            self.half(self.across, b, part), self.half(self.across_in, b, part), self.y_send.at[at], self.y_recv.at[at], self.opposite
        )

    def next_door(self, j):
        target = self.arrived.at[2 * self.lanes + j]
        return self.copy(self.near.at[j], target, self.near_send.at[j], self.near_recv.at[j], self.near_peers[j])

    def hop(self, way, hop, spot, part):
        source = (self.inject, 2 * spot + way) if hop == 1 else (self.arrived, self.lane(way, hop - 1, spot))
        to = self.lane(way, hop, spot)
        at = to * PARTS + part
        return self.copy(
            self.half(*source, part), self.half(self.arrived, to, part), self.hop_send.at[at], self.hop_recv.at[at], self.ways[way]
        )

    def hand_over(self, way, hop, spot, part):
        lane = self.lane(way, hop, spot)
        at = lane * PARTS + part
        return self.copy(
            self.half(self.arrived, lane, part),
            self.half(self.arrived, self.lanes + lane, part),
            self.core_send.at[at],
            self.core_recv.at[at],
            self.core,
        )

    def pack(self, target, at, slot, parts):
        rows = self.caches[0].shape[1]
        for part in parts:
            target[at, part * rows : (part + 1) * rows, :] = self.caches[part][slot]

    def begin(self, n):
        order = crossings(self.y_cap)
        if n < len(order):
            b, part = order[n]
            self.pack(self.across, b, self.scalars[ACROSS + b], (part,))
            self.cross(b, part).start()
        elif n < len(order) + 3:
            j = n - len(order)
            self.pack(self.near, j, self.scalars[NEAR + j], range(PARTS))
            self.next_door(j).start()

    def enter(self, way, spot, part, crossed):
        slots, rows, _ = self.caches[0].shape
        i = 2 * spot + way
        here = slice(part * rows, (part + 1) * rows)
        code = self.scalars[INJECT + i]
        block = self.caches[part][jnp.where(code < slots, code, 0)]
        if crossed == len(crossings(self.y_cap)):
            other = self.across_in[jnp.where(code < slots, 0, code - slots), here, :]
            block = jnp.where(code < slots, block, other)
        else:
            for b in range(min(i + 1, self.y_cap)):
                block = jnp.where(code == slots + b, self.across_in[b, here, :], block)
        self.inject[i, here, :] = block
        self.hop(way, 1, spot, part).start()

    def carry(self, pauses):
        order = crossings(self.y_cap)
        for n in range(Y_WINDOW):
            self.begin(n)
        crossed = 0
        pauses = dict(pauses)
        over = []
        for count, (what, way, hop, spot, part) in enumerate(self.events):
            if what == "inject":
                needed = order.index((min(2 * spot + way, self.y_cap - 1), part)) + 1
                while crossed < needed:
                    self.cross(*order[crossed]).wait_recv()
                    self.begin(crossed + Y_WINDOW)
                    crossed += 1
                self.enter(way, spot, part, crossed)
            else:
                self.hop(way, hop, spot, part).wait_recv()
                if hop < len(self.caps) and spot < self.caps[hop]:
                    self.hop(way, hop + 1, spot, part).start()
                self.hand_over(way, hop, spot, part).start()
                over.append((way, hop, spot, part))
                if len(over) > HAND_WINDOW:
                    self.hand_over(*over[-1 - HAND_WINDOW]).wait()
            if count in pauses:
                pauses.pop(count)()
        for pause in pauses.values():
            pause()
        for n in range(crossed, len(order)):
            self.cross(*order[n]).wait_recv()
        for n in range(max(Y_WINDOW, crossed + Y_WINDOW), len(order) + 3):
            self.begin(n)
        for j in range(3):
            self.next_door(j).wait_recv()
        for key in over[-HAND_WINDOW:]:
            self.hand_over(*key).wait()

    def where(self, i):
        kind, lane = self.scalars[KIND + i], self.scalars[LANE + i]
        first = 0
        for n in range(2 * 2 * len(self.caps)):
            way, hop = n // len(self.caps) % 2, n % len(self.caps) + 1
            first = jnp.where(lane == n, n // (2 * len(self.caps)) * self.lanes + self.lane(way, hop, 0), first)
        return jnp.where(kind >= 0, 2 * self.lanes + kind, first + self.scalars[SPOT + i])

    def finish(self):
        for b, part in crossings(self.y_cap):
            self.cross(b, part).wait_send()
        for j in range(3):
            self.next_door(j).wait_send()
        for what, way, hop, spot, part in self.events:
            if what == "pass":
                self.hop(way, hop, spot, part).wait_send()


def layer_kernel(
    replicas,
    tensors,
    tier,
    scalar_ref,
    row_ref,
    gain_ref,
    hidden_hbm,
    query_hbm,
    ck_hbm,
    cv_hbm,
    kw_hbm,
    vw_hbm,
    ow_hbm,
    branch_ref,
    list_hbm,
    ck,
    cv,
    hid,
    qry,
    kw,
    vw,
    ow,
    flat,
    listed,
    fresh_k,
    fresh_v,
    mix,
    score,
    rs_stage,
    rs_recv,
    reduced,
    in_sem,
    rs_send_sem,
    rs_recv_sem,
    list_sem,
    *transport,
):
    me = lax.axis_index("replica")
    at = lax.axis_index("tensor")
    slots, rows, width = ck.shape
    live = listed.shape[0]
    kept = live - MOVES
    groups = query_hbm.shape[2] // width

    loads = [
        pltpu.make_async_copy(source, target, in_sem.at[i])
        for i, (source, target) in enumerate(
            (
                (ck_hbm, ck),
                (cv_hbm, cv),
                (hidden_hbm, hid),
                (kw_hbm, kw),
                (vw_hbm, vw),
                (query_hbm, qry),
                (ow_hbm, ow),
            )
        )
    ]
    loads[0].start()
    loads[1].start()

    caches = (ck, cv)
    road = Ring(tier, replicas, me, scalar_ref, caches, *transport)

    barrier = pltpu.get_barrier_semaphore()
    road.greet(barrier)

    def greet_tensor(j, _):
        pl.semaphore_signal(barrier, inc=1, device_id={"tensor": lax.rem(at + j, tensors)}, device_id_type=MESH)
        return 0

    lax.fori_loop(1, tensors, greet_tensor, 0)
    pl.semaphore_wait(barrier, road.partners + tensors - 1)

    loads[0].wait()
    loads[1].wait()
    for load in loads[2:]:
        load.start()

    def flatten():
        loads[2].wait()
        for s in range(slots):
            flat[2 * s : 2 * s + 2, :] = hid[s]

    def project_keys():
        loads[3].wait()
        fresh_k[...] = jnp.dot(flat[...], kw[...], preferred_element_type=jnp.float32)

    def project_values():
        loads[4].wait()
        raw_v = jnp.dot(flat[...], vw[...], preferred_element_type=jnp.float32)
        fresh_v[...] = raw_v.astype(jnp.bfloat16).astype(jnp.float32)

    lane = lax.broadcasted_iota(jnp.int32, (1, width), 1)

    def rotate_keys():
        raw_k = fresh_k[...]
        mean_square = jnp.mean(raw_k * raw_k, axis=-1, keepdims=True)
        normed = raw_k * lax.rsqrt(mean_square + EPS) * gain_ref[...]
        half = width // 2
        index = jnp.where(lane < half, lane, lane - half).astype(jnp.float32)
        angles = row_ref[: 2 * slots, :] * jnp.exp(index * (-2.0 * math.log(THETA) / width))
        turned = pltpu.roll(normed, half, 1)
        sine = jnp.sin(angles)
        rotated = normed * jnp.cos(angles) + turned * jnp.where(lane < half, -sine, sine)
        fresh_k[...] = rotated.astype(jnp.bfloat16).astype(jnp.float32)

    row_ids = lax.broadcasted_iota(jnp.int32, (rows, width), 0)
    column_ids = lax.broadcasted_iota(jnp.int32, (2 * groups, rows), 1)
    step_ids = lax.broadcasted_iota(jnp.int32, (2 * groups, rows), 0) % 2

    def placed(stored, fresh, slot, length):
        full = jnp.where(row_ids < length, stored.astype(jnp.float32), 0.0)
        full = jnp.where(row_ids == length, fresh[pl.ds(2 * slot, 1), :], full)
        full = jnp.where(row_ids == length + 1, fresh[pl.ds(2 * slot + 1, 1), :], full)
        return full.astype(jnp.bfloat16)

    heads = 2 * groups

    def attend(first, count, stored, unroll):
        def fill(i, _):
            e = first + i
            slot, length = scalar_ref[LIVE + e], scalar_ref[LENGTH + e]
            stored_k, stored_v = stored(i)
            listed[e, :rows, :] = placed(stored_k, fresh_k, slot, length)
            listed[e, rows:, :] = placed(stored_v, fresh_v, slot, length)
            pltpu.make_async_copy(listed.at[e], list_hbm.at[e], list_sem.at[e]).start()
            return 0

        def weigh(i, _):
            e = first + i
            slot, length = scalar_ref[LIVE + e], scalar_ref[LENGTH + e]
            q = qry[slot].astype(jnp.float32)
            q = jnp.concatenate([q[:, g * width : (g + 1) * width] for g in range(groups)], axis=0).astype(jnp.bfloat16)
            scores = lax.dot_general(
                q, listed[e, :rows, :], (((1,), (1,)), ((), ())), preferred_element_type=jnp.float32
            ) * width ** (-0.5)
            at = pl.ds(pl.multiple_of(e * heads, heads), heads)
            score[at, :] = jnp.where(column_ids <= length + step_ids, scores, -jnp.inf)
            return 0

        def blend(i, _):
            e = first + i
            at = pl.ds(pl.multiple_of(e * heads, heads), heads)
            mix[at, :] = jnp.dot(score[at, :].astype(jnp.bfloat16), listed[e, rows:, :], preferred_element_type=jnp.float32)
            return 0

        lax.fori_loop(0, count, fill, 0, unroll=2)
        lax.fori_loop(0, count, weigh, 0, unroll=unroll)
        every = slice(first * heads, (first + count) * heads)
        scores = score[every, :]
        weights = jnp.exp(scores - jnp.max(scores, axis=-1, keepdims=True))
        score[every, :] = weights / jnp.sum(weights, axis=-1, keepdims=True)
        lax.fori_loop(0, count, blend, 0, unroll=unroll)

    def own(i):
        slot = scalar_ref[LIVE + i]
        return ck[slot], cv[slot]

    def brought(i):
        source = road.where(i)
        return road.arrived[source, :rows, :], road.arrived[source, rows:, :]

    def attend_kept():
        loads[5].wait()
        attend(0, kept, own, kept)
        mix[heads * live :, :] = jnp.zeros((mix.shape[0] - heads * live, width), jnp.float32)
        reduced[...] = jnp.zeros_like(reduced)
        loads[6].wait()

    road.carry(zip(PAUSES, (flatten, project_keys, project_values, rotate_keys, attend_kept)))
    attend(kept, MOVES, brought, 7)

    steps = [
        jnp.concatenate([mix[pl.ds(2 * g + t, STEP_ROWS, stride=heads), :] for g in range(groups)], axis=1)
        for t in range(2)
    ]
    mixture = jnp.concatenate(steps, axis=0).astype(jnp.bfloat16)
    out_width = branch_ref.shape[1]

    def part(j):
        first = pl.multiple_of(lax.rem(at + j, tensors) * out_width, 128)
        return jnp.dot(mixture, ow[:, pl.ds(first, out_width)], preferred_element_type=jnp.float32)

    def give(j):
        return pltpu.make_async_remote_copy(
            src_ref=rs_stage.at[j],
            dst_ref=rs_recv.at[j],
            send_sem=rs_send_sem.at[j],
            recv_sem=rs_recv_sem.at[j],
            device_id={"tensor": lax.rem(at + j, tensors)},
            device_id_type=MESH,
        )

    def give_part(j, _):
        rs_stage[j] = part(j).astype(jnp.bfloat16)
        give(j).start()
        return 0

    lax.fori_loop(1, tensors, give_part, 0)
    total = part(0)
    road.finish()
    for j in range(1, tensors):
        give(j).wait_recv()
        total = total + rs_recv[j].astype(jnp.float32)
    reduced[: 2 * STEP_ROWS, :] = total.astype(jnp.bfloat16)
    rows_at = row_ref[2 * slots :, :]
    pick = (lane.astype(jnp.float32) == rows_at).astype(jnp.float32).astype(jnp.bfloat16)
    branch_ref[...] = jnp.dot(pick, reduced[...], preferred_element_type=jnp.float32).astype(jnp.bfloat16)

    def given(j, _):
        give(j).wait_send()
        return 0

    lax.fori_loop(1, tensors, given, 0)

    def written(e, _):
        pltpu.make_async_copy(listed.at[e], list_hbm.at[e], list_sem.at[e]).wait()
        return 0

    lax.fori_loop(0, live, written, 0)


def layer(tier, replicas, tensors, scalars, rows_at, gain, *operands):
    hidden, queries, cache_keys, cache_values, key_weight, value_weight, out_weight = operands
    slots, rows, width = cache_keys.shape
    live = slots - MOVES
    groups = queries.shape[2] // width
    out_width = out_weight.shape[1] // tensors
    smem = pl.BlockSpec(memory_space=pltpu.SMEM)
    vmem = pl.BlockSpec(memory_space=pltpu.VMEM)
    any_ = pl.BlockSpec(memory_space=pl.ANY)
    bf16 = jnp.bfloat16
    dma = pltpu.SemaphoreType.DMA

    def rollouts(n):
        return pltpu.VMEM((n, 2 * rows, width), bf16)

    caps, y_cap = tier
    lanes = 2 * sum(caps)
    transport = [
        rollouts(2 * lanes + 3),
        rollouts(2 * caps[0]),
        rollouts(y_cap),
        rollouts(y_cap),
        rollouts(3),
    ]
    sizes = (lanes * PARTS, lanes * PARTS, lanes * PARTS, lanes * PARTS, y_cap * PARTS, y_cap * PARTS, 3, 3)
    transport += [dma((n,)) for n in sizes]
    return pl.pallas_call(
        functools.partial(layer_kernel, replicas, tensors, tier),
        out_shape=(
            jax.ShapeDtypeStruct((2 * slots, out_width), bf16),
            jax.ShapeDtypeStruct((live, 2 * rows, width), bf16),
        ),
        in_specs=[smem] + [vmem] * 2 + [any_] * len(operands),
        out_specs=(vmem, any_),
        scratch_shapes=[
            pltpu.VMEM(cache_keys.shape, bf16),
            pltpu.VMEM(cache_values.shape, bf16),
            pltpu.VMEM(hidden.shape, bf16),
            pltpu.VMEM(queries.shape, bf16),
            pltpu.VMEM(key_weight.shape, bf16),
            pltpu.VMEM(value_weight.shape, bf16),
            pltpu.VMEM(out_weight.shape, bf16),
            pltpu.VMEM((2 * slots, hidden.shape[2]), bf16),
            pltpu.VMEM((live, 2 * rows, width), bf16),
            pltpu.VMEM((2 * slots, width), jnp.float32),
            pltpu.VMEM((2 * slots, width), jnp.float32),
            pltpu.VMEM((2 * groups * STEP_ROWS, width), jnp.float32),
            pltpu.VMEM((2 * groups * live, rows), jnp.float32),
            pltpu.VMEM((tensors, 2 * STEP_ROWS, out_width), bf16),
            pltpu.VMEM((tensors, 2 * STEP_ROWS, out_width), bf16),
            pltpu.VMEM((128, out_width), bf16),
            dma((len(operands),)),
            dma((tensors,)),
            dma((tensors,)),
            dma((live,)),
        ]
        + transport,
        compiler_params=pltpu.CompilerParams(
            collective_id=TIERS.index(tier),
            has_side_effects=True,
            vmem_limit_bytes=VMEM_LIMIT,
        ),
    )(scalars, rows_at, gain, *operands)


def place_kernel(scalar_ref, dead_ref, flat_ref, list_hbm, branch_ref, keys_hbm, values_hbm, listed, zeros, sem):
    rows = zeros.shape[0]
    live = listed.shape[0]
    load = pltpu.make_async_copy(list_hbm, listed, sem.at[live + MOVES, 0])
    load.start()
    zeros[...] = jnp.zeros_like(zeros)

    def copies(e):
        slot = scalar_ref[LIVE + e]
        return (
            pltpu.make_async_copy(listed.at[e, pl.ds(0, rows)], keys_hbm.at[slot], sem.at[e, 0]),
            pltpu.make_async_copy(listed.at[e, pl.ds(rows, rows)], values_hbm.at[slot], sem.at[e, 1]),
        )

    def clears(e):
        slot = dead_ref[e]
        return (
            pltpu.make_async_copy(zeros, keys_hbm.at[slot], sem.at[live + e, 0]),
            pltpu.make_async_copy(zeros, values_hbm.at[slot], sem.at[live + e, 1]),
        )

    def run(make, count, act):
        def each(e, _):
            for copy in make(e):
                getattr(copy, act)()
            return 0

        lax.fori_loop(0, count, each, 0)

    run(clears, MOVES, "start")
    load.wait()
    run(copies, live, "start")
    for s in range(branch_ref.shape[0]):
        branch_ref[s] = flat_ref[2 * s : 2 * s + 2, :]
    run(clears, MOVES, "wait")
    run(copies, live, "wait")


def place(scalars, dead_slots, branch, listed, slots):
    live, both, width = listed.shape
    shape = jax.ShapeDtypeStruct((slots, both // 2, width), listed.dtype)
    smem = pl.BlockSpec(memory_space=pltpu.SMEM)
    vmem = pl.BlockSpec(memory_space=pltpu.VMEM)
    any_ = pl.BlockSpec(memory_space=pl.ANY)
    return pl.pallas_call(
        place_kernel,
        out_shape=(jax.ShapeDtypeStruct((slots, 2, branch.shape[1]), branch.dtype), shape, shape),
        in_specs=[smem, smem, vmem, any_],
        out_specs=(vmem, any_, any_),
        scratch_shapes=[
            pltpu.VMEM(listed.shape, listed.dtype),
            pltpu.VMEM((both // 2, width), listed.dtype),
            pltpu.SemaphoreType.DMA((slots + 1, 2)),
        ],
    )(scalars, dead_slots, branch, listed)


def shards(hidden, queries, cache_keys, cache_values, key_weight, value_weight, key_gain, out_weight, lengths, move_src, move_dst):
    slots = cache_keys.shape[0]
    replicas, tensors = lax.axis_size("replica"), lax.axis_size("tensor")
    me = lax.axis_index("replica").astype(jnp.int32)
    tier, dead, scalars, rows_at = plan(me.reshape(1), lengths, move_src, move_dst, slots, replicas)
    operands = (
        scalars,
        rows_at,
        key_gain.reshape(1, -1),
        hidden,
        queries,
        cache_keys,
        cache_values,
        key_weight,
        value_weight,
        out_weight,
    )
    branches = [functools.partial(layer, t, replicas, tensors) for t in TIERS]
    branch, listed = lax.switch(tier[0], branches, *operands)
    return place(scalars, dead, branch, listed, slots)


def solution(mesh):
    placed = (
        P("replica", None, None),
        P("replica", None, "tensor"),
        P("replica", None, "tensor"),
        P("replica", None, "tensor"),
        P(None, "tensor"),
        P(None, "tensor"),
        P(),
        P("tensor", None),
        P(),
        P(),
        P(),
    )
    return jax.shard_map(
        shards,
        mesh=mesh,
        in_specs=placed,
        out_specs=(
            P("replica", None, "tensor"),
            P("replica", None, "tensor"),
            P("replica", None, "tensor"),
        ),
        check_vma=False,
    )
```

```python
import functools
import math

import jax
import jax.numpy as jnp
from jax import lax
from jax.experimental import pallas as pl
from jax.experimental.pallas import tpu as pltpu
from jax.sharding import PartitionSpec as P

EPS = 1e-06
THETA = 1000000.0
MESH = pl.DeviceIdType.MESH
VMEM_LIMIT = 60 * 1024 * 1024
MOVES = 14
KEPT_ROWS, CAME_ROWS = 8, 16
TIERS = (((7, 4, 3, 1), 10), ((7, 5, 3, 2), 10), ((8, 6, 4, 2), 11), ((9, 7, 5, 3), 12))
PARTS = 2
Y_WINDOW = 6
HAND_WINDOW = 6
PAUSES = range(5, 100, 3)


def route(slots, replicas, me, src, dst):
    width = 128

    def column(row):
        tall = jnp.broadcast_to(row.astype(jnp.float32), (width, moves))
        return jnp.concatenate([tall[:, i : i + width].T for i in range(0, moves, width)], axis=0).astype(jnp.int32)

    def down(of, *rows):
        cuts = [[row[:, i : i + width] for row in rows] for i in range(0, moves, width)]
        return jnp.concatenate([jnp.sum(of(*cut), axis=0, keepdims=True) for cut in cuts], axis=1)

    ring = replicas // 4
    half = ring // 2
    moves = src.shape[1]
    order = lax.broadcasted_iota(jnp.int32, (1, moves), 1)
    exists = order < replicas * MOVES
    from_rep, to_rep = src // slots, dst // slots
    ys, zs, cs = from_rep // (2 * ring), (from_rep // 2) % ring, from_rep % 2
    yd, zd = to_rep // (2 * ring), (to_rep // 2) % ring
    ahead = jnp.where(exists, (zd - zs + ring) % ring, 0)
    group = (yd * ring + zs) * 2 + cs
    distance = jnp.where(ahead <= half, ahead, ring - ahead)
    travels = ahead != 0
    pull = jnp.where((ahead == half) | ~travels, 0, jnp.where(ahead < half, ahead, ahead - ring))
    farthest = ahead == half

    other, other_group, other_pull = column(order), column(group), column(pull)
    other_far = column(jnp.where(farthest, group, -1))
    lean = down(lambda g: jnp.where(other_group == g, other_pull, 0), group)
    rank_far = down(lambda g, n: jnp.where((other_far == g) & (other < n), 1, 0), group, order)
    way = jnp.where(ahead < half, 0, 1)
    for i in range(4):
        back = lean > 0
        way = jnp.where(farthest & (rank_far == i), jnp.where(back, 1, 0), way)
        lean = lean + jnp.where(back, -half, half)
    list_key = group * 2 + way
    sort_key = (list_key * 8 + 7 - distance) * moves + order
    other_key = column(jnp.where(travels, sort_key, -1))
    least = list_key * (8 * moves)
    place_in = down(lambda low, key: jnp.where((other_key >= low) & (other_key < key), 1, 0), least, sort_key)
    spot = 2 * place_in + way
    crosses = travels & (ys != yd)
    y_key = from_rep * 64 + spot
    other_y = column(jnp.where(crosses, y_key, -1))
    y_rank = down(lambda low, key: jnp.where((other_y >= low) & (other_y < key), 1, 0), from_rep * 64, y_key)

    tier = jnp.full((1, 1), len(TIERS), jnp.int32)
    for i, (caps, y_cap) in reversed(list(enumerate(TIERS))):
        reach = sum(jnp.where(place_in < c, 1, 0) for c in caps)
        misfit = travels & ((distance > reach) | (crosses & (y_rank >= y_cap)))
        tier = jnp.where(jnp.sum(jnp.where(misfit, 1, 0), axis=1, keepdims=True) == 0, i, tier)

    my_y, my_z, my_c = me // (2 * ring), (me // 2) % ring, me % 2
    mine = exists & (from_rep == me)
    in_group = travels & (group == (my_y * ring + my_z) * 2 + my_c)
    kind = jnp.where(ys == yd, 0, jnp.where(cs == to_rep % 2, 1, 2))
    address = jnp.where(
        in_group,
        jnp.where(spot < 32, spot, -1),
        jnp.where(
            mine,
            jnp.where(travels, 32 + y_rank, 48 + kind),
            jnp.where(exists & (to_rep == me), 64 + dst % slots, -1),
        ),
    )
    code = (((place_in * 2 + way) * 8 + distance) * 4 + kind) * 1024 + src + 1
    value = jnp.where(in_group, jnp.where(mine, src % slots, slots + y_rank), jnp.where(mine, src % slots, code))
    lane = lax.broadcasted_iota(jnp.int32, (1, width), 1)
    hit = column(address) == lane
    table = jnp.sum(jnp.where(hit, column(value), 0), axis=0, keepdims=True)
    return jnp.where(lane == width - 1, tier, table)


INJECT, ACROSS, NEAR, LIVE, LENGTH, LANE, SPOT, KIND, TOKENS, ROW, TABLE = 0, 32, 48, 64, 96, 128, 144, 160, 176, 208, 240


def plan_kernel(
    slots,
    replicas,
    me_ref,
    len_ref,
    src_ref,
    src_row,
    dst_row,
    tier_ref,
    dead_ref,
    out_ref,
    mark,
    padded,
    table_vmem,
    table_ref,
    sem,
):
    me = me_ref[0]
    moves = padded.shape[1]
    count = src_row.shape[1]
    padded[...] = jnp.zeros_like(padded)
    padded[0:1, :count] = src_row[...]
    padded[1:2, :count] = dst_row[...]

    table_vmem[...] = route(slots, replicas, me, padded[0:1, :], padded[1:2, :])
    fetch = pltpu.make_async_copy(table_vmem, table_ref, sem)
    fetch.start()

    def clear(i, _):
        mark[i] = 0
        return 0

    lax.fori_loop(0, slots, clear, 0, unroll=8)

    def out(k, _):
        mark[src_ref[me * MOVES + k] % slots] = 1
        return 0

    lax.fori_loop(0, MOVES, out, 0, unroll=2)
    fetch.wait()
    tier_ref[0] = table_ref[0, 127]

    def copy(i, _):
        out_ref[INJECT + i] = table_ref[0, i]
        return 0

    lax.fori_loop(0, 64, copy, 0, unroll=8)

    def each(s, counts):
        kept_count, in_count, dead_count = counts
        code = table_ref[0, 64 + s]
        incoming = code > 0
        source = jnp.where(incoming, (code - 1) % 1024, me * slots + s)
        length = len_ref[source]
        stays = jnp.logical_not(incoming) & (mark[s] == 0) & (length > 0)
        alive = incoming | stays
        length = jnp.where(alive, length, 0)
        at = jnp.where(incoming, slots - 2 * MOVES + in_count, kept_count)
        where = jnp.where(alive, at, slots - 1)
        out_ref[LIVE + where] = s
        out_ref[LENGTH + where] = length
        dead_ref[dead_count] = s
        rest = (code - 1) // 1024
        kind = rest % 4
        distance = (rest // 4) % 8
        way = (rest // 32) % 2
        source_rep = source // slots
        slot_in = jnp.where(incoming, in_count, MOVES)
        other_core = jnp.where(source_rep % 2 == me % 2, 0, 1)
        out_ref[LANE + slot_in] = (other_core * 2 + way) * 4 + distance - 1
        out_ref[SPOT + slot_in] = rest // 64
        out_ref[KIND + slot_in] = jnp.where(distance == 0, kind, -1)
        out_ref[TOKENS + s] = length
        out_ref[ROW + s] = jnp.where(alive, jnp.where(incoming, 2 * KEPT_ROWS + in_count, kept_count), -1)
        one = jnp.int32(1)
        return (
            kept_count + jnp.where(stays, one, 0),
            in_count + jnp.where(incoming, one, 0),
            dead_count + jnp.where(alive, 0, one),
        )

    zero = jnp.int32(0)
    lax.fori_loop(0, slots, each, (zero, zero, zero), unroll=2)


def plan(me, lengths, move_src, move_dst, slots, replicas):
    smem = pl.BlockSpec(memory_space=pltpu.SMEM)
    vmem = pl.BlockSpec(memory_space=pltpu.VMEM)
    ints = lambda n: jax.ShapeDtypeStruct((n,), jnp.int32)
    moves = -(-move_src.shape[0] // 128) * 128
    return pl.pallas_call(
        functools.partial(plan_kernel, slots, replicas),
        out_shape=(ints(1), ints(slots + 1), ints(TABLE)),
        in_specs=[smem] * 3 + [vmem] * 2,
        out_specs=(smem,) * 3,
        scratch_shapes=[
            pltpu.SMEM((slots,), jnp.int32),
            pltpu.VMEM((8, moves), jnp.int32),
            pltpu.VMEM((1, 128), jnp.int32),
            pltpu.SMEM((1, 128), jnp.int32),
            pltpu.SemaphoreType.DMA,
        ],
    )(me, lengths, move_src, move_src.reshape(1, -1), move_dst.reshape(1, -1))


def crossings(y_cap):
    return [(b, part) for low in range(0, y_cap, 2) for part in range(PARTS) for b in range(low, min(low + 2, y_cap))]


def timetable(caps, y_cap):
    step, lag = 1.0 / PARTS, 0.5
    across = {key: (n + 1) * step + lag for n, key in enumerate(crossings(y_cap))}
    ready = [
        (across[min(i, y_cap - 1), part] + 0.01 * max(0, i - y_cap), 1, "inject", i % 2, 1, i // 2, part)
        for i in range(2 * caps[0])
        for part in range(PARTS)
    ]
    free = [0.0, 0.0]
    events = []
    while ready:
        ready.sort()
        time, _, what, way, hop, spot, part = event = ready.pop(0)
        events.append(event[2:])
        if what == "inject" or (hop < len(caps) and spot < caps[hop]):
            free[way] = max(free[way], time) + step
            onward = hop if what == "inject" else hop + 1
            ready.append((free[way] + lag, 0, "pass", way, onward, spot, part))
    return events


class Ring:
    def __init__(self, tier, replicas, me, scalars, caches, arrived, inject, across, across_in, near, *sems):
        self.caps, self.y_cap = tier
        self.me, self.scalars, self.caches = me, scalars, caches
        self.arrived, self.inject, self.across, self.across_in, self.near = arrived, inject, across, across_in, near
        self.hop_send, self.hop_recv, self.core_send, self.core_recv, self.y_send, self.y_recv, self.near_send, self.near_recv = sems
        half = replicas // 2
        line = (me // half) * half
        ahead = line + lax.rem(me - line + 2, half)
        behind = line + lax.rem(me - line + half - 2, half)
        core = me + 1 - 2 * lax.rem(me, 2)
        opposite = lax.rem(me + half, replicas)
        both = lax.rem(core + half, replicas)
        self.ways = (ahead, behind)
        self.core, self.opposite = core, opposite
        self.near_peers = (core, opposite, both)
        self.partners = 5
        self.events = timetable(self.caps, self.y_cap)
        self.lanes = 2 * sum(self.caps)

    def greet(self, barrier):
        for peer in self.ways + self.near_peers:
            pl.semaphore_signal(barrier, inc=1, device_id={"replica": peer}, device_id_type=MESH)

    def copy(self, source, target, send_sem, recv_sem, peer):
        return pltpu.make_async_remote_copy(
            src_ref=source, dst_ref=target, send_sem=send_sem, recv_sem=recv_sem, device_id={"replica": peer}, device_id_type=MESH
        )

    def lane(self, way, hop, spot):
        return way * sum(self.caps) + sum(self.caps[: hop - 1]) + spot

    def half(self, ref, at, part):
        rows = self.caches[0].shape[1]
        return ref.at[at, pl.ds(part * rows, rows)]

    def cross(self, b, part):
        at = b * PARTS + part
        return self.copy(
            self.half(self.across, b, part), self.half(self.across_in, b, part), self.y_send.at[at], self.y_recv.at[at], self.opposite
        )

    def next_door(self, j):
        target = self.arrived.at[2 * self.lanes + j]
        return self.copy(self.near.at[j], target, self.near_send.at[j], self.near_recv.at[j], self.near_peers[j])

    def hop(self, way, hop, spot, part):
        source = (self.inject, 2 * spot + way) if hop == 1 else (self.arrived, self.lane(way, hop - 1, spot))
        to = self.lane(way, hop, spot)
        at = to * PARTS + part
        return self.copy(
            self.half(*source, part), self.half(self.arrived, to, part), self.hop_send.at[at], self.hop_recv.at[at], self.ways[way]
        )

    def hand_over(self, way, hop, spot, part):
        lane = self.lane(way, hop, spot)
        at = lane * PARTS + part
        return self.copy(
            self.half(self.arrived, lane, part),
            self.half(self.arrived, self.lanes + lane, part),
            self.core_send.at[at],
            self.core_recv.at[at],
            self.core,
        )

    def pack(self, target, at, slot, parts):
        rows = self.caches[0].shape[1]
        for part in parts:
            target[at, part * rows : (part + 1) * rows, :] = self.caches[part][slot]

    def begin(self, n):
        order = crossings(self.y_cap)
        if n < len(order):
            b, part = order[n]
            self.pack(self.across, b, self.scalars[ACROSS + b], (part,))
            self.cross(b, part).start()
        elif n < len(order) + 3:
            j = n - len(order)
            self.pack(self.near, j, self.scalars[NEAR + j], range(PARTS))
            self.next_door(j).start()

    def enter(self, way, spot, part, crossed):
        slots, rows, _ = self.caches[0].shape
        i = 2 * spot + way
        here = slice(part * rows, (part + 1) * rows)
        code = self.scalars[INJECT + i]
        block = self.caches[part][jnp.where(code < slots, code, 0)]
        if crossed == len(crossings(self.y_cap)):
            other = self.across_in[jnp.where(code < slots, 0, code - slots), here, :]
            block = jnp.where(code < slots, block, other)
        else:
            for b in range(min(i + 1, self.y_cap)):
                block = jnp.where(code == slots + b, self.across_in[b, here, :], block)
        self.inject[i, here, :] = block
        self.hop(way, 1, spot, part).start()

    def carry(self, pauses):
        order = crossings(self.y_cap)
        for n in range(Y_WINDOW):
            self.begin(n)
        crossed = 0
        pauses = dict(pauses)
        over = []
        for count, (what, way, hop, spot, part) in enumerate(self.events):
            if what == "inject":
                needed = order.index((min(2 * spot + way, self.y_cap - 1), part)) + 1
                while crossed < needed:
                    self.cross(*order[crossed]).wait_recv()
                    self.begin(crossed + Y_WINDOW)
                    crossed += 1
                self.enter(way, spot, part, crossed)
            else:
                self.hop(way, hop, spot, part).wait_recv()
                if hop < len(self.caps) and spot < self.caps[hop]:
                    self.hop(way, hop + 1, spot, part).start()
                self.hand_over(way, hop, spot, part).start()
                over.append((way, hop, spot, part))
                if len(over) > HAND_WINDOW:
                    self.hand_over(*over[-1 - HAND_WINDOW]).wait()
            if count in pauses:
                pauses.pop(count)()
        for pause in pauses.values():
            pause()
        for n in range(crossed, len(order)):
            self.cross(*order[n]).wait_recv()
        for n in range(max(Y_WINDOW, crossed + Y_WINDOW), len(order) + 3):
            self.begin(n)
        for j in range(3):
            self.next_door(j).wait_recv()
        for key in over[-HAND_WINDOW:]:
            self.hand_over(*key).wait()

    def where(self, i):
        kind, lane = self.scalars[KIND + i], self.scalars[LANE + i]
        first = 0
        for n in range(2 * 2 * len(self.caps)):
            way, hop = n // len(self.caps) % 2, n % len(self.caps) + 1
            first = jnp.where(lane == n, n // (2 * len(self.caps)) * self.lanes + self.lane(way, hop, 0), first)
        return jnp.where(kind >= 0, 2 * self.lanes + kind, first + self.scalars[SPOT + i])

    def finish(self):
        for b, part in crossings(self.y_cap):
            self.cross(b, part).wait_send()
        for j in range(3):
            self.next_door(j).wait_send()
        for what, way, hop, spot, part in self.events:
            if what == "pass":
                self.hop(way, hop, spot, part).wait_send()


def layer_kernel(
    replicas,
    tensors,
    tier,
    scalar_ref,
    gain_ref,
    hidden_hbm,
    query_hbm,
    ck_hbm,
    cv_hbm,
    kw_hbm,
    vw_hbm,
    ow_hbm,
    branch_ref,
    list_hbm,
    ck,
    cv,
    hid,
    qry,
    kw,
    vw,
    ow,
    flat,
    listed,
    fresh_k,
    fresh_v,
    mix,
    score,
    rs_stage,
    rs_recv,
    reduced,
    row_ref,
    in_sem,
    rs_send_sem,
    rs_recv_sem,
    list_sem,
    *transport,
):
    me = lax.axis_index("replica")
    at = lax.axis_index("tensor")
    slots, rows, width = ck.shape
    live = listed.shape[0]
    kept = live - MOVES
    groups = query_hbm.shape[2] // width

    loads = [
        pltpu.make_async_copy(source, target, in_sem.at[i])
        for i, (source, target) in enumerate(
            (
                (ck_hbm, ck),
                (cv_hbm, cv),
                (hidden_hbm, hid),
                (kw_hbm, kw),
                (vw_hbm, vw),
                (query_hbm, qry),
                (ow_hbm, ow),
            )
        )
    ]
    loads[0].start()
    loads[1].start()

    caches = (ck, cv)
    road = Ring(tier, replicas, me, scalar_ref, caches, *transport)

    barrier = pltpu.get_barrier_semaphore()
    road.greet(barrier)

    def greet_tensor(j, _):
        pl.semaphore_signal(barrier, inc=1, device_id={"tensor": lax.rem(at + j, tensors)}, device_id_type=MESH)
        return 0

    lax.fori_loop(1, tensors, greet_tensor, 0)
    pl.semaphore_wait(barrier, road.partners + tensors - 1)

    loads[0].wait()
    loads[1].wait()
    for load in loads[2:]:
        load.start()

    def clear():
        mix[...] = jnp.zeros_like(mix)
        reduced[...] = jnp.zeros_like(reduced)

    def tell():
        def one(s, _):
            tokens, row = scalar_ref[TOKENS + s], scalar_ref[ROW + s]
            stride = jnp.where(row < 2 * KEPT_ROWS, KEPT_ROWS, CAME_ROWS)
            for t in range(2):
                at = jnp.where(row < 0, -1, row + t * stride)
                row_ref[pl.ds(2 * s + t, 1), :] = jnp.full((1, width), tokens + t, jnp.int32).astype(jnp.float32)
                row_ref[pl.ds(2 * (slots + s) + t, 1), :] = jnp.full((1, width), at, jnp.int32).astype(jnp.float32)
            return 0

        lax.fori_loop(0, slots, one, 0, unroll=2)

    def flatten():
        loads[2].wait()
        for s in range(slots):
            flat[2 * s : 2 * s + 2, :] = hid[s]

    def project_keys():
        loads[3].wait()
        fresh_k[...] = jnp.dot(flat[...], kw[...], preferred_element_type=jnp.float32)

    def project_values():
        loads[4].wait()
        raw_v = jnp.dot(flat[...], vw[...], preferred_element_type=jnp.float32)
        fresh_v[...] = raw_v.astype(jnp.bfloat16).astype(jnp.float32)

    lane = lax.broadcasted_iota(jnp.int32, (1, width), 1)

    def rotate_keys():
        raw_k = fresh_k[...]
        mean_square = jnp.mean(raw_k * raw_k, axis=-1, keepdims=True)
        normed = raw_k * lax.rsqrt(mean_square + EPS) * gain_ref[...]
        half = width // 2
        index = jnp.where(lane < half, lane, lane - half).astype(jnp.float32)
        angles = row_ref[: 2 * slots, :] * jnp.exp(index * (-2.0 * math.log(THETA) / width))
        turned = pltpu.roll(normed, half, 1)
        sine = jnp.sin(angles)
        rotated = normed * jnp.cos(angles) + turned * jnp.where(lane < half, -sine, sine)
        fresh_k[...] = rotated.astype(jnp.bfloat16).astype(jnp.float32)

    row_ids = lax.broadcasted_iota(jnp.int32, (rows, width), 0)
    column_ids = lax.broadcasted_iota(jnp.int32, (2 * groups, rows), 1)
    step_ids = lax.broadcasted_iota(jnp.int32, (2 * groups, rows), 0) % 2

    def placed(stored, fresh, slot, length):
        full = jnp.where(row_ids < length, stored.astype(jnp.float32), 0.0)
        full = jnp.where(row_ids == length, fresh[pl.ds(2 * slot, 1), :], full)
        full = jnp.where(row_ids == length + 1, fresh[pl.ds(2 * slot + 1, 1), :], full)
        return full.astype(jnp.bfloat16)

    heads = 2 * groups

    def attend(first, count, stored, unroll):
        def fill(i, _):
            e = first + i
            slot, length = scalar_ref[LIVE + e], scalar_ref[LENGTH + e]
            stored_k, stored_v = stored(i)
            listed[e, :rows, :] = placed(stored_k, fresh_k, slot, length)
            listed[e, rows:, :] = placed(stored_v, fresh_v, slot, length)
            pltpu.make_async_copy(listed.at[e], list_hbm.at[e], list_sem.at[e]).start()
            return 0

        def weigh(i, _):
            e = first + i
            slot, length = scalar_ref[LIVE + e], scalar_ref[LENGTH + e]
            q = qry[slot].astype(jnp.float32)
            q = jnp.concatenate([q[:, g * width : (g + 1) * width] for g in range(groups)], axis=0).astype(jnp.bfloat16)
            scores = lax.dot_general(
                q, listed[e, :rows, :], (((1,), (1,)), ((), ())), preferred_element_type=jnp.float32
            ) * width ** (-0.5)
            at = pl.ds(pl.multiple_of(e * heads, heads), heads)
            score[at, :] = jnp.where(column_ids <= length + step_ids, scores, -jnp.inf)
            return 0

        def blend(i, _):
            e = first + i
            at = pl.ds(pl.multiple_of(e * heads, heads), heads)
            mix[at, :] = jnp.dot(score[at, :].astype(jnp.bfloat16), listed[e, rows:, :], preferred_element_type=jnp.float32)
            return 0

        lax.fori_loop(0, count, fill, 0, unroll=2)
        lax.fori_loop(0, count, weigh, 0, unroll=unroll)
        every = slice(first * heads, (first + count) * heads)
        scores = score[every, :]
        weights = jnp.exp(scores - jnp.max(scores, axis=-1, keepdims=True))
        score[every, :] = weights / jnp.sum(weights, axis=-1, keepdims=True)
        lax.fori_loop(0, count, blend, 0, unroll=unroll)

    def own(i):
        slot = scalar_ref[LIVE + i]
        return ck[slot], cv[slot]

    def brought(i):
        source = road.where(i)
        return road.arrived[source, :rows, :], road.arrived[source, rows:, :]

    def attend_kept():
        loads[5].wait()
        attend(0, kept, own, kept)
        loads[6].wait()

    out_width = branch_ref.shape[1]
    groups_of_rows = ((0, KEPT_ROWS, 0), (kept, CAME_ROWS, 2 * KEPT_ROWS))

    def mixture(group):
        first, count, _ = groups_of_rows[group]
        steps = [
            jnp.concatenate(
                [mix[pl.ds(first * heads + 2 * g + t, count, stride=heads), :] for g in range(groups)], axis=1
            )
            for t in range(2)
        ]
        return jnp.concatenate(steps, axis=0).astype(jnp.bfloat16)

    def term(mixed, j):
        first = pl.multiple_of(lax.rem(at + j, tensors) * out_width, 128)
        return jnp.dot(mixed, ow[:, pl.ds(first, out_width)], preferred_element_type=jnp.float32)

    def give(group, j):
        _, count, low = groups_of_rows[group]
        n = group * tensors + j
        return pltpu.make_async_remote_copy(
            src_ref=rs_stage.at[j, pl.ds(low, 2 * count)],
            dst_ref=rs_recv.at[j, pl.ds(low, 2 * count)],
            send_sem=rs_send_sem.at[n],
            recv_sem=rs_recv_sem.at[n],
            device_id={"tensor": lax.rem(at + j, tensors)},
            device_id_type=MESH,
        )

    def give_term(group, mixed, j):
        _, count, low = groups_of_rows[group]
        rs_stage[j, low : low + 2 * count, :] = term(mixed, j).astype(jnp.bfloat16)
        give(group, j).start()

    def add_up(group, own_term):
        _, count, low = groups_of_rows[group]
        total = own_term
        for j in range(1, tensors):
            give(group, j).wait_recv()
            total = total + rs_recv[j, low : low + 2 * count, :].astype(jnp.float32)
        reduced[low : low + 2 * count, :] = total.astype(jnp.bfloat16)

    def give_kept(j):
        give_term(0, mixture(0), j)

    pieces = [clear, tell, flatten, project_keys, project_values, rotate_keys, attend_kept]
    pieces += [functools.partial(give_kept, j) for j in range(1, tensors)]
    road.carry(zip(PAUSES, pieces))
    attend(kept, MOVES, brought, 7)

    mixed = mixture(1)

    def give_came(j, _):
        give_term(1, mixed, j)
        return 0

    lax.fori_loop(1, tensors, give_came, 0)
    own_term = term(mixed, 0)
    road.finish()
    add_up(0, term(mixture(0), 0))
    add_up(1, own_term)
    rows_at = row_ref[2 * slots :, :]
    pick = (lane.astype(jnp.float32) == rows_at).astype(jnp.float32).astype(jnp.bfloat16)
    branch_ref[...] = jnp.dot(pick, reduced[...], preferred_element_type=jnp.float32).astype(jnp.bfloat16)

    def given(j, _):
        for group in range(2):
            give(group, j).wait_send()
        return 0

    lax.fori_loop(1, tensors, given, 0)

    def written(e, _):
        pltpu.make_async_copy(listed.at[e], list_hbm.at[e], list_sem.at[e]).wait()
        return 0

    lax.fori_loop(0, live, written, 0)


def layer(tier, replicas, tensors, scalars, gain, *operands):
    hidden, queries, cache_keys, cache_values, key_weight, value_weight, out_weight = operands
    slots, rows, width = cache_keys.shape
    live = slots - MOVES
    groups = queries.shape[2] // width
    out_width = out_weight.shape[1] // tensors
    smem = pl.BlockSpec(memory_space=pltpu.SMEM)
    vmem = pl.BlockSpec(memory_space=pltpu.VMEM)
    any_ = pl.BlockSpec(memory_space=pl.ANY)
    bf16 = jnp.bfloat16
    dma = pltpu.SemaphoreType.DMA

    def rollouts(n):
        return pltpu.VMEM((n, 2 * rows, width), bf16)

    caps, y_cap = tier
    lanes = 2 * sum(caps)
    transport = [
        rollouts(2 * lanes + 3),
        rollouts(2 * caps[0]),
        rollouts(y_cap),
        rollouts(y_cap),
        rollouts(3),
    ]
    sizes = (lanes * PARTS, lanes * PARTS, lanes * PARTS, lanes * PARTS, y_cap * PARTS, y_cap * PARTS, 3, 3)
    transport += [dma((n,)) for n in sizes]
    return pl.pallas_call(
        functools.partial(layer_kernel, replicas, tensors, tier),
        out_shape=(
            jax.ShapeDtypeStruct((2 * slots, out_width), bf16),
            jax.ShapeDtypeStruct((live, 2 * rows, width), bf16),
        ),
        in_specs=[smem, vmem] + [any_] * len(operands),
        out_specs=(vmem, any_),
        scratch_shapes=[
            pltpu.VMEM(cache_keys.shape, bf16),
            pltpu.VMEM(cache_values.shape, bf16),
            pltpu.VMEM(hidden.shape, bf16),
            pltpu.VMEM(queries.shape, bf16),
            pltpu.VMEM(key_weight.shape, bf16),
            pltpu.VMEM(value_weight.shape, bf16),
            pltpu.VMEM(out_weight.shape, bf16),
            pltpu.VMEM((2 * slots, hidden.shape[2]), bf16),
            pltpu.VMEM((live, 2 * rows, width), bf16),
            pltpu.VMEM((2 * slots, width), jnp.float32),
            pltpu.VMEM((2 * slots, width), jnp.float32),
            pltpu.VMEM((2 * groups * (slots - 2 * MOVES + CAME_ROWS), width), jnp.float32),
            pltpu.VMEM((2 * groups * live, rows), jnp.float32),
            pltpu.VMEM((tensors, 2 * (KEPT_ROWS + CAME_ROWS), out_width), bf16),
            pltpu.VMEM((tensors, 2 * (KEPT_ROWS + CAME_ROWS), out_width), bf16),
            pltpu.VMEM((128, out_width), bf16),
            pltpu.VMEM((4 * slots, width), jnp.float32),
            dma((len(operands),)),
            dma((2 * tensors,)),
            dma((2 * tensors,)),
            dma((live,)),
        ]
        + transport,
        compiler_params=pltpu.CompilerParams(
            collective_id=TIERS.index(tier),
            has_side_effects=True,
            vmem_limit_bytes=VMEM_LIMIT,
        ),
    )(scalars, gain, *operands)


def rotate(vectors, positions):
    half_width = vectors.shape[-1] // 2
    indices = jnp.arange(half_width, dtype=jnp.float32)
    frequency = jnp.exp(indices * (-2.0 * math.log(THETA) / vectors.shape[-1]))
    angles = positions[:, :, None, None] * frequency
    cosine = jnp.cos(angles)
    sine_values = jnp.sin(angles)
    former = vectors[..., :half_width]
    latter = vectors[..., half_width:]
    return jnp.concatenate(
        [former * cosine - latter * sine_values, latter * cosine + former * sine_values], -1
    )


def new_entries(hidden, key_weight, value_weight, key_gain, length):
    row_count = hidden.shape[0]
    flat_rows = hidden.reshape(row_count * 2, hidden.shape[2])
    raw_keys = jnp.dot(flat_rows, key_weight, preferred_element_type=jnp.float32).reshape(
        row_count, 2, -1, key_gain.shape[0]
    )
    mean_square = jnp.mean(raw_keys * raw_keys, axis=-1, keepdims=True)
    normed = raw_keys * lax.rsqrt(mean_square + EPS) * key_gain
    positions = (length[:, None] + jnp.arange(2, dtype=jnp.int32)[None, :]).astype(jnp.float32)
    fresh_keys = rotate(normed, positions).reshape(row_count, 2, -1).astype(jnp.bfloat16)
    fresh_values = (
        jnp.dot(flat_rows, value_weight, preferred_element_type=jnp.float32)
        .reshape(row_count, 2, -1)
        .astype(jnp.bfloat16)
    )
    return (fresh_keys, fresh_values)


def fill(stored, fresh, length, active):
    row_ids = jnp.arange(stored.shape[1], dtype=jnp.int32)[None, :, None]
    border = length[:, None, None]
    kept = jnp.where(row_ids < border, stored, jnp.zeros_like(stored))
    kept = jnp.where(row_ids == border, fresh[:, 0:1, :], kept)
    kept = jnp.where(row_ids == border + 1, fresh[:, 1:2, :], kept)
    return jnp.where(active[:, None, None], kept, jnp.zeros_like(kept))


def attend(full_keys, full_values, length, queries, head_dim):
    row_count, key_rows, width = full_keys.shape
    kv_heads = width // head_dim
    group_size = queries.shape[-1] // width
    query_heads = queries.reshape(row_count, 2, kv_heads, group_size, head_dim)
    key_heads = full_keys.reshape(row_count, key_rows, kv_heads, head_dim)
    value_heads = full_values.reshape(row_count, key_rows, kv_heads, head_dim)
    scores = jnp.einsum(
        "rsvgh,rlvh->rvsgl", query_heads, key_heads, preferred_element_type=jnp.float32
    ) * head_dim ** (-0.5)
    row_ids = jnp.arange(key_rows, dtype=jnp.int32)[None, None, :]
    limits = length[:, None, None] + jnp.arange(2, dtype=jnp.int32)[None, :, None]
    visible = row_ids <= limits
    scores = jnp.where(visible[:, None, :, None, :], scores, -jnp.inf)
    highest = jnp.max(scores, axis=-1, keepdims=True)
    weights = jnp.exp(scores - highest)
    shares = (weights / jnp.sum(weights, axis=-1, keepdims=True)).astype(jnp.bfloat16)
    mixture = jnp.einsum(
        "rvsgl,rlvh->rsvgh", shares, value_heads, preferred_element_type=jnp.float32
    )
    return mixture.reshape(row_count, 2, -1).astype(jnp.bfloat16)


def plain_layer(scalars, key_gain, hidden, queries, cache_keys, cache_values, key_weight, value_weight, out_weight, lengths, move_src, move_dst):
    local_count = cache_keys.shape[0]
    replicas = lax.axis_size("replica")
    replica_here = lax.axis_index("replica")
    first_slot = replica_here * local_count
    head_dim = key_gain.shape[0]
    all_slots = jnp.arange(lengths.shape[0], dtype=jnp.int32)
    anchor = all_slots.at[move_src].set(-1).at[move_dst].set(move_src)
    own_anchor = lax.dynamic_slice_in_dim(anchor, first_slot, local_count)
    holding = own_anchor >= 0
    new_length = jnp.where(holding, lengths[jnp.where(holding, own_anchor, 0)], 0)
    alive = new_length > 0
    local_ids = first_slot + jnp.arange(local_count, dtype=jnp.int32)
    source_rep = move_src // local_count
    target_rep = move_dst // local_count
    peer_ids = jnp.arange(replicas, dtype=jnp.int32)
    sending = (source_rep[None, :] == replica_here) & (target_rep[None, :] == peer_ids[:, None])
    has_out = jnp.any(sending, axis=1)
    send_slot = jnp.sum(jnp.where(sending, move_src[None, :] - first_slot, 0), axis=1)
    outbound = has_out[:, None, None]
    pack_keys = jnp.where(outbound, cache_keys[send_slot], jnp.zeros((), cache_keys.dtype))
    pack_values = jnp.where(outbound, cache_values[send_slot], jnp.zeros((), cache_values.dtype))
    arrived_keys, arrived_values = (
        lax.all_to_all(pack_keys, "replica", split_axis=0, concat_axis=0, tiled=True),
        lax.all_to_all(pack_values, "replica", split_axis=0, concat_axis=0, tiled=True),
    )
    arriving = move_dst[None, :] == local_ids[:, None]
    incoming = jnp.any(arriving, axis=1)
    from_rep = jnp.sum(jnp.where(arriving, source_rep[None, :], 0), axis=1)
    leaving = jnp.any(move_src[None, :] == local_ids[:, None], axis=1)
    inbound = incoming[:, None, None]
    staying = (~leaving)[:, None, None]
    zero_key = jnp.zeros((), cache_keys.dtype)
    kept_keys = jnp.where(staying, cache_keys, zero_key)
    kept_values = jnp.where(staying, cache_values, zero_key)
    base_keys = jnp.where(inbound, arrived_keys[from_rep], kept_keys)
    base_values = jnp.where(inbound, arrived_values[from_rep], kept_values)
    fresh_keys, fresh_values = new_entries(hidden, key_weight, value_weight, key_gain, new_length)
    keys_out = fill(base_keys, fresh_keys, new_length, alive)
    values_out = fill(base_values, fresh_values, new_length, alive)
    mixture = attend(keys_out, values_out, new_length, queries, head_dim)
    head_terms = jnp.dot(
        mixture.reshape(local_count * 2, -1), out_weight, preferred_element_type=jnp.float32
    )
    head_terms = head_terms.reshape(local_count, 2, -1)
    head_terms = jnp.where(alive[:, None, None], head_terms, 0.0)
    tensors = lax.axis_size("tensor")
    terms = head_terms.reshape(local_count, 2, tensors, -1)
    terms = lax.all_to_all(terms, "tensor", split_axis=2, concat_axis=2, tiled=True)
    attn_branch = jnp.sum(terms, axis=2).astype(jnp.bfloat16)
    live = lax.dynamic_slice_in_dim(scalars, LIVE, local_count - MOVES)
    listed = jnp.concatenate([keys_out[live], values_out[live]], axis=1)
    return attn_branch.reshape(2 * local_count, -1), listed


def place_kernel(scalar_ref, dead_ref, flat_ref, list_hbm, branch_ref, keys_hbm, values_hbm, listed, zeros, sem):
    rows = zeros.shape[0]
    live = listed.shape[0]
    load = pltpu.make_async_copy(list_hbm, listed, sem.at[live + MOVES, 0])
    load.start()
    zeros[...] = jnp.zeros_like(zeros)

    def copies(e):
        slot = scalar_ref[LIVE + e]
        return (
            pltpu.make_async_copy(listed.at[e, pl.ds(0, rows)], keys_hbm.at[slot], sem.at[e, 0]),
            pltpu.make_async_copy(listed.at[e, pl.ds(rows, rows)], values_hbm.at[slot], sem.at[e, 1]),
        )

    def clears(e):
        slot = dead_ref[e]
        return (
            pltpu.make_async_copy(zeros, keys_hbm.at[slot], sem.at[live + e, 0]),
            pltpu.make_async_copy(zeros, values_hbm.at[slot], sem.at[live + e, 1]),
        )

    def run(make, count, act):
        def each(e, _):
            for copy in make(e):
                getattr(copy, act)()
            return 0

        lax.fori_loop(0, count, each, 0)

    run(clears, MOVES, "start")
    load.wait()
    run(copies, live, "start")
    for s in range(branch_ref.shape[0]):
        branch_ref[s] = flat_ref[2 * s : 2 * s + 2, :]
    run(clears, MOVES, "wait")
    run(copies, live, "wait")


def place(scalars, dead_slots, branch, listed, slots):
    live, both, width = listed.shape
    shape = jax.ShapeDtypeStruct((slots, both // 2, width), listed.dtype)
    smem = pl.BlockSpec(memory_space=pltpu.SMEM)
    vmem = pl.BlockSpec(memory_space=pltpu.VMEM)
    any_ = pl.BlockSpec(memory_space=pl.ANY)
    return pl.pallas_call(
        place_kernel,
        out_shape=(jax.ShapeDtypeStruct((slots, 2, branch.shape[1]), branch.dtype), shape, shape),
        in_specs=[smem, smem, vmem, any_],
        out_specs=(vmem, any_, any_),
        scratch_shapes=[
            pltpu.VMEM(listed.shape, listed.dtype),
            pltpu.VMEM((both // 2, width), listed.dtype),
            pltpu.SemaphoreType.DMA((slots + 1, 2)),
        ],
    )(scalars, dead_slots, branch, listed)


def shards(hidden, queries, cache_keys, cache_values, key_weight, value_weight, key_gain, out_weight, lengths, move_src, move_dst):
    slots = cache_keys.shape[0]
    replicas, tensors = lax.axis_size("replica"), lax.axis_size("tensor")
    me = lax.axis_index("replica").astype(jnp.int32)
    tier, dead, scalars = plan(me.reshape(1), lengths, move_src, move_dst, slots, replicas)
    operands = (scalars, key_gain, hidden, queries, cache_keys, cache_values, key_weight, value_weight, out_weight)

    def ring(t):
        return lambda scalars, gain, *rest: layer(t, replicas, tensors, scalars, gain.reshape(1, -1), *rest[:-3])

    branches = [ring(t) for t in TIERS] + [plain_layer]
    branch, listed = lax.switch(tier[0], branches, *operands, lengths, move_src, move_dst)
    return place(scalars, dead, branch, listed, slots)


def solution(mesh):
    placed = (
        P("replica", None, None),
        P("replica", None, "tensor"),
        P("replica", None, "tensor"),
        P("replica", None, "tensor"),
        P(None, "tensor"),
        P(None, "tensor"),
        P(),
        P("tensor", None),
        P(),
        P(),
        P(),
    )
    return jax.shard_map(
        shards,
        mesh=mesh,
        in_specs=placed,
        out_specs=(
            P("replica", None, "tensor"),
            P("replica", None, "tensor"),
            P("replica", None, "tensor"),
        ),
        check_vma=False,
    )
```

```python
import functools
import math

import jax
import jax.numpy as jnp
from jax import lax
from jax.experimental import pallas as pl
from jax.experimental.pallas import tpu as pltpu
from jax.sharding import PartitionSpec as P

EPS = 1e-06
THETA = 1000000.0
MESH = pl.DeviceIdType.MESH
VMEM_LIMIT = 60 * 1024 * 1024
MOVES = 14
KEPT_ROWS, CAME_ROWS = 8, 16
TIERS = (
    ((7, 4, 3, 1), 10),
    ((7, 5, 3, 1), 10),
    ((7, 5, 3, 2), 10),
    ((7, 5, 4, 2), 10),
    ((8, 6, 4, 2), 10),
    ((7, 6, 5, 3), 10),
    ((10, 7, 5, 3), 12),
)
PARTS = 2
Y_WINDOW = 3 * PARTS
HAND_WINDOW = 3 * PARTS
PAUSES = range(5, 100, 3)


def route(slots, replicas, me, src, dst):
    width = 128

    def column(row):
        tall = jnp.broadcast_to(row.astype(jnp.float32), (width, moves))
        return jnp.concatenate([tall[:, i : i + width].T for i in range(0, moves, width)], axis=0).astype(jnp.int32)

    def down(of, *rows):
        cuts = [[row[:, i : i + width] for row in rows] for i in range(0, moves, width)]
        return jnp.concatenate([jnp.sum(of(*cut), axis=0, keepdims=True) for cut in cuts], axis=1)

    ring = replicas // 4
    half = ring // 2
    core_bits, ring_bits, slot_bits = 1, ring.bit_length() - 1, slots.bit_length() - 1
    assert slots == 1 << slot_bits and ring == 1 << ring_bits
    moves = src.shape[1]
    order = lax.broadcasted_iota(jnp.int32, (1, moves), 1)
    exists = order < replicas * MOVES
    from_rep, to_rep = src >> slot_bits, dst >> slot_bits

    def coordinates(rep):
        return rep >> (core_bits + ring_bits), (rep >> core_bits) & (ring - 1), rep & 1

    ys, zs, cs = coordinates(from_rep)
    yd, zd, cd = coordinates(to_rep)
    ahead = jnp.where(exists, (zd - zs) & (ring - 1), 0)
    group = (yd * ring + zs) * 2 + cs
    distance = jnp.where(ahead <= half, ahead, ring - ahead)
    travels = ahead != 0
    pull = jnp.where((ahead == half) | ~travels, 0, jnp.where(ahead < half, ahead, ahead - ring))
    farthest = ahead == half

    other, other_group, other_pull = column(order), column(group), column(pull)
    other_far = column(jnp.where(farthest, group, -1))
    lean = down(lambda g: jnp.where(other_group == g, other_pull, 0), group)
    rank_far = down(lambda g, n: jnp.where((other_far == g) & (other < n), 1, 0), group, order)
    way = jnp.where(ahead < half, 0, 1)
    for i in range(4):
        back = lean > 0
        way = jnp.where(farthest & (rank_far == i), jnp.where(back, 1, 0), way)
        lean = lean + jnp.where(back, -half, half)
    list_key = group * 2 + way
    sort_key = (list_key * 8 + 7 - distance) * moves + order
    other_key = column(jnp.where(travels, sort_key, -1))
    least = list_key * (8 * moves)
    place_in = down(lambda low, key: jnp.where((other_key >= low) & (other_key < key), 1, 0), least, sort_key)
    spot = 2 * place_in + way
    crosses = travels & (ys != yd)
    y_key = from_rep * 64 + spot
    other_y = column(jnp.where(crosses, y_key, -1))
    y_rank = down(lambda low, key: jnp.where((other_y >= low) & (other_y < key), 1, 0), from_rep * 64, y_key)

    tier = jnp.full((1, 1), len(TIERS), jnp.int32)
    for i, (caps, y_cap) in reversed(list(enumerate(TIERS))):
        reach = sum(jnp.where(place_in < c, 1, 0) for c in caps)
        misfit = travels & ((distance > reach) | (crosses & (y_rank >= y_cap)))
        tier = jnp.where(jnp.sum(jnp.where(misfit, 1, 0), axis=1, keepdims=True) == 0, i, tier)

    my_y, my_z, my_c = coordinates(me)
    mine = exists & (from_rep == me)
    in_group = travels & (group == (my_y * ring + my_z) * 2 + my_c)
    kind = jnp.where(ys == yd, 0, jnp.where(cs == cd, 1, 2))
    address = jnp.where(
        in_group,
        jnp.where(spot < 32, spot, -1),
        jnp.where(
            mine,
            jnp.where(travels, 32 + y_rank, 48 + kind),
            jnp.where(exists & (to_rep == me), 64 + (dst & (slots - 1)), -1),
        ),
    )
    code = (((place_in * 2 + way) * 8 + distance) * 4 + kind) * 1024 + src + 1
    value = jnp.where(mine, src & (slots - 1), jnp.where(in_group, slots + y_rank, code))
    lane = lax.broadcasted_iota(jnp.int32, (1, width), 1)
    hit = column(address) == lane
    table = jnp.sum(jnp.where(hit, column(value), 0), axis=0, keepdims=True)
    return jnp.where(lane == width - 1, tier, table)


INJECT, ACROSS, NEAR, LIVE, LENGTH, LANE, SPOT, KIND, TOKENS, ROW, TABLE = 0, 32, 48, 64, 96, 128, 144, 160, 176, 208, 240


def plan_kernel(
    slots,
    replicas,
    me_ref,
    len_ref,
    src_ref,
    src_row,
    dst_row,
    tier_ref,
    dead_ref,
    out_ref,
    mark,
    padded,
    table_vmem,
    table_ref,
    sem,
):
    me = me_ref[0]
    slot_bits = slots.bit_length() - 1
    count = src_row.shape[1]
    padded[...] = jnp.zeros_like(padded)
    padded[0:1, :count] = src_row[...]
    padded[1:2, :count] = dst_row[...]

    table_vmem[...] = route(slots, replicas, me, padded[0:1, :], padded[1:2, :])
    fetch = pltpu.make_async_copy(table_vmem, table_ref, sem)
    fetch.start()

    def clear(i, _):
        mark[i] = 0
        return 0

    lax.fori_loop(0, slots, clear, 0, unroll=8)

    def out(k, _):
        mark[src_ref[me * MOVES + k] & (slots - 1)] = 1
        return 0

    lax.fori_loop(0, MOVES, out, 0, unroll=2)
    fetch.wait()
    tier_ref[0] = table_ref[0, 127]

    def copy(i, _):
        out_ref[INJECT + i] = table_ref[0, i]
        return 0

    lax.fori_loop(0, 64, copy, 0, unroll=8)

    def each(s, counts):
        kept_count, in_count, dead_count = counts
        code = table_ref[0, 64 + s]
        incoming = code > 0
        source = jnp.where(incoming, (code - 1) & 1023, me * slots + s)
        length = len_ref[source]
        stays = jnp.logical_not(incoming) & (mark[s] == 0) & (length > 0)
        alive = incoming | stays
        length = jnp.where(alive, length, 0)
        at = jnp.where(incoming, slots - 2 * MOVES + in_count, kept_count)
        where = jnp.where(alive, at, slots - 1)
        out_ref[LIVE + where] = s
        out_ref[LENGTH + where] = length
        dead_ref[dead_count] = s
        rest = (code - 1) >> 10
        kind = rest & 3
        distance = (rest >> 2) & 7
        way = (rest >> 5) & 1
        slot_in = jnp.where(incoming, in_count, MOVES)
        other_core = ((source >> slot_bits) ^ me) & 1
        out_ref[LANE + slot_in] = (other_core * 2 + way) * 4 + distance - 1
        out_ref[SPOT + slot_in] = rest >> 6
        out_ref[KIND + slot_in] = jnp.where(distance == 0, kind, -1)
        out_ref[TOKENS + s] = length
        out_ref[ROW + s] = jnp.where(alive, jnp.where(incoming, 2 * KEPT_ROWS + in_count, kept_count), -1)
        one = jnp.int32(1)
        return (
            kept_count + jnp.where(stays, one, 0),
            in_count + jnp.where(incoming, one, 0),
            dead_count + jnp.where(alive, 0, one),
        )

    zero = jnp.int32(0)
    lax.fori_loop(0, slots, each, (zero, zero, zero), unroll=2)


def plan(me, lengths, move_src, move_dst, slots, replicas):
    smem = pl.BlockSpec(memory_space=pltpu.SMEM)
    vmem = pl.BlockSpec(memory_space=pltpu.VMEM)
    ints = lambda n: jax.ShapeDtypeStruct((n,), jnp.int32)
    moves = -(-move_src.shape[0] // 128) * 128
    return pl.pallas_call(
        functools.partial(plan_kernel, slots, replicas),
        out_shape=(ints(1), ints(slots + 1), ints(TABLE)),
        in_specs=[smem] * 3 + [vmem] * 2,
        out_specs=(smem,) * 3,
        scratch_shapes=[
            pltpu.SMEM((slots,), jnp.int32),
            pltpu.VMEM((8, moves), jnp.int32),
            pltpu.VMEM((1, 128), jnp.int32),
            pltpu.SMEM((1, 128), jnp.int32),
            pltpu.SemaphoreType.DMA,
        ],
    )(me, lengths, move_src, move_src.reshape(1, -1), move_dst.reshape(1, -1))


def crossings(y_cap):
    return [(b, part) for low in range(0, y_cap, 2) for part in range(PARTS) for b in range(low, min(low + 2, y_cap))]


def timetable(caps, y_cap):
    step, lag = 1.0 / PARTS, 0.5
    across = {key: (n + 1) * step + lag for n, key in enumerate(crossings(y_cap))}
    ready = [
        (across[min(i, y_cap - 1), part] + 0.01 * max(0, i - y_cap), 1, "inject", i % 2, 1, i // 2, part)
        for i in range(2 * caps[0])
        for part in range(PARTS)
    ]
    free = [0.0, 0.0]
    events = []
    while ready:
        ready.sort()
        time, _, what, way, hop, spot, part = event = ready.pop(0)
        events.append(event[2:])
        if what == "inject" or (hop < len(caps) and spot < caps[hop]):
            free[way] = max(free[way], time) + step
            onward = hop if what == "inject" else hop + 1
            ready.append((free[way] + lag, 0, "pass", way, onward, spot, part))
    return events


class Ring:
    def __init__(self, tier, replicas, me, scalars, caches, arrived, inject, across, across_in, near, *sems):
        self.caps, self.y_cap = tier
        self.me, self.scalars, self.caches = me, scalars, caches
        self.arrived, self.inject, self.across, self.across_in, self.near = arrived, inject, across, across_in, near
        self.hop_send, self.hop_recv, self.core_send, self.core_recv, self.y_send, self.y_recv, self.near_send, self.near_recv = sems
        half = replicas // 2
        line = (me // half) * half
        ahead = line + lax.rem(me - line + 2, half)
        behind = line + lax.rem(me - line + half - 2, half)
        core = me + 1 - 2 * lax.rem(me, 2)
        opposite = lax.rem(me + half, replicas)
        both = lax.rem(core + half, replicas)
        self.ways = (ahead, behind)
        self.core, self.opposite = core, opposite
        self.near_peers = (core, opposite, both)
        self.partners = 5
        self.events = timetable(self.caps, self.y_cap)
        self.lanes = 2 * sum(self.caps)

    def greet(self, barrier):
        for peer in self.ways + self.near_peers:
            pl.semaphore_signal(barrier, inc=1, device_id={"replica": peer}, device_id_type=MESH)

    def copy(self, source, target, send_sem, recv_sem, peer):
        return pltpu.make_async_remote_copy(
            src_ref=source, dst_ref=target, send_sem=send_sem, recv_sem=recv_sem, device_id={"replica": peer}, device_id_type=MESH
        )

    def lane(self, way, hop, spot):
        return way * sum(self.caps) + sum(self.caps[: hop - 1]) + spot

    def half(self, ref, at, part):
        rows = 2 * self.caches[0].shape[1] // PARTS
        return ref.at[at, pl.ds(part * rows, rows)]

    def own(self, slot, part):
        rows = 2 * self.caches[0].shape[1] // PARTS
        which, low = part * 2 // PARTS, part % (PARTS // 2) * rows
        return self.caches[which][slot, low : low + rows, :]

    def cross(self, b, part):
        at = b * PARTS + part
        return self.copy(
            self.half(self.across, b, part), self.half(self.across_in, b, part), self.y_send.at[at], self.y_recv.at[at], self.opposite
        )

    def next_door(self, j):
        target = self.arrived.at[2 * self.lanes + j]
        return self.copy(self.near.at[j], target, self.near_send.at[j], self.near_recv.at[j], self.near_peers[j])

    def hop(self, way, hop, spot, part):
        source = (self.inject, 2 * spot + way) if hop == 1 else (self.arrived, self.lane(way, hop - 1, spot))
        to = self.lane(way, hop, spot)
        at = to * PARTS + part
        return self.copy(
            self.half(*source, part), self.half(self.arrived, to, part), self.hop_send.at[at], self.hop_recv.at[at], self.ways[way]
        )

    def hand_over(self, way, hop, spot, part):
        lane = self.lane(way, hop, spot)
        at = lane * PARTS + part
        return self.copy(
            self.half(self.arrived, lane, part),
            self.half(self.arrived, self.lanes + lane, part),
            self.core_send.at[at],
            self.core_recv.at[at],
            self.core,
        )

    def pack(self, target, at, slot, parts):
        rows = 2 * self.caches[0].shape[1] // PARTS
        for part in parts:
            target[at, part * rows : (part + 1) * rows, :] = self.own(slot, part)

    def begin(self, n):
        order = crossings(self.y_cap)
        if n < len(order):
            b, part = order[n]
            self.pack(self.across, b, self.scalars[ACROSS + b], (part,))
            self.cross(b, part).start()
        elif n < len(order) + 3:
            j = n - len(order)
            self.pack(self.near, j, self.scalars[NEAR + j], range(PARTS))
            self.next_door(j).start()

    def enter(self, way, spot, part, crossed):
        slots = self.caches[0].shape[0]
        rows = 2 * self.caches[0].shape[1] // PARTS
        i = 2 * spot + way
        here = slice(part * rows, (part + 1) * rows)
        code = self.scalars[INJECT + i]
        block = self.own(jnp.where(code < slots, code, 0), part)
        if crossed == len(crossings(self.y_cap)):
            other = self.across_in[jnp.where(code < slots, 0, code - slots), here, :]
            block = jnp.where(code < slots, block, other)
        else:
            for b in range(min(i + 1, self.y_cap)):
                block = jnp.where(code == slots + b, self.across_in[b, here, :], block)
        self.inject[i, here, :] = block
        self.hop(way, 1, spot, part).start()

    def carry(self, loaded, pauses):
        order = crossings(self.y_cap)
        for n in range(PARTS):
            self.begin(n)
        loaded()
        for n in range(PARTS, Y_WINDOW):
            self.begin(n)
        crossed = 0
        pauses = dict(pauses)
        over = []
        for count, (what, way, hop, spot, part) in enumerate(self.events):
            if what == "inject":
                needed = order.index((min(2 * spot + way, self.y_cap - 1), part)) + 1
                while crossed < needed:
                    self.cross(*order[crossed]).wait_recv()
                    self.begin(crossed + Y_WINDOW)
                    crossed += 1
                self.enter(way, spot, part, crossed)
            else:
                self.hop(way, hop, spot, part).wait_recv()
                if hop < len(self.caps) and spot < self.caps[hop]:
                    self.hop(way, hop + 1, spot, part).start()
                self.hand_over(way, hop, spot, part).start()
                over.append((way, hop, spot, part))
                if len(over) > HAND_WINDOW:
                    self.hand_over(*over[-1 - HAND_WINDOW]).wait()
            if count in pauses:
                pauses.pop(count)()
        for pause in pauses.values():
            pause()
        for n in range(crossed, len(order)):
            self.cross(*order[n]).wait_recv()
        for n in range(max(Y_WINDOW, crossed + Y_WINDOW), len(order) + 3):
            self.begin(n)
        for j in range(3):
            self.next_door(j).wait_recv()
        for key in over[-HAND_WINDOW:]:
            self.hand_over(*key).wait()

    def where(self, i):
        kind, lane = self.scalars[KIND + i], self.scalars[LANE + i]
        first = 0
        for n in range(2 * 2 * len(self.caps)):
            way, hop = n // len(self.caps) % 2, n % len(self.caps) + 1
            first = jnp.where(lane == n, n // (2 * len(self.caps)) * self.lanes + self.lane(way, hop, 0), first)
        return jnp.where(kind >= 0, 2 * self.lanes + kind, first + self.scalars[SPOT + i])

    def finish(self):
        for b, part in crossings(self.y_cap):
            self.cross(b, part).wait_send()
        for j in range(3):
            self.next_door(j).wait_send()
        for what, way, hop, spot, part in self.events:
            if what == "pass":
                self.hop(way, hop, spot, part).wait_send()


def layer_kernel(
    replicas,
    tensors,
    tier,
    scalar_ref,
    gain_ref,
    hidden_hbm,
    query_hbm,
    ck_hbm,
    cv_hbm,
    kw_hbm,
    vw_hbm,
    ow_hbm,
    branch_ref,
    list_hbm,
    ck,
    cv,
    hid,
    qry,
    kw,
    vw,
    ow,
    flat,
    listed,
    fresh_k,
    fresh_v,
    mix,
    score,
    rs_stage,
    rs_recv,
    reduced,
    row_ref,
    in_sem,
    rs_send_sem,
    rs_recv_sem,
    list_sem,
    *transport,
):
    me = lax.axis_index("replica")
    at = lax.axis_index("tensor")
    slots, rows, width = ck.shape
    live = listed.shape[0]
    kept = live - MOVES
    groups = query_hbm.shape[2] // width

    loads = [
        pltpu.make_async_copy(source, target, in_sem.at[i])
        for i, (source, target) in enumerate(
            (
                (ck_hbm, ck),
                (cv_hbm, cv),
                (hidden_hbm, hid),
                (kw_hbm, kw),
                (vw_hbm, vw),
                (query_hbm, qry),
                (ow_hbm, ow),
            )
        )
    ]
    loads[0].start()
    loads[1].start()

    caches = (ck, cv)
    road = Ring(tier, replicas, me, scalar_ref, caches, *transport)

    barrier = pltpu.get_barrier_semaphore()
    road.greet(barrier)

    def greet_tensor(j, _):
        pl.semaphore_signal(barrier, inc=1, device_id={"tensor": lax.rem(at + j, tensors)}, device_id_type=MESH)
        return 0

    lax.fori_loop(1, tensors, greet_tensor, 0)
    pl.semaphore_wait(barrier, road.partners + tensors - 1)

    loads[0].wait()

    def clear():
        mix[...] = jnp.zeros_like(mix)
        reduced[...] = jnp.zeros_like(reduced)

    def tell():
        def one(s, _):
            tokens, row = scalar_ref[TOKENS + s], scalar_ref[ROW + s]
            stride = jnp.where(row < 2 * KEPT_ROWS, KEPT_ROWS, CAME_ROWS)
            for t in range(2):
                at = jnp.where(row < 0, -1, row + t * stride)
                row_ref[pl.ds(2 * s + t, 1), :] = jnp.full((1, width), tokens + t, jnp.int32).astype(jnp.float32)
                row_ref[pl.ds(2 * (slots + s) + t, 1), :] = jnp.full((1, width), at, jnp.int32).astype(jnp.float32)
            return 0

        lax.fori_loop(0, slots, one, 0, unroll=2)

    def flatten():
        loads[2].wait()
        for s in range(slots):
            flat[2 * s : 2 * s + 2, :] = hid[s]

    def project_keys():
        loads[3].wait()
        fresh_k[...] = jnp.dot(flat[...], kw[...], preferred_element_type=jnp.float32)

    def project_values():
        loads[4].wait()
        raw_v = jnp.dot(flat[...], vw[...], preferred_element_type=jnp.float32)
        fresh_v[...] = raw_v.astype(jnp.bfloat16).astype(jnp.float32)

    lane = lax.broadcasted_iota(jnp.int32, (1, width), 1)

    def rotate_keys():
        raw_k = fresh_k[...]
        mean_square = jnp.mean(raw_k * raw_k, axis=-1, keepdims=True)
        normed = raw_k * lax.rsqrt(mean_square + EPS) * gain_ref[...]
        half = width // 2
        index = jnp.where(lane < half, lane, lane - half).astype(jnp.float32)
        angles = row_ref[: 2 * slots, :] * jnp.exp(index * (-2.0 * math.log(THETA) / width))
        turned = pltpu.roll(normed, half, 1)
        sine = jnp.sin(angles)
        rotated = normed * jnp.cos(angles) + turned * jnp.where(lane < half, -sine, sine)
        fresh_k[...] = rotated.astype(jnp.bfloat16).astype(jnp.float32)

    row_ids = lax.broadcasted_iota(jnp.int32, (rows, width), 0)
    column_ids = lax.broadcasted_iota(jnp.int32, (2 * groups, rows), 1)
    step_ids = lax.broadcasted_iota(jnp.int32, (2 * groups, rows), 0) % 2

    def placed(stored, fresh, slot, length):
        full = jnp.where(row_ids < length, stored.astype(jnp.float32), 0.0)
        full = jnp.where(row_ids == length, fresh[pl.ds(2 * slot, 1), :], full)
        full = jnp.where(row_ids == length + 1, fresh[pl.ds(2 * slot + 1, 1), :], full)
        return full.astype(jnp.bfloat16)

    heads = 2 * groups

    def attend(first, count, stored, unroll):
        def fill(i, _):
            e = first + i
            slot, length = scalar_ref[LIVE + e], scalar_ref[LENGTH + e]
            stored_k, stored_v = stored(i)
            listed[e, :rows, :] = placed(stored_k, fresh_k, slot, length)
            listed[e, rows:, :] = placed(stored_v, fresh_v, slot, length)
            pltpu.make_async_copy(listed.at[e], list_hbm.at[e], list_sem.at[e]).start()
            return 0

        def weigh(i, _):
            e = first + i
            slot, length = scalar_ref[LIVE + e], scalar_ref[LENGTH + e]
            q = qry[slot].astype(jnp.float32)
            q = jnp.concatenate([q[:, g * width : (g + 1) * width] for g in range(groups)], axis=0).astype(jnp.bfloat16)
            scores = lax.dot_general(
                q, listed[e, :rows, :], (((1,), (1,)), ((), ())), preferred_element_type=jnp.float32
            ) * width ** (-0.5)
            at = pl.ds(pl.multiple_of(e * heads, heads), heads)
            score[at, :] = jnp.where(column_ids <= length + step_ids, scores, -jnp.inf)
            return 0

        def blend(i, _):
            e = first + i
            at = pl.ds(pl.multiple_of(e * heads, heads), heads)
            mix[at, :] = jnp.dot(score[at, :].astype(jnp.bfloat16), listed[e, rows:, :], preferred_element_type=jnp.float32)
            return 0

        lax.fori_loop(0, count, fill, 0, unroll=2)
        lax.fori_loop(0, count, weigh, 0, unroll=unroll)
        every = slice(first * heads, (first + count) * heads)
        scores = score[every, :]
        weights = jnp.exp(scores - jnp.max(scores, axis=-1, keepdims=True))
        score[every, :] = weights / jnp.sum(weights, axis=-1, keepdims=True)
        lax.fori_loop(0, count, blend, 0, unroll=unroll)

    def own(i):
        slot = scalar_ref[LIVE + i]
        return ck[slot], cv[slot]

    def brought(i):
        source = road.where(i)
        return road.arrived[source, :rows, :], road.arrived[source, rows:, :]

    def attend_kept():
        loads[5].wait()
        attend(0, kept, own, kept)
        loads[6].wait()

    out_width = branch_ref.shape[1]
    groups_of_rows = ((0, KEPT_ROWS, 0), (kept, CAME_ROWS, 2 * KEPT_ROWS))

    def mixture(group):
        first, count, _ = groups_of_rows[group]
        steps = [
            jnp.concatenate(
                [mix[pl.ds(first * heads + 2 * g + t, count, stride=heads), :] for g in range(groups)], axis=1
            )
            for t in range(2)
        ]
        return jnp.concatenate(steps, axis=0).astype(jnp.bfloat16)

    def term(mixed, j):
        first = pl.multiple_of(lax.rem(at + j, tensors) * out_width, 128)
        return jnp.dot(mixed, ow[:, pl.ds(first, out_width)], preferred_element_type=jnp.float32)

    def give(group, j):
        _, count, low = groups_of_rows[group]
        n = group * tensors + j
        return pltpu.make_async_remote_copy(
            src_ref=rs_stage.at[j, pl.ds(low, 2 * count)],
            dst_ref=rs_recv.at[j, pl.ds(low, 2 * count)],
            send_sem=rs_send_sem.at[n],
            recv_sem=rs_recv_sem.at[n],
            device_id={"tensor": lax.rem(at + j, tensors)},
            device_id_type=MESH,
        )

    def give_term(group, mixed, j):
        _, count, low = groups_of_rows[group]
        rs_stage[j, low : low + 2 * count, :] = term(mixed, j).astype(jnp.bfloat16)
        give(group, j).start()

    def add_up(group, own_term):
        _, count, low = groups_of_rows[group]
        total = own_term
        for j in range(1, tensors):
            give(group, j).wait_recv()
            total = total + rs_recv[j, low : low + 2 * count, :].astype(jnp.float32)
        reduced[low : low + 2 * count, :] = total.astype(jnp.bfloat16)

    def give_kept(j):
        give_term(0, mixture(0), j)

    pieces = [clear, tell, flatten, project_keys, project_values, rotate_keys, attend_kept]
    pieces += [functools.partial(give_kept, j) for j in range(1, tensors)]

    def loaded():
        loads[1].wait()
        for load in loads[2:]:
            load.start()

    road.carry(loaded, zip(PAUSES, pieces))
    attend(kept, MOVES, brought, 7)

    mixed = mixture(1)

    def give_came(j, _):
        give_term(1, mixed, j)
        return 0

    lax.fori_loop(1, tensors, give_came, 0)
    own_term = term(mixed, 0)
    road.finish()
    add_up(0, term(mixture(0), 0))
    add_up(1, own_term)
    rows_at = row_ref[2 * slots :, :]
    pick = (lane.astype(jnp.float32) == rows_at).astype(jnp.float32).astype(jnp.bfloat16)
    branch_ref[...] = jnp.dot(pick, reduced[...], preferred_element_type=jnp.float32).astype(jnp.bfloat16)

    def given(j, _):
        for group in range(2):
            give(group, j).wait_send()
        return 0

    lax.fori_loop(1, tensors, given, 0)

    def written(e, _):
        pltpu.make_async_copy(listed.at[e], list_hbm.at[e], list_sem.at[e]).wait()
        return 0

    lax.fori_loop(0, live, written, 0)


def layer(tier, replicas, tensors, scalars, gain, *operands):
    hidden, queries, cache_keys, cache_values, key_weight, value_weight, out_weight = operands
    slots, rows, width = cache_keys.shape
    live = slots - MOVES
    groups = queries.shape[2] // width
    out_width = out_weight.shape[1] // tensors
    smem = pl.BlockSpec(memory_space=pltpu.SMEM)
    vmem = pl.BlockSpec(memory_space=pltpu.VMEM)
    any_ = pl.BlockSpec(memory_space=pl.ANY)
    bf16 = jnp.bfloat16
    dma = pltpu.SemaphoreType.DMA

    def rollouts(n):
        return pltpu.VMEM((n, 2 * rows, width), bf16)

    caps, y_cap = tier
    lanes = 2 * sum(caps)
    transport = [
        rollouts(2 * lanes + 3),
        rollouts(2 * caps[0]),
        rollouts(y_cap),
        rollouts(y_cap),
        rollouts(3),
    ]
    sizes = (lanes * PARTS, lanes * PARTS, lanes * PARTS, lanes * PARTS, y_cap * PARTS, y_cap * PARTS, 3, 3)
    transport += [dma((n,)) for n in sizes]
    return pl.pallas_call(
        functools.partial(layer_kernel, replicas, tensors, tier),
        out_shape=(
            jax.ShapeDtypeStruct((2 * slots, out_width), bf16),
            jax.ShapeDtypeStruct((live, 2 * rows, width), bf16),
        ),
        in_specs=[smem, vmem] + [any_] * len(operands),
        out_specs=(vmem, any_),
        scratch_shapes=[
            pltpu.VMEM(cache_keys.shape, bf16),
            pltpu.VMEM(cache_values.shape, bf16),
            pltpu.VMEM(hidden.shape, bf16),
            pltpu.VMEM(queries.shape, bf16),
            pltpu.VMEM(key_weight.shape, bf16),
            pltpu.VMEM(value_weight.shape, bf16),
            pltpu.VMEM(out_weight.shape, bf16),
            pltpu.VMEM((2 * slots, hidden.shape[2]), bf16),
            pltpu.VMEM((live, 2 * rows, width), bf16),
            pltpu.VMEM((2 * slots, width), jnp.float32),
            pltpu.VMEM((2 * slots, width), jnp.float32),
            pltpu.VMEM((2 * groups * (slots - 2 * MOVES + CAME_ROWS), width), jnp.float32),
            pltpu.VMEM((2 * groups * live, rows), jnp.float32),
            pltpu.VMEM((tensors, 2 * (KEPT_ROWS + CAME_ROWS), out_width), bf16),
            pltpu.VMEM((tensors, 2 * (KEPT_ROWS + CAME_ROWS), out_width), bf16),
            pltpu.VMEM((128, out_width), bf16),
            pltpu.VMEM((4 * slots, width), jnp.float32),
            dma((len(operands),)),
            dma((2 * tensors,)),
            dma((2 * tensors,)),
            dma((live,)),
        ]
        + transport,
        compiler_params=pltpu.CompilerParams(
            collective_id=TIERS.index(tier),
            has_side_effects=True,
            vmem_limit_bytes=VMEM_LIMIT,
        ),
    )(scalars, gain, *operands)


def rotate(vectors, positions):
    half_width = vectors.shape[-1] // 2
    indices = jnp.arange(half_width, dtype=jnp.float32)
    frequency = jnp.exp(indices * (-2.0 * math.log(THETA) / vectors.shape[-1]))
    angles = positions[:, :, None, None] * frequency
    cosine = jnp.cos(angles)
    sine_values = jnp.sin(angles)
    former = vectors[..., :half_width]
    latter = vectors[..., half_width:]
    return jnp.concatenate(
        [former * cosine - latter * sine_values, latter * cosine + former * sine_values], -1
    )


def new_entries(hidden, key_weight, value_weight, key_gain, length):
    row_count = hidden.shape[0]
    flat_rows = hidden.reshape(row_count * 2, hidden.shape[2])
    raw_keys = jnp.dot(flat_rows, key_weight, preferred_element_type=jnp.float32).reshape(
        row_count, 2, -1, key_gain.shape[0]
    )
    mean_square = jnp.mean(raw_keys * raw_keys, axis=-1, keepdims=True)
    normed = raw_keys * lax.rsqrt(mean_square + EPS) * key_gain
    positions = (length[:, None] + jnp.arange(2, dtype=jnp.int32)[None, :]).astype(jnp.float32)
    fresh_keys = rotate(normed, positions).reshape(row_count, 2, -1).astype(jnp.bfloat16)
    fresh_values = (
        jnp.dot(flat_rows, value_weight, preferred_element_type=jnp.float32)
        .reshape(row_count, 2, -1)
        .astype(jnp.bfloat16)
    )
    return (fresh_keys, fresh_values)


def fill(stored, fresh, length, active):
    row_ids = jnp.arange(stored.shape[1], dtype=jnp.int32)[None, :, None]
    border = length[:, None, None]
    kept = jnp.where(row_ids < border, stored, jnp.zeros_like(stored))
    kept = jnp.where(row_ids == border, fresh[:, 0:1, :], kept)
    kept = jnp.where(row_ids == border + 1, fresh[:, 1:2, :], kept)
    return jnp.where(active[:, None, None], kept, jnp.zeros_like(kept))


def attend(full_keys, full_values, length, queries, head_dim):
    row_count, key_rows, width = full_keys.shape
    kv_heads = width // head_dim
    group_size = queries.shape[-1] // width
    query_heads = queries.reshape(row_count, 2, kv_heads, group_size, head_dim)
    key_heads = full_keys.reshape(row_count, key_rows, kv_heads, head_dim)
    value_heads = full_values.reshape(row_count, key_rows, kv_heads, head_dim)
    scores = jnp.einsum(
        "rsvgh,rlvh->rvsgl", query_heads, key_heads, preferred_element_type=jnp.float32
    ) * head_dim ** (-0.5)
    row_ids = jnp.arange(key_rows, dtype=jnp.int32)[None, None, :]
    limits = length[:, None, None] + jnp.arange(2, dtype=jnp.int32)[None, :, None]
    visible = row_ids <= limits
    scores = jnp.where(visible[:, None, :, None, :], scores, -jnp.inf)
    highest = jnp.max(scores, axis=-1, keepdims=True)
    weights = jnp.exp(scores - highest)
    shares = (weights / jnp.sum(weights, axis=-1, keepdims=True)).astype(jnp.bfloat16)
    mixture = jnp.einsum(
        "rvsgl,rlvh->rsvgh", shares, value_heads, preferred_element_type=jnp.float32
    )
    return mixture.reshape(row_count, 2, -1).astype(jnp.bfloat16)


def plain_layer(scalars, key_gain, hidden, queries, cache_keys, cache_values, key_weight, value_weight, out_weight, lengths, move_src, move_dst):
    local_count = cache_keys.shape[0]
    replicas = lax.axis_size("replica")
    replica_here = lax.axis_index("replica")
    first_slot = replica_here * local_count
    head_dim = key_gain.shape[0]
    all_slots = jnp.arange(lengths.shape[0], dtype=jnp.int32)
    anchor = all_slots.at[move_src].set(-1).at[move_dst].set(move_src)
    own_anchor = lax.dynamic_slice_in_dim(anchor, first_slot, local_count)
    holding = own_anchor >= 0
    new_length = jnp.where(holding, lengths[jnp.where(holding, own_anchor, 0)], 0)
    alive = new_length > 0
    local_ids = first_slot + jnp.arange(local_count, dtype=jnp.int32)
    source_rep = move_src // local_count
    target_rep = move_dst // local_count
    peer_ids = jnp.arange(replicas, dtype=jnp.int32)
    sending = (source_rep[None, :] == replica_here) & (target_rep[None, :] == peer_ids[:, None])
    has_out = jnp.any(sending, axis=1)
    send_slot = jnp.sum(jnp.where(sending, move_src[None, :] - first_slot, 0), axis=1)
    outbound = has_out[:, None, None]
    pack_keys = jnp.where(outbound, cache_keys[send_slot], jnp.zeros((), cache_keys.dtype))
    pack_values = jnp.where(outbound, cache_values[send_slot], jnp.zeros((), cache_values.dtype))
    arrived_keys, arrived_values = (
        lax.all_to_all(pack_keys, "replica", split_axis=0, concat_axis=0, tiled=True),
        lax.all_to_all(pack_values, "replica", split_axis=0, concat_axis=0, tiled=True),
    )
    arriving = move_dst[None, :] == local_ids[:, None]
    incoming = jnp.any(arriving, axis=1)
    from_rep = jnp.sum(jnp.where(arriving, source_rep[None, :], 0), axis=1)
    leaving = jnp.any(move_src[None, :] == local_ids[:, None], axis=1)
    inbound = incoming[:, None, None]
    staying = (~leaving)[:, None, None]
    zero_key = jnp.zeros((), cache_keys.dtype)
    kept_keys = jnp.where(staying, cache_keys, zero_key)
    kept_values = jnp.where(staying, cache_values, zero_key)
    base_keys = jnp.where(inbound, arrived_keys[from_rep], kept_keys)
    base_values = jnp.where(inbound, arrived_values[from_rep], kept_values)
    fresh_keys, fresh_values = new_entries(hidden, key_weight, value_weight, key_gain, new_length)
    keys_out = fill(base_keys, fresh_keys, new_length, alive)
    values_out = fill(base_values, fresh_values, new_length, alive)
    mixture = attend(keys_out, values_out, new_length, queries, head_dim)
    head_terms = jnp.dot(
        mixture.reshape(local_count * 2, -1), out_weight, preferred_element_type=jnp.float32
    )
    head_terms = head_terms.reshape(local_count, 2, -1)
    head_terms = jnp.where(alive[:, None, None], head_terms, 0.0)
    tensors = lax.axis_size("tensor")
    terms = head_terms.reshape(local_count, 2, tensors, -1)
    terms = lax.all_to_all(terms, "tensor", split_axis=2, concat_axis=2, tiled=True)
    attn_branch = jnp.sum(terms, axis=2).astype(jnp.bfloat16)
    live = lax.dynamic_slice_in_dim(scalars, LIVE, local_count - MOVES)
    listed = jnp.concatenate([keys_out[live], values_out[live]], axis=1)
    return attn_branch.reshape(2 * local_count, -1), listed


def place_kernel(scalar_ref, dead_ref, flat_ref, list_hbm, branch_ref, keys_hbm, values_hbm, listed, zeros, sem, load_sem):
    rows = zeros.shape[0]
    live = listed.shape[0]

    def load(e):
        return (pltpu.make_async_copy(list_hbm.at[e], listed.at[e], load_sem.at[e]),)

    def copies(e):
        slot = scalar_ref[LIVE + e]
        return (
            pltpu.make_async_copy(listed.at[e, pl.ds(0, rows)], keys_hbm.at[slot], sem.at[e, 0]),
            pltpu.make_async_copy(listed.at[e, pl.ds(rows, rows)], values_hbm.at[slot], sem.at[e, 1]),
        )

    def clears(e):
        slot = dead_ref[e]
        return (
            pltpu.make_async_copy(zeros, keys_hbm.at[slot], sem.at[live + e, 0]),
            pltpu.make_async_copy(zeros, values_hbm.at[slot], sem.at[live + e, 1]),
        )

    def run(count, *acts):
        def each(e, _):
            for make, act in acts:
                for copy in make(e):
                    getattr(copy, act)()
            return 0

        lax.fori_loop(0, count, each, 0, unroll=2)

    run(live, (load, "start"))
    zeros[...] = jnp.zeros_like(zeros)
    run(MOVES, (clears, "start"))
    run(live, (load, "wait"), (copies, "start"))
    for s in range(branch_ref.shape[0]):
        branch_ref[s] = flat_ref[2 * s : 2 * s + 2, :]
    run(MOVES, (clears, "wait"))
    run(live, (copies, "wait"))


def place(scalars, dead_slots, branch, listed, slots):
    live, both, width = listed.shape
    shape = jax.ShapeDtypeStruct((slots, both // 2, width), listed.dtype)
    smem = pl.BlockSpec(memory_space=pltpu.SMEM)
    vmem = pl.BlockSpec(memory_space=pltpu.VMEM)
    any_ = pl.BlockSpec(memory_space=pl.ANY)
    return pl.pallas_call(
        place_kernel,
        out_shape=(jax.ShapeDtypeStruct((slots, 2, branch.shape[1]), branch.dtype), shape, shape),
        in_specs=[smem, smem, vmem, any_],
        out_specs=(vmem, any_, any_),
        scratch_shapes=[
            pltpu.VMEM(listed.shape, listed.dtype),
            pltpu.VMEM((both // 2, width), listed.dtype),
            pltpu.SemaphoreType.DMA((slots, 2)),
            pltpu.SemaphoreType.DMA((live,)),
        ],
    )(scalars, dead_slots, branch, listed)


def shards(hidden, queries, cache_keys, cache_values, key_weight, value_weight, key_gain, out_weight, lengths, move_src, move_dst):
    slots = cache_keys.shape[0]
    replicas, tensors = lax.axis_size("replica"), lax.axis_size("tensor")
    me = lax.axis_index("replica").astype(jnp.int32)
    tier, dead, scalars = plan(me.reshape(1), lengths, move_src, move_dst, slots, replicas)
    operands = (scalars, key_gain, hidden, queries, cache_keys, cache_values, key_weight, value_weight, out_weight)

    def ring(t):
        return lambda scalars, gain, *rest: layer(t, replicas, tensors, scalars, gain.reshape(1, -1), *rest[:-3])

    branches = [ring(t) for t in TIERS] + [plain_layer]
    branch, listed = lax.switch(tier[0], branches, *operands, lengths, move_src, move_dst)
    return place(scalars, dead, branch, listed, slots)


def solution(mesh):
    placed = (
        P("replica", None, None),
        P("replica", None, "tensor"),
        P("replica", None, "tensor"),
        P("replica", None, "tensor"),
        P(None, "tensor"),
        P(None, "tensor"),
        P(),
        P("tensor", None),
        P(),
        P(),
        P(),
    )
    return jax.shard_map(
        shards,
        mesh=mesh,
        in_specs=placed,
        out_specs=(
            P("replica", None, "tensor"),
            P("replica", None, "tensor"),
            P("replica", None, "tensor"),
        ),
        check_vma=False,
    )
```

```python
import functools
import math

import jax
import jax.numpy as jnp
from jax import lax
from jax.experimental import pallas as pl
from jax.experimental.pallas import tpu as pltpu
from jax.sharding import PartitionSpec as P

EPS = 1e-06
THETA = 1000000.0
MESH = pl.DeviceIdType.MESH
VMEM_LIMIT = 60 * 1024 * 1024
MOVES = 14
KEPT_ROWS, CAME_ROWS = 8, 16
TIERS = (((7, 4, 3, 1), 10), ((7, 5, 3, 2), 10), ((8, 6, 4, 2), 11), ((9, 7, 5, 3), 12))
PARTS = 2
Y_WINDOW = 3 * PARTS
HAND_WINDOW = 3 * PARTS
PAUSES = range(5, 100, 3)


def route(slots, replicas, me, src, dst):
    width = 128

    def column(row):
        tall = jnp.broadcast_to(row.astype(jnp.float32), (width, moves))
        return jnp.concatenate([tall[:, i : i + width].T for i in range(0, moves, width)], axis=0).astype(jnp.int32)

    def down(of, *rows):
        cuts = [[row[:, i : i + width] for row in rows] for i in range(0, moves, width)]
        return jnp.concatenate([jnp.sum(of(*cut), axis=0, keepdims=True) for cut in cuts], axis=1)

    ring = replicas // 4
    half = ring // 2
    core_bits, ring_bits, slot_bits = 1, ring.bit_length() - 1, slots.bit_length() - 1
    assert slots == 1 << slot_bits and ring == 1 << ring_bits
    moves = src.shape[1]
    order = lax.broadcasted_iota(jnp.int32, (1, moves), 1)
    exists = order < replicas * MOVES
    from_rep, to_rep = src >> slot_bits, dst >> slot_bits

    def coordinates(rep):
        return rep >> (core_bits + ring_bits), (rep >> core_bits) & (ring - 1), rep & 1

    ys, zs, cs = coordinates(from_rep)
    yd, zd, cd = coordinates(to_rep)
    ahead = jnp.where(exists, (zd - zs) & (ring - 1), 0)
    group = (yd * ring + zs) * 2 + cs
    distance = jnp.where(ahead <= half, ahead, ring - ahead)
    travels = ahead != 0
    pull = jnp.where((ahead == half) | ~travels, 0, jnp.where(ahead < half, ahead, ahead - ring))
    farthest = ahead == half

    other, other_group, other_pull = column(order), column(group), column(pull)
    other_far = column(jnp.where(farthest, group, -1))
    lean = down(lambda g: jnp.where(other_group == g, other_pull, 0), group)
    rank_far = down(lambda g, n: jnp.where((other_far == g) & (other < n), 1, 0), group, order)
    way = jnp.where(ahead < half, 0, 1)
    for i in range(4):
        back = lean > 0
        way = jnp.where(farthest & (rank_far == i), jnp.where(back, 1, 0), way)
        lean = lean + jnp.where(back, -half, half)
    list_key = group * 2 + way
    sort_key = (list_key * 8 + 7 - distance) * moves + order
    other_key = column(jnp.where(travels, sort_key, -1))
    least = list_key * (8 * moves)
    place_in = down(lambda low, key: jnp.where((other_key >= low) & (other_key < key), 1, 0), least, sort_key)
    spot = 2 * place_in + way
    crosses = travels & (ys != yd)
    y_key = from_rep * 64 + spot
    other_y = column(jnp.where(crosses, y_key, -1))
    y_rank = down(lambda low, key: jnp.where((other_y >= low) & (other_y < key), 1, 0), from_rep * 64, y_key)

    tier = jnp.full((1, 1), len(TIERS), jnp.int32)
    for i, (caps, y_cap) in reversed(list(enumerate(TIERS))):
        reach = sum(jnp.where(place_in < c, 1, 0) for c in caps)
        misfit = travels & ((distance > reach) | (crosses & (y_rank >= y_cap)))
        tier = jnp.where(jnp.sum(jnp.where(misfit, 1, 0), axis=1, keepdims=True) == 0, i, tier)

    my_y, my_z, my_c = coordinates(me)
    mine = exists & (from_rep == me)
    in_group = travels & (group == (my_y * ring + my_z) * 2 + my_c)
    kind = jnp.where(ys == yd, 0, jnp.where(cs == cd, 1, 2))
    address = jnp.where(
        in_group,
        jnp.where(spot < 32, spot, -1),
        jnp.where(
            mine,
            jnp.where(travels, 32 + y_rank, 48 + kind),
            jnp.where(exists & (to_rep == me), 64 + (dst & (slots - 1)), -1),
        ),
    )
    code = (((place_in * 2 + way) * 8 + distance) * 4 + kind) * 1024 + src + 1
    value = jnp.where(mine, src & (slots - 1), jnp.where(in_group, slots + y_rank, code))
    lane = lax.broadcasted_iota(jnp.int32, (1, width), 1)
    hit = column(address) == lane
    table = jnp.sum(jnp.where(hit, column(value), 0), axis=0, keepdims=True)
    return jnp.where(lane == width - 1, tier, table)


INJECT, ACROSS, NEAR, LIVE, LENGTH, LANE, SPOT, KIND, TOKENS, ROW, TABLE = 0, 32, 48, 64, 96, 128, 144, 160, 176, 208, 240


def plan_kernel(
    slots,
    replicas,
    me_ref,
    len_ref,
    src_ref,
    src_row,
    dst_row,
    tier_ref,
    dead_ref,
    out_ref,
    mark,
    padded,
    table_vmem,
    table_ref,
    sem,
):
    me = me_ref[0]
    slot_bits = slots.bit_length() - 1
    count = src_row.shape[1]
    padded[...] = jnp.zeros_like(padded)
    padded[0:1, :count] = src_row[...]
    padded[1:2, :count] = dst_row[...]

    table_vmem[...] = route(slots, replicas, me, padded[0:1, :], padded[1:2, :])
    fetch = pltpu.make_async_copy(table_vmem, table_ref, sem)
    fetch.start()

    def clear(i, _):
        mark[i] = 0
        return 0

    lax.fori_loop(0, slots, clear, 0, unroll=8)

    def out(k, _):
        mark[src_ref[me * MOVES + k] & (slots - 1)] = 1
        return 0

    lax.fori_loop(0, MOVES, out, 0, unroll=2)
    fetch.wait()
    tier_ref[0] = table_ref[0, 127]

    def copy(i, _):
        out_ref[INJECT + i] = table_ref[0, i]
        return 0

    lax.fori_loop(0, 64, copy, 0, unroll=8)

    def each(s, counts):
        kept_count, in_count, dead_count = counts
        code = table_ref[0, 64 + s]
        incoming = code > 0
        source = jnp.where(incoming, (code - 1) & 1023, me * slots + s)
        length = len_ref[source]
        stays = jnp.logical_not(incoming) & (mark[s] == 0) & (length > 0)
        alive = incoming | stays
        length = jnp.where(alive, length, 0)
        at = jnp.where(incoming, slots - 2 * MOVES + in_count, kept_count)
        where = jnp.where(alive, at, slots - 1)
        out_ref[LIVE + where] = s
        out_ref[LENGTH + where] = length
        dead_ref[dead_count] = s
        rest = (code - 1) >> 10
        kind = rest & 3
        distance = (rest >> 2) & 7
        way = (rest >> 5) & 1
        slot_in = jnp.where(incoming, in_count, MOVES)
        other_core = ((source >> slot_bits) ^ me) & 1
        out_ref[LANE + slot_in] = (other_core * 2 + way) * 4 + distance - 1
        out_ref[SPOT + slot_in] = rest >> 6
        out_ref[KIND + slot_in] = jnp.where(distance == 0, kind, -1)
        out_ref[TOKENS + s] = length
        out_ref[ROW + s] = jnp.where(alive, jnp.where(incoming, 2 * KEPT_ROWS + in_count, kept_count), -1)
        one = jnp.int32(1)
        return (
            kept_count + jnp.where(stays, one, 0),
            in_count + jnp.where(incoming, one, 0),
            dead_count + jnp.where(alive, 0, one),
        )

    zero = jnp.int32(0)
    lax.fori_loop(0, slots, each, (zero, zero, zero), unroll=2)


def plan(me, lengths, move_src, move_dst, slots, replicas):
    smem = pl.BlockSpec(memory_space=pltpu.SMEM)
    vmem = pl.BlockSpec(memory_space=pltpu.VMEM)
    ints = lambda n: jax.ShapeDtypeStruct((n,), jnp.int32)
    moves = -(-move_src.shape[0] // 128) * 128
    return pl.pallas_call(
        functools.partial(plan_kernel, slots, replicas),
        out_shape=(ints(1), ints(slots + 1), ints(TABLE)),
        in_specs=[smem] * 3 + [vmem] * 2,
        out_specs=(smem,) * 3,
        scratch_shapes=[
            pltpu.SMEM((slots,), jnp.int32),
            pltpu.VMEM((8, moves), jnp.int32),
            pltpu.VMEM((1, 128), jnp.int32),
            pltpu.SMEM((1, 128), jnp.int32),
            pltpu.SemaphoreType.DMA,
        ],
    )(me, lengths, move_src, move_src.reshape(1, -1), move_dst.reshape(1, -1))


def crossings(y_cap):
    return [(b, part) for low in range(0, y_cap, 2) for part in range(PARTS) for b in range(low, min(low + 2, y_cap))]


def timetable(caps, y_cap):
    step, lag = 1.0 / PARTS, 0.5
    across = {key: (n + 1) * step + lag for n, key in enumerate(crossings(y_cap))}
    ready = [
        (across[min(i, y_cap - 1), part] + 0.01 * max(0, i - y_cap), 1, "inject", i % 2, 1, i // 2, part)
        for i in range(2 * caps[0])
        for part in range(PARTS)
    ]
    free = [0.0, 0.0]
    events = []
    while ready:
        ready.sort()
        time, _, what, way, hop, spot, part = event = ready.pop(0)
        events.append(event[2:])
        if what == "inject" or (hop < len(caps) and spot < caps[hop]):
            free[way] = max(free[way], time) + step
            onward = hop if what == "inject" else hop + 1
            ready.append((free[way] + lag, 0, "pass", way, onward, spot, part))
    return events


class Ring:
    def __init__(self, tier, replicas, me, scalars, caches, arrived, inject, across, across_in, near, *sems):
        self.caps, self.y_cap = tier
        self.me, self.scalars, self.caches = me, scalars, caches
        self.arrived, self.inject, self.across, self.across_in, self.near = arrived, inject, across, across_in, near
        self.hop_send, self.hop_recv, self.core_send, self.core_recv, self.y_send, self.y_recv, self.near_send, self.near_recv = sems
        half = replicas // 2
        line = (me // half) * half
        ahead = line + lax.rem(me - line + 2, half)
        behind = line + lax.rem(me - line + half - 2, half)
        core = me + 1 - 2 * lax.rem(me, 2)
        opposite = lax.rem(me + half, replicas)
        both = lax.rem(core + half, replicas)
        self.ways = (ahead, behind)
        self.core, self.opposite = core, opposite
        self.near_peers = (core, opposite, both)
        self.partners = 5
        self.events = timetable(self.caps, self.y_cap)
        self.lanes = 2 * sum(self.caps)

    def greet(self, barrier):
        for peer in self.ways + self.near_peers:
            pl.semaphore_signal(barrier, inc=1, device_id={"replica": peer}, device_id_type=MESH)

    def copy(self, source, target, send_sem, recv_sem, peer):
        return pltpu.make_async_remote_copy(
            src_ref=source, dst_ref=target, send_sem=send_sem, recv_sem=recv_sem, device_id={"replica": peer}, device_id_type=MESH
        )

    def lane(self, way, hop, spot):
        return way * sum(self.caps) + sum(self.caps[: hop - 1]) + spot

    def half(self, ref, at, part):
        rows = 2 * self.caches[0].shape[1] // PARTS
        return ref.at[at, pl.ds(part * rows, rows)]

    def own(self, slot, part):
        rows = 2 * self.caches[0].shape[1] // PARTS
        which, low = part * 2 // PARTS, part % (PARTS // 2) * rows
        return self.caches[which][slot, low : low + rows, :]

    def cross(self, b, part):
        at = b * PARTS + part
        return self.copy(
            self.half(self.across, b, part), self.half(self.across_in, b, part), self.y_send.at[at], self.y_recv.at[at], self.opposite
        )

    def next_door(self, j):
        target = self.arrived.at[2 * self.lanes + j]
        return self.copy(self.near.at[j], target, self.near_send.at[j], self.near_recv.at[j], self.near_peers[j])

    def hop(self, way, hop, spot, part):
        source = (self.inject, 2 * spot + way) if hop == 1 else (self.arrived, self.lane(way, hop - 1, spot))
        to = self.lane(way, hop, spot)
        at = to * PARTS + part
        return self.copy(
            self.half(*source, part), self.half(self.arrived, to, part), self.hop_send.at[at], self.hop_recv.at[at], self.ways[way]
        )

    def hand_over(self, way, hop, spot, part):
        lane = self.lane(way, hop, spot)
        at = lane * PARTS + part
        return self.copy(
            self.half(self.arrived, lane, part),
            self.half(self.arrived, self.lanes + lane, part),
            self.core_send.at[at],
            self.core_recv.at[at],
            self.core,
        )

    def pack(self, target, at, slot, parts):
        rows = 2 * self.caches[0].shape[1] // PARTS
        for part in parts:
            target[at, part * rows : (part + 1) * rows, :] = self.own(slot, part)

    def begin(self, n):
        order = crossings(self.y_cap)
        if n < len(order):
            b, part = order[n]
            self.pack(self.across, b, self.scalars[ACROSS + b], (part,))
            self.cross(b, part).start()
        elif n < len(order) + 3:
            j = n - len(order)
            self.pack(self.near, j, self.scalars[NEAR + j], range(PARTS))
            self.next_door(j).start()

    def enter(self, way, spot, part, crossed):
        slots = self.caches[0].shape[0]
        rows = 2 * self.caches[0].shape[1] // PARTS
        i = 2 * spot + way
        here = slice(part * rows, (part + 1) * rows)
        code = self.scalars[INJECT + i]
        block = self.own(jnp.where(code < slots, code, 0), part)
        if crossed == len(crossings(self.y_cap)):
            other = self.across_in[jnp.where(code < slots, 0, code - slots), here, :]
            block = jnp.where(code < slots, block, other)
        else:
            for b in range(min(i + 1, self.y_cap)):
                block = jnp.where(code == slots + b, self.across_in[b, here, :], block)
        self.inject[i, here, :] = block
        self.hop(way, 1, spot, part).start()

    def carry(self, loaded, pauses):
        order = crossings(self.y_cap)
        for n in range(PARTS):
            self.begin(n)
        loaded()
        for n in range(PARTS, Y_WINDOW):
            self.begin(n)
        crossed = 0
        pauses = dict(pauses)
        over = []
        for count, (what, way, hop, spot, part) in enumerate(self.events):
            if what == "inject":
                needed = order.index((min(2 * spot + way, self.y_cap - 1), part)) + 1
                while crossed < needed:
                    self.cross(*order[crossed]).wait_recv()
                    self.begin(crossed + Y_WINDOW)
                    crossed += 1
                self.enter(way, spot, part, crossed)
            else:
                self.hop(way, hop, spot, part).wait_recv()
                if hop < len(self.caps) and spot < self.caps[hop]:
                    self.hop(way, hop + 1, spot, part).start()
                self.hand_over(way, hop, spot, part).start()
                over.append((way, hop, spot, part))
                if len(over) > HAND_WINDOW:
                    self.hand_over(*over[-1 - HAND_WINDOW]).wait()
            if count in pauses:
                pauses.pop(count)()
        for pause in pauses.values():
            pause()
        for n in range(crossed, len(order)):
            self.cross(*order[n]).wait_recv()
        for n in range(max(Y_WINDOW, crossed + Y_WINDOW), len(order) + 3):
            self.begin(n)
        for j in range(3):
            self.next_door(j).wait_recv()
        for key in over[-HAND_WINDOW:]:
            self.hand_over(*key).wait()

    def where(self, i):
        kind, lane = self.scalars[KIND + i], self.scalars[LANE + i]
        first = 0
        for n in range(2 * 2 * len(self.caps)):
            way, hop = n // len(self.caps) % 2, n % len(self.caps) + 1
            first = jnp.where(lane == n, n // (2 * len(self.caps)) * self.lanes + self.lane(way, hop, 0), first)
        return jnp.where(kind >= 0, 2 * self.lanes + kind, first + self.scalars[SPOT + i])

    def finish(self):
        for b, part in crossings(self.y_cap):
            self.cross(b, part).wait_send()
        for j in range(3):
            self.next_door(j).wait_send()
        for what, way, hop, spot, part in self.events:
            if what == "pass":
                self.hop(way, hop, spot, part).wait_send()


def layer_kernel(
    replicas,
    tensors,
    tier,
    scalar_ref,
    gain_ref,
    hidden_hbm,
    query_hbm,
    ck_hbm,
    cv_hbm,
    kw_hbm,
    vw_hbm,
    ow_hbm,
    branch_ref,
    list_hbm,
    ck,
    cv,
    hid,
    qry,
    kw,
    vw,
    ow,
    flat,
    listed,
    fresh_k,
    fresh_v,
    mix,
    score,
    rs_stage,
    rs_recv,
    reduced,
    row_ref,
    in_sem,
    rs_send_sem,
    rs_recv_sem,
    list_sem,
    *transport,
):
    me = lax.axis_index("replica")
    at = lax.axis_index("tensor")
    slots, rows, width = ck.shape
    live = listed.shape[0]
    kept = live - MOVES
    groups = query_hbm.shape[2] // width

    loads = [
        pltpu.make_async_copy(source, target, in_sem.at[i])
        for i, (source, target) in enumerate(
            (
                (ck_hbm, ck),
                (cv_hbm, cv),
                (hidden_hbm, hid),
                (kw_hbm, kw),
                (vw_hbm, vw),
                (query_hbm, qry),
                (ow_hbm, ow),
            )
        )
    ]
    loads[0].start()
    loads[1].start()

    caches = (ck, cv)
    road = Ring(tier, replicas, me, scalar_ref, caches, *transport)

    barrier = pltpu.get_barrier_semaphore()
    road.greet(barrier)

    def greet_tensor(j, _):
        pl.semaphore_signal(barrier, inc=1, device_id={"tensor": lax.rem(at + j, tensors)}, device_id_type=MESH)
        return 0

    lax.fori_loop(1, tensors, greet_tensor, 0)
    pl.semaphore_wait(barrier, road.partners + tensors - 1)

    loads[0].wait()

    def clear():
        mix[...] = jnp.zeros_like(mix)
        reduced[...] = jnp.zeros_like(reduced)

    def tell():
        def one(s, _):
            tokens, row = scalar_ref[TOKENS + s], scalar_ref[ROW + s]
            stride = jnp.where(row < 2 * KEPT_ROWS, KEPT_ROWS, CAME_ROWS)
            for t in range(2):
                at = jnp.where(row < 0, -1, row + t * stride)
                row_ref[pl.ds(2 * s + t, 1), :] = jnp.full((1, width), tokens + t, jnp.int32).astype(jnp.float32)
                row_ref[pl.ds(2 * (slots + s) + t, 1), :] = jnp.full((1, width), at, jnp.int32).astype(jnp.float32)
            return 0

        lax.fori_loop(0, slots, one, 0, unroll=2)

    def flatten():
        loads[2].wait()
        for s in range(slots):
            flat[2 * s : 2 * s + 2, :] = hid[s]

    def project_keys():
        loads[3].wait()
        fresh_k[...] = jnp.dot(flat[...], kw[...], preferred_element_type=jnp.float32)

    def project_values():
        loads[4].wait()
        raw_v = jnp.dot(flat[...], vw[...], preferred_element_type=jnp.float32)
        fresh_v[...] = raw_v.astype(jnp.bfloat16).astype(jnp.float32)

    lane = lax.broadcasted_iota(jnp.int32, (1, width), 1)

    def rotate_keys():
        raw_k = fresh_k[...]
        mean_square = jnp.mean(raw_k * raw_k, axis=-1, keepdims=True)
        normed = raw_k * lax.rsqrt(mean_square + EPS) * gain_ref[...]
        half = width // 2
        index = jnp.where(lane < half, lane, lane - half).astype(jnp.float32)
        angles = row_ref[: 2 * slots, :] * jnp.exp(index * (-2.0 * math.log(THETA) / width))
        turned = pltpu.roll(normed, half, 1)
        sine = jnp.sin(angles)
        rotated = normed * jnp.cos(angles) + turned * jnp.where(lane < half, -sine, sine)
        fresh_k[...] = rotated.astype(jnp.bfloat16).astype(jnp.float32)

    row_ids = lax.broadcasted_iota(jnp.int32, (rows, width), 0)
    column_ids = lax.broadcasted_iota(jnp.int32, (2 * groups, rows), 1)
    step_ids = lax.broadcasted_iota(jnp.int32, (2 * groups, rows), 0) % 2

    def placed(stored, fresh, slot, length):
        full = jnp.where(row_ids < length, stored.astype(jnp.float32), 0.0)
        full = jnp.where(row_ids == length, fresh[pl.ds(2 * slot, 1), :], full)
        full = jnp.where(row_ids == length + 1, fresh[pl.ds(2 * slot + 1, 1), :], full)
        return full.astype(jnp.bfloat16)

    heads = 2 * groups

    def attend(first, count, stored, unroll):
        def fill(i, _):
            e = first + i
            slot, length = scalar_ref[LIVE + e], scalar_ref[LENGTH + e]
            stored_k, stored_v = stored(i)
            listed[e, :rows, :] = placed(stored_k, fresh_k, slot, length)
            listed[e, rows:, :] = placed(stored_v, fresh_v, slot, length)
            pltpu.make_async_copy(listed.at[e], list_hbm.at[e], list_sem.at[e]).start()
            return 0

        def weigh(i, _):
            e = first + i
            slot, length = scalar_ref[LIVE + e], scalar_ref[LENGTH + e]
            q = qry[slot].astype(jnp.float32)
            q = jnp.concatenate([q[:, g * width : (g + 1) * width] for g in range(groups)], axis=0).astype(jnp.bfloat16)
            scores = lax.dot_general(
                q, listed[e, :rows, :], (((1,), (1,)), ((), ())), preferred_element_type=jnp.float32
            ) * width ** (-0.5)
            at = pl.ds(pl.multiple_of(e * heads, heads), heads)
            score[at, :] = jnp.where(column_ids <= length + step_ids, scores, -jnp.inf)
            return 0

        def blend(i, _):
            e = first + i
            at = pl.ds(pl.multiple_of(e * heads, heads), heads)
            mix[at, :] = jnp.dot(score[at, :].astype(jnp.bfloat16), listed[e, rows:, :], preferred_element_type=jnp.float32)
            return 0

        lax.fori_loop(0, count, fill, 0, unroll=2)
        lax.fori_loop(0, count, weigh, 0, unroll=unroll)
        every = slice(first * heads, (first + count) * heads)
        scores = score[every, :]
        weights = jnp.exp(scores - jnp.max(scores, axis=-1, keepdims=True))
        score[every, :] = weights / jnp.sum(weights, axis=-1, keepdims=True)
        lax.fori_loop(0, count, blend, 0, unroll=unroll)

    def own(i):
        slot = scalar_ref[LIVE + i]
        return ck[slot], cv[slot]

    def brought(i):
        source = road.where(i)
        return road.arrived[source, :rows, :], road.arrived[source, rows:, :]

    def attend_kept():
        loads[5].wait()
        attend(0, kept, own, kept)
        loads[6].wait()

    out_width = branch_ref.shape[1]
    groups_of_rows = ((0, KEPT_ROWS, 0), (kept, CAME_ROWS, 2 * KEPT_ROWS))

    def mixture(group):
        first, count, _ = groups_of_rows[group]
        steps = [
            jnp.concatenate(
                [mix[pl.ds(first * heads + 2 * g + t, count, stride=heads), :] for g in range(groups)], axis=1
            )
            for t in range(2)
        ]
        return jnp.concatenate(steps, axis=0).astype(jnp.bfloat16)

    def term(mixed, j):
        first = pl.multiple_of(lax.rem(at + j, tensors) * out_width, 128)
        return jnp.dot(mixed, ow[:, pl.ds(first, out_width)], preferred_element_type=jnp.float32)

    def give(group, j):
        _, count, low = groups_of_rows[group]
        n = group * tensors + j
        return pltpu.make_async_remote_copy(
            src_ref=rs_stage.at[j, pl.ds(low, 2 * count)],
            dst_ref=rs_recv.at[j, pl.ds(low, 2 * count)],
            send_sem=rs_send_sem.at[n],
            recv_sem=rs_recv_sem.at[n],
            device_id={"tensor": lax.rem(at + j, tensors)},
            device_id_type=MESH,
        )

    def give_term(group, mixed, j):
        _, count, low = groups_of_rows[group]
        rs_stage[j, low : low + 2 * count, :] = term(mixed, j).astype(jnp.bfloat16)
        give(group, j).start()

    def add_up(group, own_term):
        _, count, low = groups_of_rows[group]
        total = own_term
        for j in range(1, tensors):
            give(group, j).wait_recv()
            total = total + rs_recv[j, low : low + 2 * count, :].astype(jnp.float32)
        reduced[low : low + 2 * count, :] = total.astype(jnp.bfloat16)

    def give_kept(j):
        give_term(0, mixture(0), j)

    pieces = [clear, tell, flatten, project_keys, project_values, rotate_keys, attend_kept]
    pieces += [functools.partial(give_kept, j) for j in range(1, tensors)]

    def loaded():
        loads[1].wait()
        for load in loads[2:]:
            load.start()

    road.carry(loaded, zip(PAUSES, pieces))
    attend(kept, MOVES, brought, 7)

    mixed = mixture(1)

    def give_came(j, _):
        give_term(1, mixed, j)
        return 0

    lax.fori_loop(1, tensors, give_came, 0)
    own_term = term(mixed, 0)
    road.finish()
    add_up(0, term(mixture(0), 0))
    add_up(1, own_term)
    rows_at = row_ref[2 * slots :, :]
    pick = (lane.astype(jnp.float32) == rows_at).astype(jnp.float32).astype(jnp.bfloat16)
    branch_ref[...] = jnp.dot(pick, reduced[...], preferred_element_type=jnp.float32).astype(jnp.bfloat16)

    def given(j, _):
        for group in range(2):
            give(group, j).wait_send()
        return 0

    lax.fori_loop(1, tensors, given, 0)

    def written(e, _):
        pltpu.make_async_copy(listed.at[e], list_hbm.at[e], list_sem.at[e]).wait()
        return 0

    lax.fori_loop(0, live, written, 0)


def layer(tier, replicas, tensors, scalars, gain, *operands):
    hidden, queries, cache_keys, cache_values, key_weight, value_weight, out_weight = operands
    slots, rows, width = cache_keys.shape
    live = slots - MOVES
    groups = queries.shape[2] // width
    out_width = out_weight.shape[1] // tensors
    smem = pl.BlockSpec(memory_space=pltpu.SMEM)
    vmem = pl.BlockSpec(memory_space=pltpu.VMEM)
    any_ = pl.BlockSpec(memory_space=pl.ANY)
    bf16 = jnp.bfloat16
    dma = pltpu.SemaphoreType.DMA

    def rollouts(n):
        return pltpu.VMEM((n, 2 * rows, width), bf16)

    caps, y_cap = tier
    lanes = 2 * sum(caps)
    transport = [
        rollouts(2 * lanes + 3),
        rollouts(2 * caps[0]),
        rollouts(y_cap),
        rollouts(y_cap),
        rollouts(3),
    ]
    sizes = (lanes * PARTS, lanes * PARTS, lanes * PARTS, lanes * PARTS, y_cap * PARTS, y_cap * PARTS, 3, 3)
    transport += [dma((n,)) for n in sizes]
    return pl.pallas_call(
        functools.partial(layer_kernel, replicas, tensors, tier),
        out_shape=(
            jax.ShapeDtypeStruct((2 * slots, out_width), bf16),
            jax.ShapeDtypeStruct((live, 2 * rows, width), bf16),
        ),
        in_specs=[smem, vmem] + [any_] * len(operands),
        out_specs=(vmem, any_),
        scratch_shapes=[
            pltpu.VMEM(cache_keys.shape, bf16),
            pltpu.VMEM(cache_values.shape, bf16),
            pltpu.VMEM(hidden.shape, bf16),
            pltpu.VMEM(queries.shape, bf16),
            pltpu.VMEM(key_weight.shape, bf16),
            pltpu.VMEM(value_weight.shape, bf16),
            pltpu.VMEM(out_weight.shape, bf16),
            pltpu.VMEM((2 * slots, hidden.shape[2]), bf16),
            pltpu.VMEM((live, 2 * rows, width), bf16),
            pltpu.VMEM((2 * slots, width), jnp.float32),
            pltpu.VMEM((2 * slots, width), jnp.float32),
            pltpu.VMEM((2 * groups * (slots - 2 * MOVES + CAME_ROWS), width), jnp.float32),
            pltpu.VMEM((2 * groups * live, rows), jnp.float32),
            pltpu.VMEM((tensors, 2 * (KEPT_ROWS + CAME_ROWS), out_width), bf16),
            pltpu.VMEM((tensors, 2 * (KEPT_ROWS + CAME_ROWS), out_width), bf16),
            pltpu.VMEM((128, out_width), bf16),
            pltpu.VMEM((4 * slots, width), jnp.float32),
            dma((len(operands),)),
            dma((2 * tensors,)),
            dma((2 * tensors,)),
            dma((live,)),
        ]
        + transport,
        compiler_params=pltpu.CompilerParams(
            collective_id=TIERS.index(tier),
            has_side_effects=True,
            vmem_limit_bytes=VMEM_LIMIT,
        ),
    )(scalars, gain, *operands)


def rotate(vectors, positions):
    half_width = vectors.shape[-1] // 2
    indices = jnp.arange(half_width, dtype=jnp.float32)
    frequency = jnp.exp(indices * (-2.0 * math.log(THETA) / vectors.shape[-1]))
    angles = positions[:, :, None, None] * frequency
    cosine = jnp.cos(angles)
    sine_values = jnp.sin(angles)
    former = vectors[..., :half_width]
    latter = vectors[..., half_width:]
    return jnp.concatenate(
        [former * cosine - latter * sine_values, latter * cosine + former * sine_values], -1
    )


def new_entries(hidden, key_weight, value_weight, key_gain, length):
    row_count = hidden.shape[0]
    flat_rows = hidden.reshape(row_count * 2, hidden.shape[2])
    raw_keys = jnp.dot(flat_rows, key_weight, preferred_element_type=jnp.float32).reshape(
        row_count, 2, -1, key_gain.shape[0]
    )
    mean_square = jnp.mean(raw_keys * raw_keys, axis=-1, keepdims=True)
    normed = raw_keys * lax.rsqrt(mean_square + EPS) * key_gain
    positions = (length[:, None] + jnp.arange(2, dtype=jnp.int32)[None, :]).astype(jnp.float32)
    fresh_keys = rotate(normed, positions).reshape(row_count, 2, -1).astype(jnp.bfloat16)
    fresh_values = (
        jnp.dot(flat_rows, value_weight, preferred_element_type=jnp.float32)
        .reshape(row_count, 2, -1)
        .astype(jnp.bfloat16)
    )
    return (fresh_keys, fresh_values)


def fill(stored, fresh, length, active):
    row_ids = jnp.arange(stored.shape[1], dtype=jnp.int32)[None, :, None]
    border = length[:, None, None]
    kept = jnp.where(row_ids < border, stored, jnp.zeros_like(stored))
    kept = jnp.where(row_ids == border, fresh[:, 0:1, :], kept)
    kept = jnp.where(row_ids == border + 1, fresh[:, 1:2, :], kept)
    return jnp.where(active[:, None, None], kept, jnp.zeros_like(kept))


def attend(full_keys, full_values, length, queries, head_dim):
    row_count, key_rows, width = full_keys.shape
    kv_heads = width // head_dim
    group_size = queries.shape[-1] // width
    query_heads = queries.reshape(row_count, 2, kv_heads, group_size, head_dim)
    key_heads = full_keys.reshape(row_count, key_rows, kv_heads, head_dim)
    value_heads = full_values.reshape(row_count, key_rows, kv_heads, head_dim)
    scores = jnp.einsum(
        "rsvgh,rlvh->rvsgl", query_heads, key_heads, preferred_element_type=jnp.float32
    ) * head_dim ** (-0.5)
    row_ids = jnp.arange(key_rows, dtype=jnp.int32)[None, None, :]
    limits = length[:, None, None] + jnp.arange(2, dtype=jnp.int32)[None, :, None]
    visible = row_ids <= limits
    scores = jnp.where(visible[:, None, :, None, :], scores, -jnp.inf)
    highest = jnp.max(scores, axis=-1, keepdims=True)
    weights = jnp.exp(scores - highest)
    shares = (weights / jnp.sum(weights, axis=-1, keepdims=True)).astype(jnp.bfloat16)
    mixture = jnp.einsum(
        "rvsgl,rlvh->rsvgh", shares, value_heads, preferred_element_type=jnp.float32
    )
    return mixture.reshape(row_count, 2, -1).astype(jnp.bfloat16)


def plain_layer(scalars, key_gain, hidden, queries, cache_keys, cache_values, key_weight, value_weight, out_weight, lengths, move_src, move_dst):
    local_count = cache_keys.shape[0]
    replicas = lax.axis_size("replica")
    replica_here = lax.axis_index("replica")
    first_slot = replica_here * local_count
    head_dim = key_gain.shape[0]
    all_slots = jnp.arange(lengths.shape[0], dtype=jnp.int32)
    anchor = all_slots.at[move_src].set(-1).at[move_dst].set(move_src)
    own_anchor = lax.dynamic_slice_in_dim(anchor, first_slot, local_count)
    holding = own_anchor >= 0
    new_length = jnp.where(holding, lengths[jnp.where(holding, own_anchor, 0)], 0)
    alive = new_length > 0
    local_ids = first_slot + jnp.arange(local_count, dtype=jnp.int32)
    source_rep = move_src // local_count
    target_rep = move_dst // local_count
    peer_ids = jnp.arange(replicas, dtype=jnp.int32)
    sending = (source_rep[None, :] == replica_here) & (target_rep[None, :] == peer_ids[:, None])
    has_out = jnp.any(sending, axis=1)
    send_slot = jnp.sum(jnp.where(sending, move_src[None, :] - first_slot, 0), axis=1)
    outbound = has_out[:, None, None]
    pack_keys = jnp.where(outbound, cache_keys[send_slot], jnp.zeros((), cache_keys.dtype))
    pack_values = jnp.where(outbound, cache_values[send_slot], jnp.zeros((), cache_values.dtype))
    arrived_keys, arrived_values = (
        lax.all_to_all(pack_keys, "replica", split_axis=0, concat_axis=0, tiled=True),
        lax.all_to_all(pack_values, "replica", split_axis=0, concat_axis=0, tiled=True),
    )
    arriving = move_dst[None, :] == local_ids[:, None]
    incoming = jnp.any(arriving, axis=1)
    from_rep = jnp.sum(jnp.where(arriving, source_rep[None, :], 0), axis=1)
    leaving = jnp.any(move_src[None, :] == local_ids[:, None], axis=1)
    inbound = incoming[:, None, None]
    staying = (~leaving)[:, None, None]
    zero_key = jnp.zeros((), cache_keys.dtype)
    kept_keys = jnp.where(staying, cache_keys, zero_key)
    kept_values = jnp.where(staying, cache_values, zero_key)
    base_keys = jnp.where(inbound, arrived_keys[from_rep], kept_keys)
    base_values = jnp.where(inbound, arrived_values[from_rep], kept_values)
    fresh_keys, fresh_values = new_entries(hidden, key_weight, value_weight, key_gain, new_length)
    keys_out = fill(base_keys, fresh_keys, new_length, alive)
    values_out = fill(base_values, fresh_values, new_length, alive)
    mixture = attend(keys_out, values_out, new_length, queries, head_dim)
    head_terms = jnp.dot(
        mixture.reshape(local_count * 2, -1), out_weight, preferred_element_type=jnp.float32
    )
    head_terms = head_terms.reshape(local_count, 2, -1)
    head_terms = jnp.where(alive[:, None, None], head_terms, 0.0)
    tensors = lax.axis_size("tensor")
    terms = head_terms.reshape(local_count, 2, tensors, -1)
    terms = lax.all_to_all(terms, "tensor", split_axis=2, concat_axis=2, tiled=True)
    attn_branch = jnp.sum(terms, axis=2).astype(jnp.bfloat16)
    live = lax.dynamic_slice_in_dim(scalars, LIVE, local_count - MOVES)
    listed = jnp.concatenate([keys_out[live], values_out[live]], axis=1)
    return attn_branch.reshape(2 * local_count, -1), listed


def place_kernel(scalar_ref, dead_ref, flat_ref, list_hbm, branch_ref, keys_hbm, values_hbm, listed, zeros, sem, load_sem):
    rows = zeros.shape[0]
    live = listed.shape[0]

    def load(e):
        return (pltpu.make_async_copy(list_hbm.at[e], listed.at[e], load_sem.at[e]),)

    def copies(e):
        slot = scalar_ref[LIVE + e]
        return (
            pltpu.make_async_copy(listed.at[e, pl.ds(0, rows)], keys_hbm.at[slot], sem.at[e, 0]),
            pltpu.make_async_copy(listed.at[e, pl.ds(rows, rows)], values_hbm.at[slot], sem.at[e, 1]),
        )

    def clears(e):
        slot = dead_ref[e]
        return (
            pltpu.make_async_copy(zeros, keys_hbm.at[slot], sem.at[live + e, 0]),
            pltpu.make_async_copy(zeros, values_hbm.at[slot], sem.at[live + e, 1]),
        )

    def run(count, *acts):
        def each(e, _):
            for make, act in acts:
                for copy in make(e):
                    getattr(copy, act)()
            return 0

        lax.fori_loop(0, count, each, 0, unroll=2)

    run(live, (load, "start"))
    zeros[...] = jnp.zeros_like(zeros)
    run(MOVES, (clears, "start"))
    run(live, (load, "wait"), (copies, "start"))
    for s in range(branch_ref.shape[0]):
        branch_ref[s] = flat_ref[2 * s : 2 * s + 2, :]
    run(MOVES, (clears, "wait"))
    run(live, (copies, "wait"))


def place(scalars, dead_slots, branch, listed, slots):
    live, both, width = listed.shape
    shape = jax.ShapeDtypeStruct((slots, both // 2, width), listed.dtype)
    smem = pl.BlockSpec(memory_space=pltpu.SMEM)
    vmem = pl.BlockSpec(memory_space=pltpu.VMEM)
    any_ = pl.BlockSpec(memory_space=pl.ANY)
    return pl.pallas_call(
        place_kernel,
        out_shape=(jax.ShapeDtypeStruct((slots, 2, branch.shape[1]), branch.dtype), shape, shape),
        in_specs=[smem, smem, vmem, any_],
        out_specs=(vmem, any_, any_),
        scratch_shapes=[
            pltpu.VMEM(listed.shape, listed.dtype),
            pltpu.VMEM((both // 2, width), listed.dtype),
            pltpu.SemaphoreType.DMA((slots, 2)),
            pltpu.SemaphoreType.DMA((live,)),
        ],
    )(scalars, dead_slots, branch, listed)


def shards(hidden, queries, cache_keys, cache_values, key_weight, value_weight, key_gain, out_weight, lengths, move_src, move_dst):
    slots = cache_keys.shape[0]
    replicas, tensors = lax.axis_size("replica"), lax.axis_size("tensor")
    me = lax.axis_index("replica").astype(jnp.int32)
    tier, dead, scalars = plan(me.reshape(1), lengths, move_src, move_dst, slots, replicas)
    operands = (scalars, key_gain, hidden, queries, cache_keys, cache_values, key_weight, value_weight, out_weight)

    def ring(t):
        return lambda scalars, gain, *rest: layer(t, replicas, tensors, scalars, gain.reshape(1, -1), *rest[:-3])

    branches = [ring(t) for t in TIERS] + [plain_layer]
    branch, listed = lax.switch(tier[0], branches, *operands, lengths, move_src, move_dst)
    return place(scalars, dead, branch, listed, slots)


def solution(mesh):
    placed = (
        P("replica", None, None),
        P("replica", None, "tensor"),
        P("replica", None, "tensor"),
        P("replica", None, "tensor"),
        P(None, "tensor"),
        P(None, "tensor"),
        P(),
        P("tensor", None),
        P(),
        P(),
        P(),
    )
    return jax.shard_map(
        shards,
        mesh=mesh,
        in_specs=placed,
        out_specs=(
            P("replica", None, "tensor"),
            P("replica", None, "tensor"),
            P("replica", None, "tensor"),
        ),
        check_vma=False,
    )
```
